32 devices in a mesh: dp: 8 (over z, core), tensor: 4 (over y, x).
Axes of the slice: x: 2, y: 2, z: 4, core: 2. Of those that a mesh axis runs over, the one named last changes fastest.
Arguments:
- layer_input: bfloat16 [8, 2048, 2048], P('dp', 'tensor'), may hold values from -6 to 6
- ln_gain: bfloat16 [2048], P(('dp', 'tensor')), may hold values from 0.5 to 1.5
- ln_bias: bfloat16 [2048], P(('dp', 'tensor')), may hold values from -1.1953125 to 1.1953125
- out_bias: bfloat16 [2048], P(('dp', 'tensor')), may hold values from -1.796875 to 1.796875
- w_qkv: bfloat16 [2048, 3, 2048], P('dp', None, 'tensor'), may hold values from -0.125 to 0.125
- b_qkv: bfloat16 [3, 32, 64], P(None, 'tensor', 'dp'), may hold values from -1.796875 to 1.796875
- w_out: bfloat16 [2048, 2048], P('tensor', 'dp'), may hold values from -1 to 1
- w_fc1: bfloat16 [2048, 8192], P('dp', 'tensor'), may hold values from -0.125 to 0.125
- b_fc1: bfloat16 [128, 64], P('tensor', 'dp'), may hold values from -1.796875 to 1.796875
- w_fc2: bfloat16 [8192, 2048], P('tensor', 'dp'), may hold values from -0.0625 to 0.0625
- out_grad: bfloat16 [8, 2048, 2048], P('dp', 'tensor'), may hold values from -6 to 6
Outputs:
- layer_output: bfloat16 [8, 2048, 2048], P('dp', 'tensor')
- input_grad: float32 [8, 2048, 2048], P('dp', 'tensor')
- ln_gain_grad: float32 [2048], P(('dp', 'tensor'))
- ln_bias_grad: float32 [2048], P(('dp', 'tensor'))
- out_bias_grad: float32 [2048], P(('dp', 'tensor'))
- w_qkv_grad: float32 [2048, 3, 2048], P('dp', None, 'tensor')
- b_qkv_grad: float32 [3, 32, 64], P(None, 'tensor', 'dp')
- w_out_grad: float32 [2048, 2048], P('tensor', 'dp')
- w_fc1_grad: float32 [2048, 8192], P('dp', 'tensor')
- b_fc1_grad: float32 [128, 64], P('tensor', 'dp')
- w_fc2_grad: float32 [8192, 2048], P('tensor', 'dp')
The draws below stay inside these ranges and needn't reach their ends.
All inputs are finite; a program needn't handle non-finite values.
Results may differ from the reference program's by a relative error of at most 0.014.
Values may be sent and summed in bfloat16 or wider, within the bound.
No kernel may reach another device: no remote copies, remote signals or barrier semaphores. Data moves between devices by JAX's collectives and lax.ppermute only.
A program may use at most 192 MiB of HBM per device.

```python
import math
import jax
import jax.numpy as jnp
from jax import lax

D = 2048
H = 32
HD = 64
ROT = 32
FF = 8192
SEQ = 2048
BATCH = 8
N_TENSOR = 4


def level_of(key, dims, pieces, least, high):
    level, own = 1.0, jax.random.fold_in(key, 6)
    for position, parts in pieces:
        heights = jnp.exp(jax.random.uniform(jax.random.fold_in(own, position), (parts,), jnp.float32, least / len(pieces), high / len(pieces)))
        level = level * jnp.repeat(heights, dims[position] // parts).reshape([-1 if axis == position else 1 for axis in range(len(dims))])
    return level


def scatter_about(key, dims, scale, limit, pieces=(), kind=jnp.bfloat16):
    drawn = scale * jax.random.normal(key, dims, jnp.float32)
    if pieces:
        drawn = drawn * level_of(key, dims, pieces, -0.22, 0.18)
    return jnp.clip(drawn, -limit, limit).astype(kind)


def setup_inputs(seed: int = 0) -> dict:
    arg_keys = jax.random.split(jax.random.key(seed), 12)
    layer_input = scatter_about(arg_keys[0], (BATCH, SEQ, D), 1.0, 6.0, ((0, 8), (1, 4)))
    ln_gain = jnp.clip(1.0 + 0.1 * jax.random.normal(arg_keys[1], (D,), jnp.float32), 0.5, 1.5).astype(jnp.bfloat16)
    ln_bias = scatter_about(arg_keys[2], (D,), 0.2, 1.1953125, ((0, 32),))
    out_bias = scatter_about(arg_keys[3], (D,), 0.3, 1.796875, ((0, 32),))
    w_qkv = scatter_about(arg_keys[4], (D, 3, H * HD), D ** -0.5, 0.125, ((0, 8), (2, 4)))
    b_qkv = scatter_about(arg_keys[5], (3, H, HD), 0.3, 1.796875, ((1, 4), (2, 8)))
    w_out = scatter_about(arg_keys[6], (H * HD, D), (H * HD // 64) ** -0.5, 1.0, ((0, 4), (1, 8)))
    w_fc1 = scatter_about(arg_keys[7], (D, FF), D ** -0.5, 0.125, ((0, 8), (1, 4)))
    b_fc1 = scatter_about(arg_keys[8], (FF // HD, HD), 0.3, 1.796875, ((0, 4), (1, 8)))
    w_fc2 = scatter_about(arg_keys[9], (FF, D), FF ** -0.5, 0.0625, ((0, 4), (1, 8)))
    out_grad = scatter_about(arg_keys[10], (BATCH, SEQ, D), 1.0, 6.0, ((0, 8), (1, 4)))
    return {"layer_input": layer_input, "ln_gain": ln_gain, "ln_bias": ln_bias, "out_bias": out_bias, "w_qkv": w_qkv, "b_qkv": b_qkv, "w_out": w_out, "w_fc1": w_fc1, "b_fc1": b_fc1, "w_fc2": w_fc2, "out_grad": out_grad}


EPSILON = 1e-05
HIGHEST = lax.Precision.HIGHEST

@jax.custom_vjp
def low(v):
    return lax.optimization_barrier(v.astype(jnp.bfloat16)).astype(jnp.float32)

@jax.custom_vjp
def low_back(v):
    return v

def low_keep(v):
    return (low(v), None)

def low_pass(kept, grad):
    return (grad,)

def back_keep(v):
    return (v, None)

def back_low(kept, grad):
    return (low(grad),)
low.defvjp(low_keep, low_pass)
low_back.defvjp(back_keep, back_low)

def rotary_tables():
    half_rot = ROT // 2
    frequency = 10000.0 ** (-2.0 * jnp.arange(half_rot, dtype=jnp.float32) / ROT)
    angles = jnp.arange(SEQ, dtype=jnp.float32)[:, None] * frequency[None, :]
    return (jnp.cos(angles), jnp.sin(angles))

def rotate(tensor, cosine, sine_table):
    half_rot = ROT // 2
    first_half = tensor[..., :half_rot]
    second_half = tensor[..., half_rot:ROT]
    cos_rows = cosine[:, None, :]
    sin_rows = sine_table[:, None, :]
    return jnp.concatenate([first_half * cos_rows - second_half * sin_rows, second_half * cos_rows + first_half * sin_rows, tensor[..., ROT:]], axis=-1)

def sequence_out(inputs, ln_gain, ln_bias, out_bias, w_qkv, b_qkv, w_out, w_fc1, b_fc1, w_fc2):
    center = lax.optimization_barrier(jnp.mean(inputs, axis=-1, keepdims=True))
    centered = inputs - center
    variance = lax.optimization_barrier(jnp.mean(centered * centered, axis=-1, keepdims=True))
    normed = low(centered * lax.rsqrt(variance + EPSILON) * ln_gain + ln_bias)
    inner_width = H * HD
    group_inner = inner_width // N_TENSOR
    group_ff = FF // N_TENSOR
    normed_groups = jnp.stack([low_back(normed) for group in range(N_TENSOR)])
    merged = jnp.einsum('gsd,dcgj->scgj', normed_groups, w_qkv.reshape(D, 3, N_TENSOR, group_inner), precision=HIGHEST)
    merged = merged.reshape(SEQ, 3 * inner_width) + b_qkv.reshape(3 * inner_width)
    merged = low_back(merged).reshape(SEQ, 3, H, HD)
    cosine, sine_table = rotary_tables()
    queries = low(rotate(merged[:, 0], cosine, sine_table))
    keys = low(rotate(merged[:, 1], cosine, sine_table))
    values = low(merged[:, 2])
    block_rows = 512 if SEQ % 512 == 0 else SEQ
    positions = jnp.arange(SEQ, dtype=jnp.int32)
    scale = 1.0 / math.sqrt(HD)

    def attend_block(offset):
        q_rows = lax.dynamic_slice_in_dim(queries, offset, block_rows, 0)
        scores = low_back(jnp.einsum('qhd,khd->hqk', q_rows, keys, precision=HIGHEST) * scale)
        allowed = positions[None, :] <= (offset + positions[:block_rows])[:, None]
        scores = jnp.where(allowed[None], scores, -1e+30)
        row_max = lax.optimization_barrier(jnp.max(scores, axis=-1, keepdims=True))
        exp_scores = jnp.exp(scores - row_max)
        row_total = lax.optimization_barrier(jnp.sum(exp_scores, axis=-1, keepdims=True))
        probs_low = low(exp_scores / row_total)
        return jnp.einsum('hqk,khd->qhd', probs_low, values, precision=HIGHEST)
    offsets = jnp.arange(SEQ // block_rows, dtype=jnp.int32) * block_rows
    context = lax.map(jax.checkpoint(attend_block), offsets).reshape(SEQ, inner_width)
    context = low_back(low(context))
    hidden = jnp.einsum('gsd,dgf->sgf', normed_groups, w_fc1.reshape(D, N_TENSOR, group_ff), precision=HIGHEST)
    hidden = low_back(hidden.reshape(SEQ, FF) + b_fc1.reshape(FF))
    activation = low(jax.nn.gelu(hidden, approximate=True))
    attn_groups = jnp.einsum('sgi,gid->gsd', context.reshape(SEQ, N_TENSOR, group_inner), w_out.reshape(N_TENSOR, group_inner, D), precision=HIGHEST)
    mlp_groups = jnp.einsum('sgf,gfd->gsd', activation.reshape(SEQ, N_TENSOR, group_ff), w_fc2.reshape(N_TENSOR, group_ff, D), precision=HIGHEST)
    branch_partial = low(attn_groups + mlp_groups)
    branch = low_back(lax.optimization_barrier(jnp.sum(branch_partial, axis=0)))
    return inputs + branch + out_bias

def reference(layer_input, ln_gain, ln_bias, out_bias, w_qkv, b_qkv, w_out, w_fc1, b_fc1, w_fc2, out_grad):
    params = tuple((piece_arg.astype(jnp.float32) for piece_arg in (ln_gain, ln_bias, out_bias, w_qkv, b_qkv, w_out, w_fc1, b_fc1, w_fc2)))
    inputs = layer_input.astype(jnp.float32)

    def forward(all_inputs, *weights):

        def one_sequence(seq_rows):
            return sequence_out(seq_rows, *weights)
        return lax.map(jax.checkpoint(one_sequence), all_inputs)
    outputs, pullback = jax.vjp(forward, inputs, *params)
    gradients = pullback(out_grad.astype(jnp.float32))
    return (outputs.astype(jnp.bfloat16), gradients[0], gradients[1], gradients[2], gradients[3], gradients[4], gradients[5], gradients[6], gradients[7], gradients[8], gradients[9])
```

```python
import functools
import math

import jax
import jax.numpy as jnp
from jax import lax
from jax.experimental import pallas as pl
from jax.experimental.pallas import tpu as pltpu
from jax.sharding import PartitionSpec as P

HD = 64
ROT = 32
EPSILON = 1e-05
NEG = -1e30
LOG2E = math.log2(math.e)
BF = jnp.bfloat16
F32 = jnp.float32
VMEM_BYTES = 56 << 20

NN = (((1,), (0,)), ((), ()))
NT = (((1,), (1,)), ((), ()))
TN = (((0,), (0,)), ((), ()))


def dot(a, b, dims):
    return lax.dot_general(a, b, dims, preferred_element_type=F32)


def call(kernel, name, flops, moved, **kwargs):
    return pl.pallas_call(
        kernel,
        name=name,
        compiler_params=pltpu.CompilerParams(vmem_limit_bytes=VMEM_BYTES),
        cost_estimate=pl.CostEstimate(flops=int(flops), bytes_accessed=int(moved), transcendentals=0),
        **kwargs,
    )


def struct(shape, dtype=BF):
    return jax.ShapeDtypeStruct(shape, dtype)


def order_columns(blocks, x, g):
    rows, width = x.shape
    count = blocks.shape[0]
    cols = width // count

    def kernel(blk, x_ref, g_ref, xo_ref, go_ref, sum_ref):
        xo_ref[...] = x_ref[...]
        go_ref[...] = g_ref[...]
        total = jnp.sum(g_ref[...].astype(F32), axis=0, keepdims=True)
        sum_ref[...] = jnp.broadcast_to(total, (8, cols))

    source = pl.BlockSpec((rows, cols), lambda p, blk: (0, blk[p]))
    target = pl.BlockSpec((rows, cols), lambda p, blk: (0, p))
    return call(
        kernel,
        "order_columns",
        0,
        8 * rows * width,
        grid_spec=pltpu.PrefetchScalarGridSpec(
            num_scalar_prefetch=1,
            grid=(count,),
            in_specs=[source, source],
            out_specs=[target, target, pl.BlockSpec((8, cols), lambda p, blk: (0, blk[p]))],
        ),
        out_shape=[struct(x.shape), struct(x.shape), struct((8, width), F32)],
    )(blocks, x, g)


def rotary_rows(length):
    half = ROT // 2
    frequency = 10000.0 ** (-2.0 * jnp.arange(half, dtype=F32) / ROT)
    angles = jnp.arange(length, dtype=F32)[:, None] * frequency[None, :]
    cosine, sine = jnp.cos(angles), jnp.sin(angles)
    ones, zeros = jnp.ones((length, HD - ROT), F32), jnp.zeros((length, HD - ROT), F32)
    blank = jnp.zeros_like(sine)
    keep = jnp.concatenate([cosine, cosine, ones], axis=1)
    ahead = jnp.concatenate([-sine, blank, zeros], axis=1)
    behind = jnp.concatenate([blank, sine, zeros], axis=1)
    return tuple(jnp.concatenate([t, t], axis=1) for t in (keep, ahead, behind))


def turn(u, keep, ahead, behind):
    return u * keep + pltpu.roll(u, 128 - ROT // 2, 1) * ahead + pltpu.roll(u, ROT // 2, 1) * behind


def norm_project(out_blocks, pieces, rows, gain, shift, bias, tables, w_own, w_sib):
    width = pieces[0].shape[1]
    half = w_own.shape[0]
    inner = bias.shape[1] // 3
    starts, total = [], 0
    for piece in pieces:
        starts.append(total)
        total += piece.shape[0] // rows
    length = total * rows
    n = len(pieces)

    def kernel(blk, *refs):
        piece_refs = refs[:n]
        gain_ref, shift_ref, bias_ref, keep_ref, ahead_ref, behind_ref, wo_ref, ws_ref = refs[n : n + 8]
        normed_ref, unit_ref, qkv_ref, rows_ref = refs[n + 8 :]
        step = pl.program_id(0)
        for i in range(n):
            last = starts[i + 1] if i + 1 < n else total

            @pl.when((step >= starts[i]) & (step < last))
            def _(i=i):
                rows_ref[...] = piece_refs[i][...]

        x = rows_ref[...].astype(F32)
        centered = x - jnp.mean(x, axis=1, keepdims=True)
        variance = jnp.mean(centered * centered, axis=1, keepdims=True)
        unit = centered * lax.rsqrt(variance + EPSILON)
        unit_ref[...] = unit.astype(BF)
        normed = (unit * gain_ref[...] + shift_ref[...]).astype(BF)
        normed_ref[...] = normed
        for part in range(3):
            cols = slice(part * inner, (part + 1) * inner)
            merged = (
                dot(normed[:, :half], wo_ref[:, cols], NN)
                + dot(normed[:, half:], ws_ref[:, cols], NN)
                + bias_ref[:, cols]
            )
            for pair in range(inner // 128):
                u = merged[:, pair * 128 : (pair + 1) * 128]
                if part < 2:
                    u = turn(u, keep_ref[...], ahead_ref[...], behind_ref[...])
                start = part * inner + pair * 128
                qkv_ref[:, start : start + 128] = u.astype(BF)

    def piece_spec(i):
        count = pieces[i].shape[0] // rows
        return pl.BlockSpec((rows, width), lambda j, blk: (jnp.clip(j - starts[i], 0, count - 1), 0))

    def whole(shape):
        return pl.BlockSpec(shape, lambda j, blk: (0, 0))

    def placed(cols):
        return pl.BlockSpec((rows, cols), lambda j, blk: (blk[j], 0))

    return call(
        kernel,
        "norm_project",
        2 * length * width * 3 * inner,
        6 * length * width + 12 * width * inner,
        grid_spec=pltpu.PrefetchScalarGridSpec(
            num_scalar_prefetch=1,
            grid=(total,),
            in_specs=[piece_spec(i) for i in range(n)]
            + [whole((1, width)), whole((1, width)), whole((1, 3 * inner))]
            + [placed(128)] * 3
            + [whole((half, 3 * inner))] * 2,
            out_specs=[placed(width), placed(width), placed(3 * inner)],
            scratch_shapes=[pltpu.VMEM((rows, width), BF)],
        ),
        out_shape=[struct((length, width)), struct((length, width)), struct((length, 3 * inner))],
    )(out_blocks, *pieces, gain, shift, bias, *tables, w_own, w_sib)


def attend(qkv):
    length = qkv.shape[0]
    inner = qkv.shape[1] // 3
    pairs = inner // 128
    block = min(512, length)
    count = length // block
    scale = LOG2E / math.sqrt(HD)

    def kernel(q_ref, k_ref, v_ref, o_ref, lse_ref):
        lane = lax.broadcasted_iota(jnp.int32, (1, 128), 1)
        for index in range(count):

            @pl.when(pl.program_id(1) == index)
            def _(index=index):
                queries = q_ref[...]
                blank = jnp.zeros_like(queries)
                end = (index + 1) * block
                keys, values = k_ref[:end, :], v_ref[:end, :]
                found = []
                for head in range(2):
                    mine = (lane < HD) if head == 0 else (lane >= HD)
                    scores = dot(jnp.where(mine, queries, blank), keys, NT)
                    row = lax.broadcasted_iota(jnp.int32, (block, block), 0)
                    col = lax.broadcasted_iota(jnp.int32, (block, block), 1)
                    last = jnp.where(col <= row, scores[:, end - block :], NEG)
                    if index:
                        scores = jnp.concatenate([scores[:, : end - block], last], axis=1)
                    else:
                        scores = last
                    top = jnp.max(scores, axis=1, keepdims=True)
                    weights = jnp.exp2((scores - top) * scale)
                    total = jnp.sum(weights, axis=1, keepdims=True)
                    found.append((top, total, dot(weights.astype(BF), values, NN)))
                (top0, total0, out0), (top1, total1, out1) = found
                o_ref[...] = jnp.where(lane < HD, out0 / total0, out1 / total1).astype(BF)
                log_total = jnp.where(
                    lane < HD, top0 * scale + jnp.log2(total0), top1 * scale + jnp.log2(total1)
                ).T
                lse_ref[0, 0:1, :] = log_total[0:1, :]
                lse_ref[0, 1:2, :] = log_total[HD : HD + 1, :]

    return call(
        kernel,
        "attend",
        4 * length * length * inner,
        8 * length * inner,
        grid=(pairs, count),
        in_specs=[
            pl.BlockSpec((block, 128), lambda h, i: (i, h)),
            pl.BlockSpec((length, 128), lambda h, i: (0, pairs + h)),
            pl.BlockSpec((length, 128), lambda h, i: (0, 2 * pairs + h)),
        ],
        out_specs=[
            pl.BlockSpec((block, 128), lambda h, i: (i, h)),
            pl.BlockSpec((1, 2, block), lambda h, i: (h, 0, i)),
        ],
        out_shape=[struct((length, inner)), struct((pairs, 2, length), F32)],
    )(qkv, qkv, qkv)


def attend_back(qkv, context, context_grad, log_total, tables):
    length = qkv.shape[0]
    inner = qkv.shape[1] // 3
    pairs = inner // 128
    block = min(512, length)
    count = length // block
    scale = LOG2E / math.sqrt(HD)
    shrink = 1.0 / math.sqrt(HD)

    def kernel(q_ref, k_ref, v_ref, o_ref, do_ref, lse_ref, keep_ref, ahead_ref, behind_ref, *rest):
        dq_ref, dk_ref, dv_ref, sum_ref, k_total, v_total = rest
        step = pl.program_id(1)
        lane = lax.broadcasted_iota(jnp.int32, (1, 128), 1)
        rows_here = pl.ds(pl.multiple_of(step * block, block), block)

        @pl.when(step == 0)
        def _():
            k_total[...] = jnp.zeros_like(k_total)
            v_total[...] = jnp.zeros_like(v_total)
            sum_ref[...] = jnp.zeros_like(sum_ref)

        def turn_back(u, rows):
            return turn(u, keep_ref[rows, :], -ahead_ref[rows, :], -behind_ref[rows, :])

        for index in range(count):

            @pl.when(step == index)
            def _(index=index):
                queries, grads = q_ref[...], do_ref[...]
                blank = jnp.zeros_like(queries)
                products = (grads.astype(F32) * o_ref[...].astype(F32)).T
                q_total = [None, None]
                for other in range(index + 1):
                    rows = slice(other * block, (other + 1) * block)
                    keys, values = k_ref[rows, :], v_ref[rows, :]
                    dk, dv = k_total[rows, :], v_total[rows, :]
                    for head in range(2):
                        mine = (lane < HD) if head == 0 else (lane >= HD)
                        q_head = jnp.where(mine, queries, blank)
                        do_head = jnp.where(mine, grads, blank)
                        delta = jnp.sum(
                            products[head * HD : (head + 1) * HD], axis=0, keepdims=True
                        )
                        scores = dot(keys, q_head, NT)
                        if other == index:
                            row = lax.broadcasted_iota(jnp.int32, (block, block), 0)
                            col = lax.broadcasted_iota(jnp.int32, (block, block), 1)
                            scores = jnp.where(row <= col, scores, NEG)
                        probs = jnp.exp2(scores * scale - lse_ref[0, head : head + 1, :])
                        probs_grad = dot(values, do_head, NT)
                        score_grad = (probs * (probs_grad - delta)).astype(BF)
                        dv = dv + dot(probs.astype(BF), do_head, NN)
                        dk = dk + dot(score_grad, q_head, NN)
                        term = dot(score_grad, keys, TN)
                        q_total[head] = term if other == 0 else q_total[head] + term
                    k_total[rows, :] = dk
                    v_total[rows, :] = dv
                dq = jnp.where(lane < HD, q_total[0], q_total[1]) * shrink
                rows = slice(index * block, (index + 1) * block)
                dq = turn_back(dq, rows).astype(BF)
                dq_ref[...] = dq
                sum_ref[0, 0:1, :] += jnp.sum(dq.astype(F32), axis=0, keepdims=True)

        @pl.when(step == count - 1)
        def _():
            for index in range(count):
                rows = slice(index * block, (index + 1) * block)
                dk = turn_back(k_total[rows, :] * shrink, rows).astype(BF)
                dk_ref[rows, :] = dk
                sum_ref[0, 1:2, :] += jnp.sum(dk.astype(F32), axis=0, keepdims=True)
                dv = v_total[rows, :].astype(BF)
                dv_ref[rows, :] = dv
                sum_ref[0, 2:3, :] += jnp.sum(dv.astype(F32), axis=0, keepdims=True)

    def column(offset):
        return pl.BlockSpec((length, 128), lambda h, i: (0, offset + h))

    def rows_of(offset):
        return pl.BlockSpec((block, 128), lambda h, i: (i, offset + h))

    table = pl.BlockSpec((length, 128), lambda h, i: (0, 0))
    return call(
        kernel,
        "attend_back",
        10 * length * length * inner,
        16 * length * inner,
        grid=(pairs, count),
        in_specs=[
            rows_of(0),
            column(pairs),
            column(2 * pairs),
            rows_of(0),
            rows_of(0),
            pl.BlockSpec((1, 2, block), lambda h, i: (h, 0, i)),
            table,
            table,
            table,
        ],
        out_specs=[
            rows_of(0),
            column(0),
            column(0),
            pl.BlockSpec((1, 8, 128), lambda h, i: (h, 0, 0)),
        ],
        out_shape=[struct((length, inner))] * 3 + [struct((pairs, 8, 128), F32)],
        scratch_shapes=[pltpu.VMEM((length, 128), F32)] * 2,
    )(qkv, qkv, qkv, context, context_grad, log_total, *tables)


def expand(normed, w_own, w_sib, bias):
    length, width = normed.shape
    half, units = w_own.shape
    rows, cols = min(512, length), min(1024, units)

    def kernel(a_ref, wo_ref, ws_ref, b_ref, act_ref, slope_ref):
        hidden = (
            dot(a_ref[:, :half], wo_ref[...], NN)
            + dot(a_ref[:, half:], ws_ref[...], NN)
            + b_ref[...]
        )
        c = math.sqrt(2.0 / math.pi)
        square = hidden * hidden
        inner = hidden * (c + (c * 0.044715) * square)
        gate = 0.5 + 0.5 * jnp.tanh(inner)
        act = hidden * gate
        act_ref[...] = act.astype(BF)
        slope_ref[...] = (
            gate + act * (1.0 - gate) * (2.0 * c + (6.0 * c * 0.044715) * square)
        ).astype(BF)

    out = pl.BlockSpec((rows, cols), lambda n, m: (m, n))
    weight = pl.BlockSpec((half, cols), lambda n, m: (0, n))
    return call(
        kernel,
        "expand",
        2 * length * width * units,
        2 * length * width + 2 * width * units + 4 * length * units,
        grid=(units // cols, length // rows),
        in_specs=[
            pl.BlockSpec((rows, width), lambda n, m: (m, 0)),
            weight,
            weight,
            pl.BlockSpec((1, cols), lambda n, m: (0, n)),
        ],
        out_specs=[out, out],
        out_shape=[struct((length, units))] * 2,
    )(normed, w_own, w_sib, bias)


def hidden_back(g_all, w_own, w_sib, slope):
    length, width = g_all.shape
    half, units = w_own.shape
    rows, cols = min(512, length), min(1024, units)

    def kernel(g_ref, wo_ref, ws_ref, slope_ref, out_ref, sum_ref):
        grad = dot(g_ref[:, :half], wo_ref[...], NN) + dot(g_ref[:, half:], ws_ref[...], NN)
        low = (grad * slope_ref[...].astype(F32)).astype(BF)
        out_ref[...] = low

        @pl.when(pl.program_id(1) == 0)
        def _():
            sum_ref[...] = jnp.zeros_like(sum_ref)

        sum_ref[0:1, :] += jnp.sum(low.astype(F32), axis=0, keepdims=True)

    out = pl.BlockSpec((rows, cols), lambda n, m: (m, n))
    weight = pl.BlockSpec((half, cols), lambda n, m: (0, n))
    return call(
        kernel,
        "hidden_back",
        2 * length * width * units,
        2 * length * width + 2 * width * units + 4 * length * units,
        grid=(units // cols, length // rows),
        in_specs=[pl.BlockSpec((rows, width), lambda n, m: (m, 0)), weight, weight, out],
        out_specs=[out, pl.BlockSpec((8, cols), lambda n, m: (0, n))],
        out_shape=[struct((length, units)), struct((8, units), F32)],
    )(g_all, w_own, w_sib, slope)


def context_back(g_all, w_own, w_sib):
    length, width = g_all.shape
    half, cols = w_own.shape
    inner = cols // 4
    rows = min(512, length)

    def kernel(g_ref, wo_ref, ws_ref, out_ref):
        out_ref[...] = (
            dot(g_ref[:, :half], wo_ref[...], NN) + dot(g_ref[:, half:], ws_ref[...], NN)
        ).astype(BF)

    weight = pl.BlockSpec((half, inner), lambda m: (0, 3))
    return call(
        kernel,
        "context_back",
        2 * length * width * inner,
        2 * length * width + 2 * width * inner + 2 * length * inner,
        grid=(length // rows,),
        in_specs=[pl.BlockSpec((rows, width), lambda m: (m, 0)), weight, weight],
        out_specs=pl.BlockSpec((rows, inner), lambda m: (m, 0)),
        out_shape=struct((length, inner)),
    )(g_all, w_own, w_sib)


def weight_grad(rows_in, side, right, name):
    length, width = rows_in.shape
    half = width // 2
    units = right.shape[1]
    rows, cols = min(1024, half), min(1024, units)
    per_side = half // rows

    def kernel(a_ref, b_ref, out_ref):
        out_ref[...] = dot(a_ref[...], b_ref[...], TN).astype(BF)

    return call(
        kernel,
        name,
        2 * length * half * units,
        2 * length * half + 2 * length * units + 2 * half * units,
        grid=(units // cols, per_side),
        in_specs=[
            pl.BlockSpec((length, rows), lambda n, m: (0, side * per_side + m)),
            pl.BlockSpec((length, cols), lambda n, m: (0, n)),
        ],
        out_specs=pl.BlockSpec((rows, cols), lambda n, m: (m, n)),
        out_shape=struct((half, units)),
    )(rows_in, right)


def weight_grad_heads(normed, g_all, side, dq, dk, dv, context):
    length, width = normed.shape
    half = width // 2
    inner = dq.shape[1]

    def kernel(a_ref, g_ref, q_ref, k_ref, v_ref, c_ref, out_ref):
        for part, right in enumerate((q_ref, k_ref, v_ref, c_ref)):

            @pl.when(pl.program_id(0) == part)
            def _(part=part, right=right):
                left = a_ref if part < 3 else g_ref
                out_ref[...] = dot(left[...], right[...], TN).astype(BF)

    left = pl.BlockSpec((length, half), lambda n: (0, side))
    right = pl.BlockSpec((length, inner), lambda n: (0, 0))
    return call(
        kernel,
        "weight_grad_heads",
        8 * length * half * inner,
        4 * length * half + 8 * length * inner + 8 * half * inner,
        grid=(4,),
        in_specs=[left, left, right, right, right, right],
        out_specs=pl.BlockSpec((half, inner), lambda n: (0, n)),
        out_shape=struct((half, 4 * inner)),
    )(normed, g_all, dq, dk, dv, context)


def branch_half(act, context, w_fc2, w_heads):
    length, units = act.shape
    half = w_fc2.shape[0]
    inner = context.shape[1]
    rows = min(512, length)

    def kernel(a_ref, c_ref, w_ref, o_ref, out_ref):
        out_ref[...] = (dot(a_ref[...], w_ref[...], NT) + dot(c_ref[...], o_ref[...], NT)).astype(BF)

    return call(
        kernel,
        "branch_half",
        2 * length * half * (units + inner),
        2 * length * (units + inner) + 2 * half * (units + inner) + 2 * length * half,
        grid=(length // rows,),
        in_specs=[
            pl.BlockSpec((rows, units), lambda m: (m, 0)),
            pl.BlockSpec((rows, inner), lambda m: (m, 0)),
            pl.BlockSpec((half, units), lambda m: (0, 0)),
            pl.BlockSpec((half, inner), lambda m: (0, 3)),
        ],
        out_specs=pl.BlockSpec((rows, half), lambda m: (m, 0)),
        out_shape=struct((length, half)),
    )(act, context, w_fc2, w_heads)


def normed_back_half(dq, dk, dv, hidden_grad, unit, side, w_heads, w_fc1):
    length, inner = dq.shape
    half, units = w_fc1.shape
    rows = min(512, length)

    def kernel(q_ref, k_ref, v_ref, h_ref, u_ref, w_ref, f_ref, out_ref, sum_ref):
        total = dot(h_ref[...], f_ref[...], NT)
        for part, ref in enumerate((q_ref, k_ref, v_ref)):
            total = total + dot(ref[...], w_ref[:, part * inner : (part + 1) * inner], NT)
        low = total.astype(BF)
        out_ref[...] = low

        @pl.when(pl.program_id(0) == 0)
        def _():
            sum_ref[...] = jnp.zeros_like(sum_ref)

        wide = low.astype(F32)
        sum_ref[0:1, :] += jnp.sum(wide * u_ref[...].astype(F32), axis=0, keepdims=True)
        sum_ref[1:2, :] += jnp.sum(wide, axis=0, keepdims=True)

    head = pl.BlockSpec((rows, inner), lambda m: (m, 0))
    return call(
        kernel,
        "normed_back_half",
        2 * length * half * (units + 3 * inner),
        2 * length * (units + 3 * inner) + 2 * half * (units + 3 * inner) + 4 * length * half,
        grid=(length // rows,),
        in_specs=[
            head,
            head,
            head,
            pl.BlockSpec((rows, units), lambda m: (m, 0)),
            pl.BlockSpec((rows, half), lambda m: (m, side)),
            pl.BlockSpec((half, 3 * inner), lambda m: (0, 0)),
            pl.BlockSpec((half, units), lambda m: (0, 0)),
        ],
        out_specs=[
            pl.BlockSpec((rows, half), lambda m: (m, 0)),
            pl.BlockSpec((8, half), lambda m: (0, 0)),
        ],
        out_shape=[struct((length, half)), struct((8, half), F32)],
    )(dq, dk, dv, hidden_grad, unit, w_heads, w_fc1)


def add_branch(blocks, x, own, sib, out_bias):
    rows, width = x.shape
    count = blocks.shape[0]
    cols = width // count
    per_half = count // 2

    def kernel(blk, x_ref, own_ref, sib_ref, bias_ref, out_ref):
        step = pl.program_id(0)
        base = x_ref[...].astype(F32)

        @pl.when(step < per_half)
        def _():
            out_ref[...] = (base + own_ref[...].astype(F32) + bias_ref[...]).astype(BF)

        @pl.when(step >= per_half)
        def _():
            out_ref[...] = (base + sib_ref[...].astype(F32) + bias_ref[...]).astype(BF)

    return call(
        kernel,
        "add_branch",
        0,
        6 * rows * width,
        grid_spec=pltpu.PrefetchScalarGridSpec(
            num_scalar_prefetch=1,
            grid=(count,),
            in_specs=[
                pl.BlockSpec((rows, cols), lambda p, blk: (0, p)),
                pl.BlockSpec((rows, cols), lambda p, blk: (0, jnp.minimum(p, per_half - 1))),
                pl.BlockSpec((rows, cols), lambda p, blk: (0, jnp.maximum(p - per_half, 0))),
                pl.BlockSpec((1, cols), lambda p, blk: (0, p)),
            ],
            out_specs=pl.BlockSpec((rows, cols), lambda p, blk: (0, blk[p])),
        ),
        out_shape=struct((rows, width)),
    )(blocks, x, own, sib, out_bias)


def norm_back(blocks, x, g, own, sib, gain):
    length, width = x.shape
    half = width // 2
    count = blocks.shape[0]
    cols = width // count
    rows = min(128, length)

    def kernel(blk, x_ref, g_ref, own_ref, sib_ref, gain_ref, out_ref):
        x = x_ref[...].astype(F32)
        centered = x - jnp.mean(x, axis=1, keepdims=True)
        variance = jnp.mean(centered * centered, axis=1, keepdims=True)
        inv_std = lax.rsqrt(variance + EPSILON)
        unit = centered * inv_std
        grads = jnp.concatenate([own_ref[...].astype(F32), sib_ref[...].astype(F32)], axis=1)
        scaled = grads * gain_ref[...]
        mean = jnp.mean(scaled, axis=1, keepdims=True)
        along = jnp.mean(scaled * unit, axis=1, keepdims=True)
        result = g_ref[...].astype(F32) + inv_std * (scaled - mean - unit * along)
        for p in range(count):
            place = pl.ds(pl.multiple_of(blk[p] * cols, cols), cols)
            out_ref[:, place] = result[:, p * cols : (p + 1) * cols]

    full = pl.BlockSpec((rows, width), lambda m, blk: (m, 0))
    part = pl.BlockSpec((rows, half), lambda m, blk: (m, 0))
    return call(
        kernel,
        "norm_back",
        0,
        10 * length * width,
        grid_spec=pltpu.PrefetchScalarGridSpec(
            num_scalar_prefetch=1,
            grid=(length // rows,),
            in_specs=[full, full, part, part, pl.BlockSpec((1, width), lambda m, blk: (0, 0))],
            out_specs=full,
        ),
        out_shape=struct((length, width), F32),
    )(blocks, x, g, own, sib, gain)


def flip_sum(value, axis, size, first=1):
    bit = first
    while bit < size:
        value = value + lax.ppermute(value, axis, [(i, i ^ bit) for i in range(size)])
        bit *= 2
    return value


def per_device(
    sizes, layer_input, ln_gain, ln_bias, out_bias, w_qkv, b_qkv, w_out, w_fc1, b_fc1, w_fc2, out_grad
):
    n_dp, n_tensor = sizes
    chips = n_dp // 2
    ring = [(z * 2 + c, ((z + 1) % chips) * 2 + c) for z in range(chips) for c in range(2)]
    swap = [(i, i ^ 1) for i in range(n_dp)]
    d_index, t_index = lax.axis_index("dp"), lax.axis_index("tensor")
    place, core = d_index // 2, d_index % 2
    steps = jnp.arange(chips, dtype=jnp.int32)
    behind = ((place - steps) % chips) * 2
    blocks = jnp.concatenate([behind + core, behind + (1 - core)]).astype(jnp.int32)

    local, width = layer_input.shape[1:]
    depth = w_qkv.shape[0]
    inner = w_qkv.shape[2]
    units = w_fc1.shape[1]
    heads = inner // HD
    length = local * n_tensor

    group_heads = jnp.concatenate([w_qkv.reshape(depth, 3 * inner), w_out.T], axis=1)
    groups = [group_heads, w_fc1, w_fc2.T]

    def gather(piece):
        pieces = [piece]
        for _ in range(chips - 1):
            pieces.append(lax.ppermute(pieces[-1], "dp", ring))
        own = jnp.concatenate(pieces, axis=0)
        return own, lax.ppermute(own, "dp", swap)

    third = ln_gain.shape[0]
    vectors = jnp.stack([ln_gain, ln_bias, out_bias]).astype(F32).reshape(1, 3 * third)
    table = jnp.where(jnp.arange(n_tensor)[:, None] == t_index, vectors, 0.0)
    table = flip_sum(table, "tensor", n_tensor)
    packed = jnp.concatenate(
        [table.reshape(-1), b_qkv.astype(F32).reshape(-1), b_fc1.astype(F32).reshape(-1)]
    )[None, :]
    packed = jnp.where(jnp.arange(n_dp)[:, None] == d_index, packed, 0.0)
    packed = flip_sum(packed, "dp", n_dp)
    cut = n_tensor * 3 * third
    vectors = packed[:, :cut].reshape(n_dp, n_tensor, 3, third)
    vectors = jnp.transpose(vectors, (2, 0, 1, 3)).reshape(3, n_dp, n_tensor * third)
    chosen = (blocks[:, None] == jnp.arange(n_dp)[None, :]).astype(F32)
    vectors = jnp.einsum("pd,kdj->kpj", chosen, vectors, precision=lax.Precision.HIGHEST)
    gain, shift, bias_out = (vectors[i].reshape(1, width) for i in range(3))
    tail = cut + b_qkv.size
    bias_qkv = jnp.transpose(packed[:, cut:tail].reshape(n_dp, 3, heads, -1), (1, 2, 0, 3))
    bias_qkv = bias_qkv.reshape(1, 3 * inner)
    bias_fc1 = jnp.transpose(packed[:, tail:].reshape(n_dp, units // HD, -1), (1, 0, 2))
    bias_fc1 = bias_fc1.reshape(1, units)

    x, g, bias_part = order_columns(blocks, layer_input[0], out_grad[0])
    rows = min(256, local)
    x_all = lax.all_gather(x, "tensor", axis=0, tiled=True)
    pieces, out_blocks = [x_all], jnp.arange(length // rows, dtype=jnp.int32)
    g_all = lax.all_gather(g, "tensor", axis=0, tiled=True)

    heads_own, heads_sib = gather(groups[0])
    tables = rotary_rows(length)
    normed, unit, qkv = norm_project(
        out_blocks, pieces, rows, gain, shift, bias_qkv, tables, heads_own, heads_sib
    )
    context, log_total = attend(qkv)

    fc1_own, fc1_sib = gather(groups[1])
    act, slope = expand(normed, fc1_own, fc1_sib, bias_fc1)

    def scatter(sib_part, own_part):
        other = lax.ppermute(sib_part, "dp", swap)

        def step(k):
            cut = slice(k * depth, (k + 1) * depth)
            return own_part[cut].astype(F32) + other[cut].astype(F32)

        moving = None
        for k in list(range(1, chips)) + [0]:
            total = step(k) if moving is None else step(k) + moving.astype(F32)
            if k:
                moving = lax.ppermute(total.astype(BF), "dp", ring)
        return total.astype(BF).astype(F32) if chips == 1 else total

    fc2_sib_grad = weight_grad(g_all, 1, act, "fc2_grad")
    fc2_own_grad = weight_grad(g_all, 0, act, "fc2_grad")
    w_fc2_grad = scatter(fc2_sib_grad, fc2_own_grad).T

    context_grad = context_back(g_all, heads_own, heads_sib)
    fc2_own, fc2_sib = gather(groups[2])
    hidden_grad, b_fc1_part = hidden_back(g_all, fc2_own, fc2_sib, slope)
    fc1_sib_grad = weight_grad(normed, 1, hidden_grad, "fc1_grad")
    fc1_own_grad = weight_grad(normed, 0, hidden_grad, "fc1_grad")
    w_fc1_grad = scatter(fc1_sib_grad, fc1_own_grad)

    branch = [
        lax.psum_scatter(
            branch_half(act, context, w2, wh), "tensor", scatter_dimension=0, tiled=True
        )
        for w2, wh in ((fc2_own, heads_own), (fc2_sib, heads_sib))
    ]
    layer_output = add_branch(blocks, x, branch[0], branch[1], bias_out)

    dq, dk, dv, b_qkv_part = attend_back(qkv, context, context_grad, log_total, tables)
    back = [
        normed_back_half(dq, dk, dv, hidden_grad, unit, side, wh, w1)
        for side, wh, w1 in ((0, heads_own, fc1_own), (1, heads_sib, fc1_sib))
    ]
    normed_sum = [
        lax.psum_scatter(part, "tensor", scatter_dimension=0, tiled=True) for part, _ in back
    ]
    heads_sib_grad = weight_grad_heads(normed, g_all, 1, dq, dk, dv, context)
    heads_own_grad = weight_grad_heads(normed, g_all, 0, dq, dk, dv, context)
    heads_grad = scatter(heads_sib_grad, heads_own_grad)
    w_qkv_grad = heads_grad[:, : 3 * inner].reshape(depth, 3, inner)
    w_out_grad = heads_grad[:, 3 * inner :].T

    input_grad = norm_back(blocks, x, g, normed_sum[0], normed_sum[1], gain)

    norm_sums = jnp.concatenate([back[0][1][:2], back[1][1][:2]], axis=1).reshape(2, n_dp, depth)
    norm_sums = jnp.einsum("pd,kpj->kdj", chosen, norm_sums, precision=lax.Precision.HIGHEST)
    vector_sums = jnp.concatenate([norm_sums.reshape(2, width), bias_part[:1]], axis=0)
    vector_sums = flip_sum(vector_sums, "tensor", n_tensor)
    unit_sums = jnp.concatenate(
        [
            vector_sums.reshape(-1),
            jnp.transpose(b_qkv_part[:, :3, :], (1, 0, 2)).reshape(-1),
            b_fc1_part[0],
        ]
    )
    unit_sums = flip_sum(unit_sums, "dp", n_dp)
    mine = unit_sums[: 3 * width].reshape(3, n_dp * n_tensor, third)
    mine = lax.dynamic_index_in_dim(mine, d_index * n_tensor + t_index, 1, keepdims=False)
    b_width = HD // n_dp
    b_qkv_grad = lax.dynamic_slice_in_dim(
        unit_sums[3 * width : 3 * width + 3 * inner].reshape(3, heads, HD), d_index * b_width, b_width, 2
    )
    b_fc1_grad = lax.dynamic_slice_in_dim(
        unit_sums[3 * width + 3 * inner :].reshape(units // HD, HD), d_index * b_width, b_width, 1
    )
    return (
        layer_output[None],
        input_grad[None],
        mine[0],
        mine[1],
        mine[2],
        w_qkv_grad,
        b_qkv_grad,
        w_out_grad,
        w_fc1_grad,
        b_fc1_grad,
        w_fc2_grad,
    )


def solution(mesh):
    in_specs = (
        P("dp", "tensor", None),
        P(("dp", "tensor")),
        P(("dp", "tensor")),
        P(("dp", "tensor")),
        P("dp", None, "tensor"),
        P(None, "tensor", "dp"),
        P("tensor", "dp"),
        P("dp", "tensor"),
        P("tensor", "dp"),
        P("tensor", "dp"),
        P("dp", "tensor", None),
    )
    out_specs = (
        P("dp", "tensor", None),
        P("dp", "tensor", None),
        P(("dp", "tensor")),
        P(("dp", "tensor")),
        P(("dp", "tensor")),
        P("dp", None, "tensor"),
        P(None, "tensor", "dp"),
        P("tensor", "dp"),
        P("dp", "tensor"),
        P("tensor", "dp"),
        P("tensor", "dp"),
    )
    sizes = (mesh.shape["dp"], mesh.shape["tensor"])
    return jax.shard_map(
        functools.partial(per_device, sizes),
        mesh=mesh,
        in_specs=in_specs,
        out_specs=out_specs,
        check_vma=False,
    )
```

```python
import functools
import math

import jax
import jax.numpy as jnp
from jax import lax
from jax.experimental import pallas as pl
from jax.experimental.pallas import tpu as pltpu
from jax.sharding import PartitionSpec as P

HD = 64
ROT = 32
EPSILON = 1e-05
NEG = -1e30
LOG2E = math.log2(math.e)
BF = jnp.bfloat16
F32 = jnp.float32
VMEM_BYTES = 56 << 20

NN = (((1,), (0,)), ((), ()))
NT = (((1,), (1,)), ((), ()))
TN = (((0,), (0,)), ((), ()))


def dot(a, b, dims):
    return lax.dot_general(a, b, dims, preferred_element_type=F32)


def call(kernel, name, flops, moved, operands, grid, in_specs, out_specs, out_shape, scratch=(), prefetch=(), aliases=None, after=()):
    front = len(prefetch) + len(in_specs)

    def body(*refs):
        kernel(*refs[:front], *refs[front + len(after) :])

    return pl.pallas_call(
        body,
        name=name,
        grid_spec=pltpu.PrefetchScalarGridSpec(
            num_scalar_prefetch=len(prefetch),
            grid=grid,
            in_specs=list(in_specs) + [pl.BlockSpec(memory_space=pl.ANY)] * len(after),
            out_specs=out_specs,
            scratch_shapes=list(scratch),
        ),
        out_shape=out_shape,
        input_output_aliases=aliases or {},
        compiler_params=pltpu.CompilerParams(vmem_limit_bytes=VMEM_BYTES),
        cost_estimate=pl.CostEstimate(flops=int(flops), bytes_accessed=int(moved), transcendentals=0),
    )(*prefetch, *operands, *after)


class Weights:
    def __init__(self, arrays, placed=False):
        self.arrays = list(arrays)
        self.placed = placed
        self.cols = self.arrays[0].shape[1]
        self.rows = sum(a.shape[0] for a in self.arrays)

    def copies(self, refs, blk, count, side, col, cols, target, sems):
        found = []

        def add(source, start, size, place):
            found.append(
                pltpu.make_async_copy(
                    source.at[pl.ds(start, size), pl.ds(col, cols)],
                    target.at[pl.ds(place, size), :],
                    sems.at[len(found)],
                )
            )

        half = self.rows // 2
        if self.placed:
            size = self.rows // count
            first, last = (0, count) if side is None else (side * count // 2, (side + 1) * count // 2)
            for p in range(first, last):
                add(refs[0], pl.multiple_of(blk[p] * size, size), size, (p - first) * size)
            return found
        place = 0
        for ref, array in zip(refs, self.arrays):
            size = array.shape[0]
            if side is None or place // half == side:
                add(ref, 0, size, place - (side or 0) * half)
            place += size
        return found

    def number(self, count, side=None):
        total = count if self.placed else len(self.arrays)
        return total if side is None else total // 2


def struct(shape, dtype=BF):
    return jax.ShapeDtypeStruct(shape, dtype)


def tie(values, after):
    n = len(values)
    anywhere = pl.BlockSpec(memory_space=pl.ANY)

    def kernel(*refs):
        del refs

    return pl.pallas_call(
        kernel,
        name="tie",
        in_specs=[anywhere] * (n + len(after)),
        out_specs=[anywhere] * n,
        out_shape=[struct(v.shape, v.dtype) for v in values],
        input_output_aliases={i: i for i in range(n)},
    )(*values, *after)


def order_columns(blocks, x, after=()):
    rows, width = x.shape
    count = blocks.shape[0]
    cols = width // count
    step_rows = min(256, rows)

    def kernel(blk, x_ref, out_ref, sum_ref):
        for p in range(count):
            place = pl.ds(pl.multiple_of(blk[p] * cols, cols), cols)
            out_ref[:, p * cols : (p + 1) * cols] = x_ref[:, place]

        @pl.when(pl.program_id(0) == 0)
        def _():
            sum_ref[...] = jnp.zeros_like(sum_ref)

        sum_ref[0:1, :] += jnp.sum(x_ref[...].astype(F32), axis=0, keepdims=True)

    block = pl.BlockSpec((step_rows, width), lambda m, blk: (m, 0))
    return call(
        kernel,
        "order_columns",
        0,
        4 * rows * width,
        (x,),
        (rows // step_rows,),
        [block],
        [block, pl.BlockSpec((8, width), lambda m, blk: (0, 0))],
        [struct(x.shape), struct((8, width), F32)],
        prefetch=(blocks,),
        after=after,
    )


def heads_shard(w_qkv, w_out, after):
    depth, wide = w_qkv.shape
    inner = w_out.shape[0]

    def kernel(q_ref, o_ref, out_ref):
        out_ref[:, :wide] = q_ref[...]
        out_ref[:, wide:] = o_ref[...].T

    return call(
        kernel,
        "heads_shard",
        0,
        4 * depth * (wide + inner),
        (w_qkv, w_out),
        (1,),
        [pl.BlockSpec(w_qkv.shape, lambda i: (0, 0)), pl.BlockSpec(w_out.shape, lambda i: (0, 0))],
        pl.BlockSpec((depth, wide + inner), lambda i: (0, 0)),
        struct((depth, wide + inner)),
        after=after,
    )


def stage(weight, flip, after, rows=None):
    start, count = rows or (0, weight.shape[0])
    taken = (count, weight.shape[1])
    shape = taken[::-1] if flip else taken

    def kernel(w_ref, out_ref):
        out_ref[...] = w_ref[...].T if flip else w_ref[...]

    return call(
        kernel,
        "stage_weight",
        0,
        4 * taken[0] * taken[1],
        (weight,),
        (1,),
        [pl.BlockSpec(taken, lambda i: (start // count, 0))],
        pl.BlockSpec(shape, lambda i: (0, 0)),
        struct(shape),
        after=after,
    )


def rotary_rows(length):
    lane = jnp.arange(128, dtype=jnp.int32)[None, :] % HD
    half = ROT // 2
    frequency = 10000.0 ** (-2.0 * (lane % half).astype(F32) / ROT)
    angles = jnp.arange(length, dtype=F32)[:, None] * frequency
    cosine, sine = jnp.cos(angles), jnp.sin(angles)
    keep = jnp.where(lane < ROT, cosine, 1.0)
    ahead = jnp.where(lane < half, -sine, 0.0)
    behind = jnp.where((lane >= half) & (lane < ROT), sine, 0.0)
    return keep, ahead, behind


def turn(u, keep, ahead, behind):
    return u * keep + pltpu.roll(u, 128 - ROT // 2, 1) * ahead + pltpu.roll(u, ROT // 2, 1) * behind


def norm_project(blocks, out_blocks, pieces, rows, gain, shift, bias, tables, weights, after=()):
    width = pieces[0].shape[1]
    wide = bias.shape[1]
    inner = wide // 3
    starts, total = [], 0
    for piece in pieces:
        starts.append(total)
        total += piece.shape[0] // rows
    length = total * rows
    n, k, count = len(pieces), len(weights.arrays), blocks.shape[0]

    def kernel(blk, places, *refs):
        piece_refs = refs[:n]
        gain_ref, shift_ref, bias_ref, keep_ref, ahead_ref, behind_ref = refs[n : n + 6]
        w_refs = refs[n + 6 : n + 6 + k]
        normed_ref, unit_ref, qkv_ref, rows_ref, w_ref, sems = refs[n + 6 + k :]
        step = pl.program_id(0)
        copies = weights.copies(w_refs, blk, count, None, 0, wide, w_ref, sems)

        @pl.when(step == 0)
        def _():
            for copy in copies:
                copy.start()

        for i in range(n):
            last = starts[i + 1] if i + 1 < n else total

            @pl.when((step >= starts[i]) & (step < last))
            def _(i=i):
                rows_ref[...] = piece_refs[i][...]

        x = rows_ref[...].astype(F32)
        centered = x - jnp.mean(x, axis=1, keepdims=True)
        variance = jnp.mean(centered * centered, axis=1, keepdims=True)
        unit = centered * lax.rsqrt(variance + EPSILON)
        unit_ref[...] = unit.astype(BF)
        normed = (unit * gain_ref[...] + shift_ref[...]).astype(BF)
        normed_ref[...] = normed

        @pl.when(step == 0)
        def _():
            for copy in copies:
                copy.wait()

        for part in range(3):
            cols = slice(part * inner, (part + 1) * inner)
            merged = dot(normed_ref[...], w_ref[:, cols], NN) + bias_ref[:, cols]
            for pair in range(inner // 128):
                u = merged[:, pair * 128 : (pair + 1) * 128]
                if part < 2:
                    u = turn(u, keep_ref[...], ahead_ref[...], behind_ref[...])
                start = part * inner + pair * 128
                qkv_ref[:, start : start + 128] = u.astype(BF)

    def piece_spec(i):
        number = pieces[i].shape[0] // rows
        return pl.BlockSpec((rows, width), lambda j, b, o: (jnp.clip(j - starts[i], 0, number - 1), 0))

    def whole(shape):
        return pl.BlockSpec(shape, lambda j, b, o: (0, 0))

    def placed(cols):
        return pl.BlockSpec((rows, cols), lambda j, b, o: (o[j], 0))

    return call(
        kernel,
        "norm_project",
        3 * length * width * wide,
        6 * length * width + 4 * width * wide,
        (*pieces, gain, shift, bias, *tables, *weights.arrays),
        (total,),
        [piece_spec(i) for i in range(n)]
        + [whole((1, width)), whole((1, width)), whole((1, wide))]
        + [placed(128)] * 3
        + [pl.BlockSpec(memory_space=pl.ANY)] * k,
        [placed(width), placed(width), placed(wide)],
        [struct((length, width)), struct((length, width)), struct((length, wide))],
        scratch=[
            pltpu.VMEM((rows, width), BF),
            pltpu.VMEM((width, wide), BF),
            pltpu.SemaphoreType.DMA((weights.number(count),)),
        ],
        prefetch=(blocks, out_blocks),
        after=after,
    )


def attend(qkv, first, number, before=None, after=()):
    length = qkv.shape[0]
    inner = qkv.shape[1] // 3
    pairs = inner // 128
    block = min(512, length)
    count = length // block
    scale = LOG2E / math.sqrt(HD)
    n = 0 if before is None else 1

    def kernel(q_ref, k_ref, v_ref, *refs):
        o_ref, lse_ref, turned_ref = refs[n:]
        lane = lax.broadcasted_iota(jnp.int32, (1, 128), 1)

        @pl.when(pl.program_id(1) == 0)
        def _():
            turned_ref[...] = v_ref[...].T

        for index in range(count):

            @pl.when(pl.program_id(1) == index)
            def _(index=index):
                queries = q_ref[...]
                blank = jnp.zeros_like(queries)
                end = (index + 1) * block
                found = []
                for head in range(2):
                    mine = (lane < HD) if head == 0 else (lane >= HD)
                    scores = dot(k_ref[:end, :], jnp.where(mine, queries, blank), NT)
                    row = lax.broadcasted_iota(jnp.int32, (block, block), 0)
                    col = lax.broadcasted_iota(jnp.int32, (block, block), 1)
                    last = jnp.where(row <= col, scores[end - block :], NEG)
                    if index:
                        scores = jnp.concatenate([scores[: end - block], last], axis=0)
                    else:
                        scores = last
                    top = jnp.max(scores, axis=0, keepdims=True)
                    weights = jnp.exp2((scores - top) * scale)
                    total = jnp.sum(weights, axis=0, keepdims=True)
                    out = dot(turned_ref[head * HD : (head + 1) * HD, :end], weights.astype(BF), NN)
                    found.append(out / total)
                    lse_ref[0, head : head + 1, :] = top * scale + jnp.log2(total)
                o_ref[...] = jnp.concatenate(found, axis=0).T.astype(BF)

    return call(
        kernel,
        "attend",
        40 * length * length * 128 * number,
        8 * length * 128 * number,
        (qkv, qkv, qkv) + ((before,) if n else ()),
        (number, count),
        [
            pl.BlockSpec((block, 128), lambda h, i: (i, first + h)),
            pl.BlockSpec((length, 128), lambda h, i: (0, pairs + first + h)),
            pl.BlockSpec((length, 128), lambda h, i: (0, 2 * pairs + first + h)),
        ]
        + [pl.BlockSpec(memory_space=pl.ANY)] * n,
        [
            pl.BlockSpec((block, 128), lambda h, i: (i, first + h)),
            pl.BlockSpec((1, 2, block), lambda h, i: (h, 0, i)),
        ],
        [struct((length, inner)), struct((number, 2, length), F32)],
        scratch=[pltpu.VMEM((128, length), BF)],
        aliases={3: 0} if n else {},
        after=after,
    )


def attend_back(qkv, context, context_grad, log_total, tables, after=()):
    length = qkv.shape[0]
    inner = qkv.shape[1] // 3
    pairs = inner // 128
    block = min(512, length)
    count = length // block
    scale = LOG2E / math.sqrt(HD)
    shrink = 1.0 / math.sqrt(HD)

    def kernel(q_ref, k_ref, v_ref, o_ref, do_ref, lse_ref, keep_ref, ahead_ref, behind_ref, *rest):
        dq_ref, dk_ref, dv_ref, sum_ref, k_total, v_total = rest
        step = pl.program_id(1)
        lane = lax.broadcasted_iota(jnp.int32, (1, 128), 1)

        @pl.when(step == 0)
        def _():
            k_total[...] = jnp.zeros_like(k_total)
            v_total[...] = jnp.zeros_like(v_total)
            sum_ref[...] = jnp.zeros_like(sum_ref)

        def turn_back(u, rows):
            return turn(u, keep_ref[rows, :], -ahead_ref[rows, :], -behind_ref[rows, :])

        for index in range(count):

            @pl.when(step == index)
            def _(index=index):
                queries, grads = q_ref[...], do_ref[...]
                blank = jnp.zeros_like(queries)
                queries_turned, grads_turned = queries.T, grads.T
                products = grads.astype(F32) * o_ref[...].astype(F32)
                log_totals = lse_ref[0].T
                q_total = [None, None]
                for other in range(index + 1):
                    rows = slice(other * block, (other + 1) * block)
                    keys, values = k_ref[rows, :], v_ref[rows, :]
                    for head in range(2):
                        mine = (lane < HD) if head == 0 else (lane >= HD)
                        here = slice(head * HD, (head + 1) * HD)
                        delta = jnp.sum(products[:, here], axis=1, keepdims=True)
                        scores = dot(jnp.where(mine, queries, blank), keys, NT)
                        if other == index:
                            row = lax.broadcasted_iota(jnp.int32, (block, block), 0)
                            col = lax.broadcasted_iota(jnp.int32, (block, block), 1)
                            scores = jnp.where(col <= row, scores, NEG)
                        probs = jnp.exp2(scores * scale - log_totals[:, head : head + 1])
                        probs_grad = dot(jnp.where(mine, grads, blank), values, NT)
                        score_grad = (probs * (probs_grad - delta)).astype(BF)
                        v_total[here, rows] += dot(grads_turned[here, :], probs.astype(BF), NN)
                        k_total[here, rows] += dot(queries_turned[here, :], score_grad, NN)
                        term = dot(score_grad, keys, NN)
                        q_total[head] = term if other == 0 else q_total[head] + term
                dq = jnp.where(lane < HD, q_total[0], q_total[1]) * shrink
                rows = slice(index * block, (index + 1) * block)
                dq = turn_back(dq, rows).astype(BF)
                dq_ref[...] = dq
                sum_ref[0, 0:1, :] += jnp.sum(dq.astype(F32), axis=0, keepdims=True)

        @pl.when(step == count - 1)
        def _():
            for index in range(count):
                rows = slice(index * block, (index + 1) * block)
                dk = turn_back(k_total[:, rows].T * shrink, rows).astype(BF)
                dk_ref[rows, :] = dk
                sum_ref[0, 1:2, :] += jnp.sum(dk.astype(F32), axis=0, keepdims=True)
                dv = v_total[:, rows].T.astype(BF)
                dv_ref[rows, :] = dv
                sum_ref[0, 2:3, :] += jnp.sum(dv.astype(F32), axis=0, keepdims=True)

    def column(offset):
        return pl.BlockSpec((length, 128), lambda h, i: (0, offset + h))

    def rows_of(offset):
        return pl.BlockSpec((block, 128), lambda h, i: (i, offset + h))

    table = pl.BlockSpec((length, 128), lambda h, i: (0, 0))
    return call(
        kernel,
        "attend_back",
        60 * length * length * inner,
        16 * length * inner,
        (qkv, qkv, qkv, context, context_grad, log_total, *tables),
        (pairs, count),
        [
            rows_of(0),
            column(pairs),
            column(2 * pairs),
            rows_of(0),
            rows_of(0),
            pl.BlockSpec((1, 2, block), lambda h, i: (h, 0, i)),
            table,
            table,
            table,
        ],
        [rows_of(0), column(0), column(0), pl.BlockSpec((1, 8, 128), lambda h, i: (h, 0, 0))],
        [struct((length, inner))] * 3 + [struct((pairs, 8, 128), F32)],
        scratch=[pltpu.VMEM((128, length), F32)] * 2,
        after=after,
    )


def times_weights(blocks, rows_in, weights, col, total_cols, name, extra, outs, finish, after=()):
    length, width = rows_in.shape
    rows, cols = min(512, length), min(1024, total_cols)
    chunks = total_cols // cols
    k, count, e = len(weights.arrays), blocks.shape[0], len(extra)
    number = weights.number(count)

    def kernel(blk, a_ref, *refs):
        w_refs, extra_refs, out_refs = refs[:k], refs[k : k + e], refs[k + e : -2]
        w_ref, sems = refs[-2:]
        copies = [
            weights.copies(w_refs, blk, count, None, col + c * cols, cols, w_ref.at[c], sems.at[c])
            for c in range(chunks)
        ]

        @pl.when((pl.program_id(0) == 0) & (pl.program_id(1) == 0))
        def _():
            for chunk in copies:
                for copy in chunk:
                    copy.start()

        for c in range(chunks):

            @pl.when((pl.program_id(0) == c) & (pl.program_id(1) == 0))
            def _(c=c):
                for copy in copies[c]:
                    copy.wait()

        finish(dot(a_ref[...], w_ref[pl.program_id(0)], NN), extra_refs, out_refs)

    specs = {
        "block": pl.BlockSpec((rows, cols), lambda n, m, blk: (m, n)),
        "row": pl.BlockSpec((1, cols), lambda n, m, blk: (0, n)),
        "sum": pl.BlockSpec((8, cols), lambda n, m, blk: (0, n)),
    }
    shapes = {"block": struct((length, total_cols)), "sum": struct((8, total_cols), F32)}
    return call(
        kernel,
        name,
        2 * length * width * total_cols,
        2 * length * width + 2 * width * total_cols + 4 * length * total_cols,
        (rows_in, *weights.arrays, *(value for _, value in extra)),
        (chunks, length // rows),
        [pl.BlockSpec((rows, width), lambda n, m, blk: (m, 0))]
        + [pl.BlockSpec(memory_space=pl.ANY)] * k
        + [specs[kind] for kind, _ in extra],
        [specs[kind] for kind in outs],
        [shapes[kind] for kind in outs],
        scratch=[
            pltpu.VMEM((chunks, width, cols), BF),
            pltpu.SemaphoreType.DMA((chunks, number)),
        ],
        prefetch=(blocks,),
        after=after,
    )


def expand(blocks, normed, weights, bias, after=()):
    def finish(product, extra_refs, out_refs):
        hidden = product + extra_refs[0][...]
        c = math.sqrt(2.0 / math.pi)
        square = hidden * hidden
        inner = hidden * (c + (c * 0.044715) * square)
        gate = 0.5 + 0.5 * jnp.tanh(inner)
        act = hidden * gate
        out_refs[0][...] = act.astype(BF)
        out_refs[1][...] = (
            gate + act * (1.0 - gate) * (2.0 * c + (6.0 * c * 0.044715) * square)
        ).astype(BF)

    return times_weights(
        blocks, normed, weights, 0, weights.cols, "expand", [("row", bias)], ["block", "block"], finish, after
    )


def hidden_back(blocks, g_all, weights, slope, after=()):
    def finish(product, extra_refs, out_refs):
        low = (product * extra_refs[0][...].astype(F32)).astype(BF)
        out_refs[0][...] = low

        @pl.when(pl.program_id(1) == 0)
        def _():
            out_refs[1][...] = jnp.zeros_like(out_refs[1])

        out_refs[1][0:1, :] += jnp.sum(low.astype(F32), axis=0, keepdims=True)

    return times_weights(
        blocks, g_all, weights, 0, weights.cols, "hidden_back", [("block", slope)], ["block", "sum"], finish, after
    )


def context_back(blocks, g_all, weights, after=()):
    inner = weights.cols // 4

    def finish(product, extra_refs, out_refs):
        out_refs[0][...] = product.astype(BF)

    return times_weights(
        blocks, g_all, weights, 3 * inner, inner, "context_back", [], ["block"], finish, after
    )[0]


def weight_grad(blocks, rows_in, rights, cols, name, after=()):
    length, width = rows_in.shape
    half = width // 2
    count = blocks.shape[0]
    depth = width // count
    starts, total = [], 0
    for right in rights:
        starts.append(total)
        total += right.shape[1] // cols
    n = len(rights)

    def kernel(blk, a_ref, *refs):
        out_ref = refs[n]
        chunk, side = pl.program_id(0), pl.program_id(1)
        for i in range(n):
            last = starts[i + 1] if i + 1 < n else total

            @pl.when((chunk >= starts[i]) & (chunk < last))
            def _(i=i):
                product = dot(a_ref[...], refs[i][...], TN).astype(BF)
                for p in range(count // 2):
                    place = pl.multiple_of(blk[side * (count // 2) + p] * depth, depth)
                    out_ref[pl.ds(place, depth), :] = product[p * depth : (p + 1) * depth]

    def right_spec(i):
        number = rights[i].shape[1] // cols
        return pl.BlockSpec(
            (length, cols), lambda n, s, blk: (0, jnp.clip(n - starts[i], 0, number - 1))
        )

    return call(
        kernel,
        name,
        2 * length * width * total * cols,
        2 * length * width + 4 * length * total * cols + 2 * width * total * cols,
        (rows_in, *rights),
        (total, 2),
        [pl.BlockSpec((length, half), lambda n, s, blk: (0, s))] + [right_spec(i) for i in range(n)],
        pl.BlockSpec((width, cols), lambda n, s, blk: (0, n)),
        struct((width, total * cols)),
        prefetch=(blocks,),
        after=after,
    )


def weight_grad_halves(rows_in, rights, cols, name, after=()):
    length, width = rows_in.shape
    half = width // 2
    starts, total = [], 0
    for right in rights:
        starts.append(total)
        total += right.shape[1] // cols
    n = len(rights)

    def kernel(a_ref, *refs):
        sib_ref, own_ref = refs[n:]
        side, chunk = pl.program_id(0), pl.program_id(1)
        for i in range(n):
            last = starts[i + 1] if i + 1 < n else total

            @pl.when((chunk >= starts[i]) & (chunk < last))
            def _(i=i):
                product = dot(a_ref[...], refs[i][...], TN).astype(BF)

                @pl.when(side == 0)
                def _():
                    sib_ref[...] = product

                @pl.when(side == 1)
                def _():
                    own_ref[...] = product

    def right_spec(i):
        number = rights[i].shape[1] // cols
        return pl.BlockSpec((length, cols), lambda s, n: (0, jnp.clip(n - starts[i], 0, number - 1)))

    return call(
        kernel,
        name,
        2 * length * width * total * cols,
        2 * length * width + 4 * length * total * cols + 2 * width * total * cols,
        (rows_in, *rights),
        (2, total),
        [pl.BlockSpec((length, half), lambda s, n: (0, 1 - s))] + [right_spec(i) for i in range(n)],
        [
            pl.BlockSpec((half, cols), lambda s, n: (0, jnp.where(s == 0, n, total - 1))),
            pl.BlockSpec((half, cols), lambda s, n: (0, jnp.where(s == 0, 0, n))),
        ],
        [struct((half, total * cols))] * 2,
        after=after,
    )


def split_outputs(split, rows, half, count):
    if split is None:
        return [(0, half, {m: m for m in range(count)}, lambda m, blk: (m, 0))]
    send_first = (({0: 1, 1: 0}), lambda m, blk: (jnp.where(m < 1, 1, 0), 0))
    keep_first = (({2: 1, 3: 0}), lambda m, blk: (jnp.where(m < 3, 1, 0), 0))
    send_second = (({0: 1, 2: 0}), lambda m, blk: (jnp.where(m < 2, 1, 0), 0))
    keep_second = (({1: 1, 3: 0}), lambda m, blk: (jnp.where(m < 3, 1, 0), 0))
    if split == "first":
        return [(0, half, *send_first), (0, half, *keep_first)]
    if split == "second":
        return [(0, half, *send_second), (0, half, *keep_second)]
    part = half // 2
    return [
        (0, part, *send_first),
        (0, part, *keep_first),
        (part, part, *send_second),
        (part, part, *keep_second),
    ]


def store_outputs(plan, out_refs, low):
    step = pl.program_id(0)
    for (col, cols, steps, _), ref in zip(plan, out_refs):
        if len(steps) > 2:
            ref[...] = low[:, col : col + cols]
            continue
        first, second = steps

        @pl.when((step == first) | (step == second))
        def _(ref=ref, col=col, cols=cols):
            ref[...] = low[:, col : col + cols]


def rows_back(blocks, order, split, lefts, groups, side, name, unit=None, after=()):
    length = lefts[0].shape[0]
    count, places = blocks.shape[0], order.shape[0]
    half = groups[0][0].rows // 2
    rows = length // places
    widths = [left.shape[1] for left in lefts]
    depth = sum(widths)
    n = len(lefts)
    arrays = [array for weights, _, _ in groups for array in weights.arrays]
    k = len(arrays)
    number = sum(weights.number(count, side) for weights, _, _ in groups)
    plan = split_outputs(split, rows, half, places)
    u = 0 if unit is None else 1

    def kernel(blk, places_ref, *refs):
        left_refs, unit_refs, w_refs = refs[:n], refs[n : n + u], refs[n + u : n + u + k]
        out_refs = refs[n + u + k : n + u + k + len(plan)]
        sum_refs = refs[n + u + k + len(plan) : n + 2 * u + k + len(plan)]
        joined_ref, w_ref, sems = refs[-3:]

        copies, at, col, used = [], 0, 0, 0
        for weights, start, cols in groups:
            more = len(weights.arrays)
            found = weights.copies(
                w_refs[at : at + more],
                blk,
                count,
                side,
                start,
                cols,
                w_ref.at[:, pl.ds(col, cols)],
                sems.at[pl.ds(used, weights.number(count, side))],
            )
            copies += found
            at, col, used = at + more, col + cols, used + len(found)

        @pl.when(pl.program_id(0) == 0)
        def _():
            for copy in copies:
                copy.start()

        col = 0
        for ref, cols in zip(left_refs, widths):
            joined_ref[:, col : col + cols] = ref[...]
            col += cols

        @pl.when(pl.program_id(0) == 0)
        def _():
            for copy in copies:
                copy.wait()

        low = dot(joined_ref[...], w_ref[...], NT).astype(BF)
        store_outputs(plan, out_refs, low)
        if u:

            @pl.when(pl.program_id(0) == 0)
            def _():
                sum_refs[0][...] = jnp.zeros_like(sum_refs[0])

            wide = low.astype(F32)
            sum_refs[0][0:1, :] += jnp.sum(wide * unit_refs[0][...].astype(F32), axis=0, keepdims=True)
            sum_refs[0][1:2, :] += jnp.sum(wide, axis=0, keepdims=True)

    def left_spec(cols, column=0):
        return pl.BlockSpec((rows, cols), lambda m, blk, o: (o[m], column))

    def out_spec(cols, where):
        return pl.BlockSpec((rows, cols), lambda m, blk, o: where(m, blk))

    return call(
        kernel,
        name,
        2 * length * half * depth,
        2 * length * depth + 2 * half * depth + 2 * length * half,
        (*lefts, *([unit] if u else []), *arrays),
        (places,),
        [left_spec(cols) for cols in widths]
        + [left_spec(half, side)] * u
        + [pl.BlockSpec(memory_space=pl.ANY)] * k,
        [out_spec(cols, where) for _, cols, _, where in plan]
        + [pl.BlockSpec((8, half), lambda m, blk, o: (0, 0))] * u,
        [struct((len(steps) * rows, cols)) for _, cols, steps, _ in plan] + [struct((8, half), F32)] * u,
        scratch=[
            pltpu.VMEM((rows, depth), BF),
            pltpu.VMEM((half, depth), BF),
            pltpu.SemaphoreType.DMA((number,)),
        ],
        prefetch=(blocks, order),
        after=after,
    )


def end_call(kernel, name, blocks, fulls, terms, vector, dtype, after):
    length, width = fulls[0].shape
    rows = min(128, length)
    n = len(fulls)
    counts = [len(part) for part in terms]

    def body(blk, *refs):
        at, parts = n, []
        for number in counts:
            total = refs[at][...].astype(F32)
            for ref in refs[at + 1 : at + number]:
                total = total + ref[...].astype(F32)
            parts.append(total)
            at += number
        result = kernel([ref[...].astype(F32) for ref in refs[:n]], jnp.concatenate(parts, axis=1), refs[at][...])
        out_ref = refs[at + 1]
        cols = width // blocks.shape[0]
        for p in range(blocks.shape[0]):
            place = pl.ds(pl.multiple_of(blk[p] * cols, cols), cols)
            out_ref[:, place] = result[:, p * cols : (p + 1) * cols].astype(dtype)

    full = pl.BlockSpec((rows, width), lambda m, blk: (m, 0))
    flat = [array for part in terms for array in part]
    return call(
        body,
        name,
        0,
        10 * length * width,
        (*fulls, *flat, vector),
        (length // rows,),
        [full] * n
        + [pl.BlockSpec((rows, array.shape[1]), lambda m, blk: (m, 0)) for array in flat]
        + [pl.BlockSpec((1, width), lambda m, blk: (0, 0))],
        full,
        struct((length, width), dtype),
        prefetch=(blocks,),
        after=after,
    )


def add_branch(blocks, x, terms, out_bias, after=()):
    return end_call(
        lambda fulls, branch, bias: fulls[0] + branch + bias, "add_branch", blocks, (x,), terms, out_bias, BF, after
    )


def norm_back(blocks, x, g, terms, gain, after=()):
    def kernel(fulls, grads, scale):
        x, g = fulls
        centered = x - jnp.mean(x, axis=1, keepdims=True)
        variance = jnp.mean(centered * centered, axis=1, keepdims=True)
        inv_std = lax.rsqrt(variance + EPSILON)
        unit = centered * inv_std
        scaled = grads * scale
        mean = jnp.mean(scaled, axis=1, keepdims=True)
        along = jnp.mean(scaled * unit, axis=1, keepdims=True)
        return g + inv_std * (scaled - mean - unit * along)

    return end_call(kernel, "norm_back", blocks, (x, g), terms, gain, F32, after)


def flip(value, axis, size, bit):
    return lax.ppermute(value, axis, [(i, i ^ bit) for i in range(size)])


def flip_sums(value, axis, size):
    found, bit = [value], 1
    while bit < size:
        found.append(found[-1] + flip(found[-1], axis, size, bit))
        bit *= 2
    return found


def pick(steps, k):
    return steps[min(k, len(steps) - 1)]


class Ring:
    def __init__(self, n_dp):
        self.size = n_dp
        self.chips = n_dp // 2

    def send(self, value):
        pairs = [
            (z * 2 + c, ((z + 1) % self.chips) * 2 + c) for z in range(self.chips) for c in range(2)
        ]
        return lax.ppermute(value, "dp", pairs)

    def swap(self, value):
        return flip(value, "dp", self.size, 1)

    def extend(self, pieces, steps, after):
        while len(pieces) <= min(steps, self.chips - 1):
            pieces.append(self.send(pieces[-1]))
        pieces[-1:] = tie(pieces[-1:], after)


def per_device(
    sizes, layer_input, ln_gain, ln_bias, out_bias, w_qkv, b_qkv, w_out, w_fc1, b_fc1, w_fc2, out_grad
):
    n_dp, n_tensor = sizes
    ring = Ring(n_dp)
    chips = ring.chips
    d_index, t_index = lax.axis_index("dp"), lax.axis_index("tensor")
    place, core = d_index // 2, d_index % 2
    steps = jnp.arange(chips, dtype=jnp.int32)
    behind = ((place - steps) % chips) * 2
    blocks = jnp.concatenate([behind + core, behind + (1 - core)]).astype(jnp.int32)
    square = n_tensor == 4

    local, width = layer_input.shape[1:]
    depth = w_qkv.shape[0]
    inner = w_qkv.shape[2]
    units = w_fc1.shape[1]
    heads = inner // HD
    length = local * n_tensor
    pairs = inner // 128

    third = ln_gain.shape[0]
    vectors = jnp.stack([ln_gain, ln_bias, out_bias]).astype(F32).reshape(1, 3 * third)
    table = jnp.where(jnp.arange(n_tensor)[:, None] == t_index, vectors, 0.0)
    tables_small = flip_sums(table, "tensor", n_tensor)
    packed = jnp.concatenate(
        [tables_small[-1].reshape(-1), b_qkv.astype(F32).reshape(-1), b_fc1.astype(F32).reshape(-1)]
    )[None, :]
    packed = jnp.where(jnp.arange(n_dp)[:, None] == d_index, packed, 0.0)
    packed_steps = flip_sums(packed, "dp", n_dp)
    packed = packed_steps[-1]
    cut = n_tensor * 3 * third
    vectors = packed[:, :cut].reshape(n_dp, n_tensor, 3, third)
    vectors = jnp.transpose(vectors, (2, 0, 1, 3)).reshape(3, n_dp, n_tensor * third)
    chosen = (blocks[:, None] == jnp.arange(n_dp)[None, :]).astype(F32)
    vectors = jnp.einsum("pd,kdj->kpj", chosen, vectors, precision=lax.Precision.HIGHEST)
    gain, shift, bias_out = (vectors[i].reshape(1, width) for i in range(3))
    tail = cut + b_qkv.size
    bias_qkv = jnp.transpose(packed[:, cut:tail].reshape(n_dp, 3, heads, -1), (1, 2, 0, 3))
    bias_qkv = bias_qkv.reshape(1, 3 * inner)
    bias_fc1 = jnp.transpose(packed[:, tail:].reshape(n_dp, units // HD, -1), (1, 0, 2))
    bias_fc1 = bias_fc1.reshape(1, units)
    tables = rotary_rows(length)

    x, _ = order_columns(blocks, layer_input[0])
    shard = heads_shard(w_qkv.reshape(depth, 3 * inner), w_out, [x])
    rows = min(256, local)
    heads_own, heads_sib = [shard], []
    if square:
        cut = local // 2
        lower = x[cut:]
        beside, below = [flip(x[:cut], "tensor", 4, 1)], [flip(x[:cut], "tensor", 4, 2)]
        heads_own.append(ring.send(shard))
        heads_sib.append(ring.swap(shard))
        lower, heads_own[1], beside[0], below[0] = tie(
            [lower, heads_own[1], beside[0], below[0]], [tables_small[-1], heads_sib[0]]
        )
        beside.append(flip(lower, "tensor", 4, 1))
        below.append(flip(lower, "tensor", 4, 2))
        heads_own.append(ring.send(heads_own[1]))
        heads_sib.append(ring.swap(heads_own[1]))
        heads_own[2], beside[1], below[1] = tie(
            [heads_own[2], beside[1], below[1]], [pick(packed_steps, 2), heads_sib[1], tables[0]]
        )
        across = [flip(beside[0], "tensor", 4, 2), flip(below[1], "tensor", 4, 1)]
        for _ in range(chips - 3):
            heads_own.append(ring.send(heads_own[-1]))
            heads_sib.append(ring.swap(heads_own[-2]))
        heads_own[-1], *across = tie([heads_own[-1], *across], [gain, heads_sib[-1]])
        heads_sib.append(ring.swap(heads_own[-1]))
        pieces = [x, *beside, *below, *across]
        rows = min(rows, cut)
        each = local // rows
        relative = [r * each + i for r in (0, 1, 2, 3) for i in range(each)]
        relative = jnp.array(relative, jnp.int32)
        out_blocks = ((relative // each) ^ t_index) * each + relative % each
        g, bias_part = order_columns(blocks, out_grad[0], after=across)
        order = (jnp.array([3, 1, 2, 0], jnp.int32) ^ t_index).astype(jnp.int32)
    else:
        for _ in range(chips - 1):
            heads_own.append(ring.send(heads_own[-1]))
        heads_sib = [ring.swap(piece) for piece in heads_own]
        pieces = [lax.all_gather(x, "tensor", axis=0, tiled=True)]
        out_blocks = jnp.arange(length // rows, dtype=jnp.int32)
        g, bias_part = order_columns(blocks, out_grad[0])
        order = jnp.arange(n_tensor, dtype=jnp.int32)
    heads_weights = Weights(heads_own + heads_sib)
    g_all = lax.all_gather(g, "tensor", axis=0, tiled=True)

    def split(kind):
        return kind if square else None

    bits = {"first": [1], "second": [2], "both": [1, 2]}

    def cross_once(kind, parts):
        if not square:
            return [lax.psum_scatter(parts[0], "tensor", scatter_dimension=0, tiled=True)]
        return [flip(parts[2 * i], "tensor", 4, bit) for i, bit in enumerate(bits[kind])]

    def cross_add(parts, got):
        if not square:
            return []
        kept = parts[1::2]
        return [(k[local:].astype(F32) + r[local:].astype(F32)).astype(BF) for k, r in zip(kept, got)]

    def cross_twice(kind, sums):
        return [flip(value, "tensor", 4, 3 - bit) for value, bit in zip(sums, bits[kind])] if square else []

    def cross_terms(parts, got, last):
        if not square:
            return [got]
        return [list(terms) for terms in zip(parts[1::2], got, last)]

    fc1_pieces = [stage(w_fc1, False, [heads_own[-1]])]
    normed, unit, qkv = norm_project(
        blocks, out_blocks, pieces, rows, gain, shift, bias_qkv, tables, heads_weights, after=[fc1_pieces[0]]
    )
    ring.extend(fc1_pieces, 1, [qkv])
    first = pairs // 2
    context, log_first = attend(qkv, 0, first, after=[fc1_pieces[-1]])
    ring.extend(fc1_pieces, 2, [log_first])
    context, log_second = attend(qkv, first, pairs - first, before=context, after=[fc1_pieces[-1]])
    log_total = jnp.concatenate([log_first, log_second], axis=0)
    ring.extend(fc1_pieces, chips - 1, [log_second])
    fc1_own = jnp.concatenate(fc1_pieces, axis=0)
    fc1_weights = Weights([fc1_own, ring.swap(fc1_own)])
    fc2_shard = stage(w_fc2, True, [fc1_own])
    fc2_weights = Weights([lax.all_gather(fc2_shard, "dp", axis=0, tiled=True)], placed=True)
    context_grad = context_back(blocks, g_all, heads_weights, after=[fc2_shard, log_second])
    act, slope = expand(blocks, normed, fc1_weights, bias_fc1, after=[context_grad])

    def scatter(parts):
        return lax.psum_scatter(parts, "dp", scatter_dimension=0, tiled=True)

    fc2_sums = scatter(weight_grad(blocks, g_all, [act, context], min(512, inner), "fc2_grad"))
    backs = attend_back(qkv, context, context_grad, log_total, tables, after=[act])
    heads_cols, fc2_cols = (heads_weights, 0, 3 * inner), (fc2_weights, 0, units)
    out_cols, fc1_cols = (heads_weights, 3 * inner, inner), (fc1_weights, 0, units)
    branch = []
    for side, kind in enumerate(("first", "second")):
        parts = rows_back(
            blocks, order, split(kind), [act, context], [fc2_cols, out_cols], side, "branch_half",
            after=[backs[0]] if side == 0 else branch[0],
        )
        branch.append(parts)
    branch_got = [cross_once("first", branch[0]), cross_once("second", branch[1])]
    hidden_grad, b_fc1_part = hidden_back(blocks, g_all, fc2_weights, slope, after=branch[1])
    fc1_grad = weight_grad(blocks, normed, [hidden_grad], min(512, units), "fc1_grad")
    fc1_grad, branch_got[0][0], branch_got[1][0] = tie([fc1_grad, branch_got[0][0], branch_got[1][0]], [])
    fc1_sums = scatter(fc1_grad)
    branch_sums = [cross_add(parts, got) for parts, got in zip(branch, branch_got)]
    branch_last = [cross_twice(kind, sums) for kind, sums in zip(("first", "second"), branch_sums)]
    heads_grads = weight_grad_halves(
        normed, backs[:3], inner, "heads_grad", after=[fc1_grad, *branch_sums[0], *branch_sums[1]]
    )
    if square:
        heads_sib_grad, heads_own_grad, branch_last[0][0], branch_last[1][0] = tie(
            [*heads_grads, branch_last[0][0], branch_last[1][0]], []
        )
    else:
        heads_sib_grad, heads_own_grad = heads_grads
    branch_terms = [
        part for parts in zip(branch, branch_got, branch_last) for part in cross_terms(*parts)
    ]
    heads_other = ring.swap(heads_sib_grad)
    lefts = [*backs[:3], hidden_grad]
    back_own = rows_back(
        blocks, order, split("both"), lefts, [heads_cols, fc1_cols], 0, "normed_back_half", unit=unit,
        after=[heads_own_grad],
    )
    *back_own, heads_other = tie([*back_own, heads_other], [])

    def ring_add(k, moving):
        cut = slice(k * depth, (k + 1) * depth)
        total = heads_own_grad[cut].astype(F32) + heads_other[cut].astype(F32)
        return total if moving is None else total + moving.astype(F32)

    own_got = cross_once("both", back_own[:-1])
    message = ring_add(1, None).astype(BF)
    moving = ring.send(message)
    back_sib = rows_back(
        blocks, order, split("both"), lefts, [heads_cols, fc1_cols], 1, "normed_back_half", unit=unit,
        after=[message],
    )
    n = len(back_sib)
    *joined, moving = tie([*back_sib, *own_got, moving], [])
    back_sib, own_got = joined[:n], joined[n:]
    sib_got = cross_once("both", back_sib[:-1])
    own_sums = cross_add(back_own[:-1], own_got)
    own_last = cross_twice("both", own_sums)
    message = ring_add(2, moving).astype(BF) if chips > 2 else None
    for k in range(2, chips):
        moving = ring.send(message if k == 2 else ring_add(k, moving).astype(BF))
    layer_output = add_branch(blocks, x, branch_terms, bias_out, after=[back_sib[0], *own_sums])
    layer_output, *sib_got = tie([layer_output, *sib_got], [])
    sib_last = cross_twice("both", cross_add(back_sib[:-1], sib_got))
    heads_sums = ring_add(0, moving)
    back_terms = cross_terms(back_own[:-1], own_got, own_last) + cross_terms(back_sib[:-1], sib_got, sib_last)
    input_grad = norm_back(blocks, x, g, back_terms, gain)

    w_qkv_grad = heads_sums.reshape(depth, 3, inner)
    w_out_grad = fc2_sums[:, units:].T.astype(F32)
    w_fc1_grad = fc1_sums.astype(F32)
    w_fc2_grad = fc2_sums[:, :units].T.astype(F32)

    norm_sums = jnp.concatenate([back_own[-1][:2], back_sib[-1][:2]], axis=1).reshape(2, n_dp, depth)
    norm_sums = jnp.einsum("pd,kpj->kdj", chosen, norm_sums, precision=lax.Precision.HIGHEST)
    vector_sums = jnp.concatenate([norm_sums.reshape(2, width), bias_part[:1]], axis=0)
    vector_sums = flip_sums(vector_sums, "tensor", n_tensor)[-1]
    unit_sums = jnp.concatenate(
        [
            vector_sums.reshape(-1),
            jnp.transpose(backs[3][:, :3, :], (1, 0, 2)).reshape(-1),
            b_fc1_part[0],
        ]
    )
    unit_sums = flip_sums(unit_sums, "dp", n_dp)[-1]
    mine = unit_sums[: 3 * width].reshape(3, n_dp * n_tensor, third)
    mine = lax.dynamic_index_in_dim(mine, d_index * n_tensor + t_index, 1, keepdims=False)
    b_width = HD // n_dp
    b_qkv_grad = lax.dynamic_slice_in_dim(
        unit_sums[3 * width : 3 * width + 3 * inner].reshape(3, heads, HD), d_index * b_width, b_width, 2
    )
    b_fc1_grad = lax.dynamic_slice_in_dim(
        unit_sums[3 * width + 3 * inner :].reshape(units // HD, HD), d_index * b_width, b_width, 1
    )
    return (
        layer_output[None],
        input_grad[None],
        mine[0],
        mine[1],
        mine[2],
        w_qkv_grad,
        b_qkv_grad,
        w_out_grad,
        w_fc1_grad,
        b_fc1_grad,
        w_fc2_grad,
    )


def solution(mesh):
    in_specs = (
        P("dp", "tensor", None),
        P(("dp", "tensor")),
        P(("dp", "tensor")),
        P(("dp", "tensor")),
        P("dp", None, "tensor"),
        P(None, "tensor", "dp"),
        P("tensor", "dp"),
        P("dp", "tensor"),
        P("tensor", "dp"),
        P("tensor", "dp"),
        P("dp", "tensor", None),
    )
    out_specs = (
        P("dp", "tensor", None),
        P("dp", "tensor", None),
        P(("dp", "tensor")),
        P(("dp", "tensor")),
        P(("dp", "tensor")),
        P("dp", None, "tensor"),
        P(None, "tensor", "dp"),
        P("tensor", "dp"),
        P("dp", "tensor"),
        P("tensor", "dp"),
        P("tensor", "dp"),
    )
    sizes = (mesh.shape["dp"], mesh.shape["tensor"])
    return jax.shard_map(
        functools.partial(per_device, sizes),
        mesh=mesh,
        in_specs=in_specs,
        out_specs=out_specs,
        check_vma=False,
    )
```

```python
import functools
import math

import jax
import jax.numpy as jnp
from jax import lax
from jax.experimental import pallas as pl
from jax.experimental.pallas import tpu as pltpu
from jax.sharding import PartitionSpec as P

HD = 64
ROT = 32
EPSILON = 1e-05
NEG = -1e30
LOG2E = math.log2(math.e)
BF = jnp.bfloat16
F32 = jnp.float32
VMEM_BYTES = 56 << 20

NN = (((1,), (0,)), ((), ()))
NT = (((1,), (1,)), ((), ()))
TN = (((0,), (0,)), ((), ()))


def dot(a, b, dims):
    return lax.dot_general(a, b, dims, preferred_element_type=F32)


def eight_rows(value):
    rows, cols = value.shape
    return jnp.sum(value.reshape(rows // 8, 8, cols), axis=0)


def call(kernel, name, flops, moved, operands, grid, in_specs, out_specs, out_shape, scratch=(), prefetch=(), aliases=None, after=()):
    front = len(prefetch) + len(in_specs)

    def body(*refs):
        kernel(*refs[:front], *refs[front + len(after) :])

    return pl.pallas_call(
        body,
        name=name,
        grid_spec=pltpu.PrefetchScalarGridSpec(
            num_scalar_prefetch=len(prefetch),
            grid=grid,
            in_specs=list(in_specs) + [pl.BlockSpec(memory_space=pl.ANY)] * len(after),
            out_specs=out_specs,
            scratch_shapes=list(scratch),
        ),
        out_shape=out_shape,
        input_output_aliases=aliases or {},
        compiler_params=pltpu.CompilerParams(vmem_limit_bytes=VMEM_BYTES),
        cost_estimate=pl.CostEstimate(flops=int(flops), bytes_accessed=int(moved), transcendentals=0),
    )(*prefetch, *operands, *after)


class Weights:
    def __init__(self, arrays, size=None, placed=False):
        self.arrays = list(arrays)
        self.placed = placed
        self.cols = self.arrays[0].shape[1]
        self.size = size or self.arrays[0].shape[0]
        self.rows = self.arrays[0].shape[0] if placed else self.size * len(self.arrays)

    def copies(self, refs, blk, count, side, col, cols, target, sems):
        found = []

        def add(source, start, size, place):
            found.append(
                pltpu.make_async_copy(
                    source.at[pl.ds(start, size), pl.ds(col, cols)],
                    target.at[pl.ds(place, size), :],
                    sems.at[len(found)],
                )
            )

        half = self.rows // 2
        if self.placed:
            size = self.rows // count
            first, last = (0, count) if side is None else (side * count // 2, (side + 1) * count // 2)
            for p in range(first, last):
                add(refs[0], pl.multiple_of(blk[p] * size, size), size, (p - first) * size)
            return found
        place = 0
        for ref in refs:
            size = self.size
            if side is None or place // half == side:
                add(ref, 0, size, place - (side or 0) * half)
            place += size
        return found

    def number(self, count, side=None):
        total = count if self.placed else len(self.arrays)
        return total if side is None else total // 2


def struct(shape, dtype=BF):
    return jax.ShapeDtypeStruct(shape, dtype)


def tie(values, after):
    n = len(values)
    anywhere = pl.BlockSpec(memory_space=pl.ANY)

    def kernel(*refs):
        del refs

    return pl.pallas_call(
        kernel,
        name="tie",
        in_specs=[anywhere] * (n + len(after)),
        out_specs=[anywhere] * n,
        out_shape=[struct(v.shape, v.dtype) for v in values],
        input_output_aliases={i: i for i in range(n)},
    )(*values, *after)


def order_columns(blocks, x, after=()):
    rows, width = x.shape
    count = blocks.shape[0]
    cols = width // count
    step_rows = min(256, rows)

    def kernel(blk, x_ref, out_ref, sum_ref):
        for p in range(count):
            place = pl.ds(pl.multiple_of(blk[p] * cols, cols), cols)
            out_ref[:, p * cols : (p + 1) * cols] = x_ref[:, place]

        @pl.when(pl.program_id(0) == 0)
        def _():
            sum_ref[...] = jnp.zeros_like(sum_ref)

        sum_ref[0:1, :] += jnp.sum(x_ref[...].astype(F32), axis=0, keepdims=True)

    block = pl.BlockSpec((step_rows, width), lambda m, blk: (m, 0))
    return call(
        kernel,
        "order_columns",
        0,
        4 * rows * width,
        (x,),
        (rows // step_rows,),
        [block],
        [block, pl.BlockSpec((8, width), lambda m, blk: (0, 0))],
        [struct(x.shape), struct((8, width), F32)],
        prefetch=(blocks,),
        after=after,
    )


def heads_shard(w_qkv, w_out):
    depth, wide = w_qkv.shape
    inner = w_out.shape[0]

    def kernel(q_ref, o_ref, out_ref):
        out_ref[:, :wide] = q_ref[...]
        out_ref[:, wide:] = o_ref[...].T

    return call(
        kernel,
        "heads_shard",
        0,
        4 * depth * (wide + inner),
        (w_qkv, w_out),
        (1,),
        [pl.BlockSpec(w.shape, lambda i: (0, 0)) for w in (w_qkv, w_out)],
        pl.BlockSpec((depth, wide + inner), lambda i: (0, 0)),
        struct((depth, wide + inner)),
    )


def stage(weight, flip, after, rows=None):
    start, count = rows or (0, weight.shape[0])
    taken = (count, weight.shape[1])
    shape = taken[::-1] if flip else taken

    def kernel(w_ref, out_ref):
        out_ref[...] = w_ref[...].T if flip else w_ref[...]

    return call(
        kernel,
        "stage_weight",
        0,
        4 * taken[0] * taken[1],
        (weight,),
        (1,),
        [pl.BlockSpec(taken, lambda i: (start // count, 0))],
        pl.BlockSpec(shape, lambda i: (0, 0)),
        struct(shape),
        after=after,
    )


def rotary_rows(length):
    lane = jnp.arange(128, dtype=jnp.int32)[None, :] % HD
    half = ROT // 2
    frequency = 10000.0 ** (-2.0 * (lane % half).astype(F32) / ROT)
    angles = jnp.arange(length, dtype=F32)[:, None] * frequency
    cosine, sine = jnp.cos(angles), jnp.sin(angles)
    keep = jnp.where(lane < ROT, cosine, 1.0)
    ahead = jnp.where(lane < half, -sine, 0.0)
    behind = jnp.where((lane >= half) & (lane < ROT), sine, 0.0)
    return keep, ahead, behind


def turn(u, keep, ahead, behind):
    return u * keep + pltpu.roll(u, 128 - ROT // 2, 1) * ahead + pltpu.roll(u, ROT // 2, 1) * behind


def ordered(ref, blk, count, cols):
    return jnp.concatenate(
        [ref[:, pl.ds(pl.multiple_of(blk[p] * cols, cols), cols)] for p in range(count)], axis=1
    )


def norm_project(blocks, x_all, gain, shift, bias, tables, weights, after=()):
    length, width = x_all.shape
    wide = bias.shape[1]
    inner = wide // 3
    rows = min(256, length)
    k, count = len(weights.arrays), blocks.shape[0]

    def kernel(blk, x_ref, gain_ref, shift_ref, bias_ref, keep_ref, ahead_ref, behind_ref, *refs):
        w_refs = refs[:k]
        normed_ref, unit_ref, qkv_ref, w_ref, sems = refs[k:]
        step = pl.program_id(0)
        copies = weights.copies(w_refs, blk, count, None, 0, wide, w_ref, sems)

        @pl.when(step == 0)
        def _():
            for copy in copies:
                copy.start()

        x = ordered(x_ref, blk, count, width // count).astype(F32)
        centered = x - jnp.mean(x, axis=1, keepdims=True)
        variance = jnp.mean(centered * centered, axis=1, keepdims=True)
        unit = centered * lax.rsqrt(variance + EPSILON)
        unit_ref[...] = unit.astype(BF)
        normed_ref[...] = (unit * gain_ref[...] + shift_ref[...]).astype(BF)

        @pl.when(step == 0)
        def _():
            for copy in copies:
                copy.wait()

        for part in range(3):
            cols = slice(part * inner, (part + 1) * inner)
            merged = dot(normed_ref[...], w_ref[:, cols], NN) + bias_ref[:, cols]
            for pair in range(inner // 128):
                u = merged[:, pair * 128 : (pair + 1) * 128]
                if part < 2:
                    u = turn(u, keep_ref[...], ahead_ref[...], behind_ref[...])
                start = part * inner + pair * 128
                qkv_ref[:, start : start + 128] = u.astype(BF)

    def whole(shape):
        return pl.BlockSpec(shape, lambda j, blk: (0, 0))

    def block(cols):
        return pl.BlockSpec((rows, cols), lambda j, blk: (j, 0))

    return call(
        kernel,
        "norm_project",
        3 * length * width * wide,
        6 * length * width + 4 * width * wide,
        (x_all, gain, shift, bias, *tables, *weights.arrays),
        (length // rows,),
        [block(width), whole((1, width)), whole((1, width)), whole((1, wide))]
        + [block(128)] * 3
        + [pl.BlockSpec(memory_space=pl.ANY)] * k,
        [block(width), block(width), block(wide)],
        [struct((length, width)), struct((length, width)), struct((length, wide))],
        scratch=[pltpu.VMEM((width, wide), BF), pltpu.SemaphoreType.DMA((weights.number(count),))],
        prefetch=(blocks,),
        after=after,
    )


def attend(qkv, first, number, before=None, after=()):
    length = qkv.shape[0]
    inner = qkv.shape[1] // 3
    pairs = inner // 128
    block = min(512, length)
    count = length // block
    scale = LOG2E / math.sqrt(HD)
    n = 0 if before is None else 1

    def kernel(q_ref, k_ref, v_ref, *refs):
        o_ref, lse_ref, turned_ref = refs[n:]
        lane = lax.broadcasted_iota(jnp.int32, (1, 128), 1)

        @pl.when(pl.program_id(1) == 0)
        def _():
            turned_ref[...] = v_ref[...].T

        for index in range(count):

            @pl.when(pl.program_id(1) == index)
            def _(index=index):
                queries = q_ref[...]
                blank = jnp.zeros_like(queries)
                end = (index + 1) * block
                found = []
                for head in range(2):
                    mine = (lane < HD) if head == 0 else (lane >= HD)
                    scores = dot(k_ref[:end, :], jnp.where(mine, queries, blank), NT)
                    row = lax.broadcasted_iota(jnp.int32, (block, block), 0)
                    col = lax.broadcasted_iota(jnp.int32, (block, block), 1)
                    last = jnp.where(row <= col, scores[end - block :], NEG)
                    if index:
                        scores = jnp.concatenate([scores[: end - block], last], axis=0)
                    else:
                        scores = last
                    top = jnp.max(scores, axis=0, keepdims=True)
                    weights = jnp.exp2((scores - top) * scale)
                    total = jnp.sum(weights, axis=0, keepdims=True)
                    out = dot(turned_ref[head * HD : (head + 1) * HD, :end], weights.astype(BF), NN)
                    found.append(out / total)
                    lse_ref[0, head : head + 1, :] = top * scale + jnp.log2(total)
                o_ref[...] = jnp.concatenate(found, axis=0).T.astype(BF)

    return call(
        kernel,
        "attend",
        40 * length * length * 128 * number,
        8 * length * 128 * number,
        (qkv, qkv, qkv) + ((before,) if n else ()),
        (number, count),
        [
            pl.BlockSpec((block, 128), lambda h, i: (i, first + h)),
            pl.BlockSpec((length, 128), lambda h, i: (0, pairs + first + h)),
            pl.BlockSpec((length, 128), lambda h, i: (0, 2 * pairs + first + h)),
        ]
        + [pl.BlockSpec(memory_space=pl.ANY)] * n,
        [
            pl.BlockSpec((block, 128), lambda h, i: (i, first + h)),
            pl.BlockSpec((1, 2, block), lambda h, i: (h, 0, i)),
        ],
        [struct((length, inner)), struct((number, 2, length), F32)],
        scratch=[pltpu.VMEM((128, length), BF)],
        aliases={3: 0} if n else {},
        after=after,
    )


def attend_back(qkv, context, context_grad, log_total, tables, after=()):
    length = qkv.shape[0]
    inner = qkv.shape[1] // 3
    pairs = inner // 128
    block = min(512, length)
    count = length // block
    scale = LOG2E / math.sqrt(HD)
    shrink = 1.0 / math.sqrt(HD)

    def kernel(q_ref, k_ref, v_ref, o_ref, do_ref, lse_ref, keep_ref, ahead_ref, behind_ref, *rest):
        dq_ref, dk_ref, dv_ref, sum_ref, k_total, v_total = rest
        step = pl.program_id(1)
        lane = lax.broadcasted_iota(jnp.int32, (1, 128), 1)

        @pl.when(step == 0)
        def _():
            k_total[...] = jnp.zeros_like(k_total)
            v_total[...] = jnp.zeros_like(v_total)
            sum_ref[...] = jnp.zeros_like(sum_ref)

        def turn_back(u, rows):
            return turn(u, keep_ref[rows, :], -ahead_ref[rows, :], -behind_ref[rows, :])

        for index in range(count):

            @pl.when(step == index)
            def _(index=index):
                queries, grads = q_ref[...], do_ref[...]
                blank = jnp.zeros_like(queries)
                queries_turned, grads_turned = queries.T, grads.T
                products = grads.astype(F32) * o_ref[...].astype(F32)
                log_totals = lse_ref[0].T
                q_total = [None, None]
                for other in range(index + 1):
                    rows = slice(other * block, (other + 1) * block)
                    keys, values = k_ref[rows, :], v_ref[rows, :]
                    for head in range(2):
                        mine = (lane < HD) if head == 0 else (lane >= HD)
                        here = slice(head * HD, (head + 1) * HD)
                        delta = jnp.sum(products[:, here], axis=1, keepdims=True)
                        scores = dot(jnp.where(mine, queries, blank), keys, NT)
                        if other == index:
                            row = lax.broadcasted_iota(jnp.int32, (block, block), 0)
                            col = lax.broadcasted_iota(jnp.int32, (block, block), 1)
                            scores = jnp.where(col <= row, scores, NEG)
                        probs = jnp.exp2(scores * scale - log_totals[:, head : head + 1])
                        probs_grad = dot(jnp.where(mine, grads, blank), values, NT)
                        score_grad = (probs * (probs_grad - delta)).astype(BF)
                        v_total[here, rows] += dot(grads_turned[here, :], probs.astype(BF), NN)
                        k_total[here, rows] += dot(queries_turned[here, :], score_grad, NN)
                        term = dot(score_grad, keys, NN)
                        q_total[head] = term if other == 0 else q_total[head] + term
                dq = jnp.where(lane < HD, q_total[0], q_total[1]) * shrink
                rows = slice(index * block, (index + 1) * block)
                dq = turn_back(dq, rows).astype(BF)
                dq_ref[...] = dq
                sum_ref[0, 0:8, :] += eight_rows(dq.astype(F32))

        @pl.when(step == count - 1)
        def _():
            for index in range(count):
                rows = slice(index * block, (index + 1) * block)
                dk = turn_back(k_total[:, rows].T * shrink, rows).astype(BF)
                dk_ref[rows, :] = dk
                sum_ref[0, 8:16, :] += eight_rows(dk.astype(F32))
                dv = v_total[:, rows].T.astype(BF)
                dv_ref[rows, :] = dv
                sum_ref[0, 16:24, :] += eight_rows(dv.astype(F32))

    def column(offset):
        return pl.BlockSpec((length, 128), lambda h, i: (0, offset + h))

    def rows_of(offset):
        return pl.BlockSpec((block, 128), lambda h, i: (i, offset + h))

    table = pl.BlockSpec((length, 128), lambda h, i: (0, 0))
    return call(
        kernel,
        "attend_back",
        60 * length * length * inner,
        16 * length * inner,
        (qkv, qkv, qkv, context, context_grad, log_total, *tables),
        (pairs, count),
        [
            rows_of(0),
            column(pairs),
            column(2 * pairs),
            rows_of(0),
            rows_of(0),
            pl.BlockSpec((1, 2, block), lambda h, i: (h, 0, i)),
            table,
            table,
            table,
        ],
        [rows_of(0), column(0), column(0), pl.BlockSpec((1, 24, 128), lambda h, i: (h, 0, 0))],
        [struct((length, inner))] * 3 + [struct((pairs, 24, 128), F32)],
        scratch=[pltpu.VMEM((128, length), F32)] * 2,
        after=after,
    )


def times_weights(blocks, rows_in, weights, name, extra, outs, finish, after=()):
    length, width = rows_in.shape
    total_cols = weights.cols
    rows, cols = min(512, length), min(1024, total_cols)
    chunks = total_cols // cols
    k, count, e = len(weights.arrays), blocks.shape[0], len(extra)
    number = weights.number(count)

    def kernel(blk, a_ref, *refs):
        w_refs, extra_refs, out_refs = refs[:k], refs[k : k + e], refs[k + e : -2]
        w_ref, sems = refs[-2:]
        chunk, step = pl.program_id(0), pl.program_id(1)
        copies = [
            weights.copies(w_refs, blk, count, None, c * cols, cols, w_ref.at[c], sems.at[c])
            for c in range(chunks)
        ]

        @pl.when((chunk == 0) & (step == 0))
        def _():
            for per_chunk in copies:
                for copy in per_chunk:
                    copy.start()

        for c in range(chunks):

            @pl.when((chunk == c) & (step == 0))
            def _(c=c):
                for copy in copies[c]:
                    copy.wait()

        finish(dot(a_ref[...], w_ref[chunk], NN), step == 0, extra_refs, out_refs)

    specs = {
        "block": pl.BlockSpec((rows, cols), lambda n, m, blk: (m, n)),
        "row": pl.BlockSpec((1, cols), lambda n, m, blk: (0, n)),
        "sum": pl.BlockSpec((8, cols), lambda n, m, blk: (0, n)),
    }
    shapes = {"block": struct((length, total_cols)), "sum": struct((8, total_cols), F32)}
    return call(
        kernel,
        name,
        2 * length * width * total_cols,
        2 * length * width + 2 * width * total_cols + 4 * length * total_cols,
        (rows_in, *weights.arrays, *(value for _, value in extra)),
        (chunks, length // rows),
        [pl.BlockSpec((rows, width), lambda n, m, blk: (m, 0))]
        + [pl.BlockSpec(memory_space=pl.ANY)] * k
        + [specs[kind] for kind, _ in extra],
        [specs[kind] for kind in outs],
        [shapes[kind] for kind in outs],
        scratch=[
            pltpu.VMEM((chunks, width, cols), BF),
            pltpu.SemaphoreType.DMA((chunks, number)),
        ],
        prefetch=(blocks,),
        after=after,
    )


def expand(blocks, normed, weights, bias, after=()):
    def finish(product, first, extra_refs, out_refs):
        hidden = product + extra_refs[0][...]
        c = math.sqrt(2.0 / math.pi)
        square = hidden * hidden
        inner = hidden * (c + (c * 0.044715) * square)
        gate = 0.5 + 0.5 * jnp.tanh(inner)
        act = hidden * gate
        out_refs[0][...] = act.astype(BF)
        out_refs[1][...] = (
            gate + act * (1.0 - gate) * (2.0 * c + (6.0 * c * 0.044715) * square)
        ).astype(BF)

    return times_weights(
        blocks, normed, weights, "expand", [("row", bias)], ["block", "block"], finish, after
    )


def hidden_back(blocks, g_all, weights, slope, after=()):
    def finish(product, first, extra_refs, out_refs):
        grad = product * extra_refs[0][...].astype(F32)
        out_refs[0][...] = grad.astype(BF)

        @pl.when(first)
        def _():
            out_refs[1][...] = jnp.zeros_like(out_refs[1])

        out_refs[1][...] += eight_rows(grad)

    return times_weights(
        blocks, g_all, weights, "hidden_back", [("block", slope)], ["block", "sum"], finish, after
    )


def columns_of(rights, cols):
    starts, total = [], 0
    for right in rights:
        starts.append(total)
        total += right.shape[1] // cols
    return starts + [total]


def weight_grad(blocks, rows_in, rights, cols, name, weights=None, after=()):
    length, width = rows_in.shape
    half = width // 2
    count = blocks.shape[0]
    depth = width // count
    starts = columns_of(rights, cols)
    n, total = len(rights), starts[-1]
    k = len(weights.arrays) if weights else 0
    more = 1 if k else 0

    def kernel(blk, a_ref, *refs):
        w_refs, out_ref = refs[n : n + k], refs[n + k]
        chunk, side = pl.program_id(0), pl.program_id(1)
        if more:
            back_ref, w_ref, sum_ref, sems = refs[n + k + 1 :]
            inner = w_ref.shape[1]
            copies = weights.copies(w_refs, blk, count, None, 3 * inner, inner, w_ref, sems)

            @pl.when((chunk == 0) & (side == 0))
            def _():
                for copy in copies:
                    copy.start()

            @pl.when((chunk == total) & (side == 0))
            def _():
                for copy in copies:
                    copy.wait()
                sum_ref[...] = dot(a_ref[...], w_ref[:half, :], NN)

            @pl.when((chunk == total) & (side == 1))
            def _():
                back_ref[...] = (sum_ref[...] + dot(a_ref[...], w_ref[half:, :], NN)).astype(BF)

        for i in range(n):

            @pl.when((chunk >= starts[i]) & (chunk < starts[i + 1]))
            def _(i=i):
                product = dot(a_ref[...], refs[i][...], TN).astype(BF)
                for p in range(count // 2):
                    place = pl.multiple_of(blk[side * (count // 2) + p] * depth, depth)
                    out_ref[pl.ds(place, depth), :] = product[p * depth : (p + 1) * depth]

    def right_spec(i):
        number = starts[i + 1] - starts[i]
        return pl.BlockSpec(
            (length, cols), lambda n, s, blk: (0, jnp.clip(n - starts[i], 0, number - 1))
        )

    out_specs = [pl.BlockSpec((width, cols), lambda n, s, blk: (0, jnp.minimum(n, total - 1)))]
    out_shape = [struct((width, total * cols))]
    scratch = []
    if more:
        inner = weights.cols // 4
        out_specs.append(pl.BlockSpec((length, inner), lambda n, s, blk: (0, 0)))
        out_shape.append(struct((length, inner)))
        scratch = [
            pltpu.VMEM((width, inner), BF),
            pltpu.VMEM((length, inner), F32),
            pltpu.SemaphoreType.DMA((weights.number(count),)),
        ]
    return call(
        kernel,
        name,
        2 * length * width * total * cols,
        2 * length * width + 4 * length * total * cols + 2 * width * total * cols,
        (rows_in, *rights, *(weights.arrays if more else ())),
        (total + more, 2),
        [pl.BlockSpec((length, half), lambda n, s, blk: (0, s))]
        + [right_spec(i) for i in range(n)]
        + [pl.BlockSpec(memory_space=pl.ANY)] * k,
        out_specs,
        out_shape,
        scratch=scratch,
        prefetch=(blocks,),
        after=after,
    )


def weight_grad_halves(rows_in, rights, cols, name, after=()):
    length, width = rows_in.shape
    half = width // 2
    starts = columns_of(rights, cols)
    n, total = len(rights), starts[-1]

    def kernel(a_ref, *refs):
        sib_ref, own_ref = refs[n:]
        side, chunk = pl.program_id(0), pl.program_id(1)
        for i in range(n):

            @pl.when((chunk >= starts[i]) & (chunk < starts[i + 1]))
            def _(i=i):
                product = dot(a_ref[...], refs[i][...], TN).astype(BF)

                @pl.when(side == 0)
                def _():
                    sib_ref[...] = product

                @pl.when(side == 1)
                def _():
                    own_ref[...] = product

    def right_spec(i):
        number = starts[i + 1] - starts[i]
        return pl.BlockSpec((length, cols), lambda s, n: (0, jnp.clip(n - starts[i], 0, number - 1)))

    return call(
        kernel,
        name,
        2 * length * width * total * cols,
        2 * length * width + 4 * length * total * cols + 2 * width * total * cols,
        (rows_in, *rights),
        (2, total),
        [pl.BlockSpec((length, half), lambda s, n: (0, 1 - s))] + [right_spec(i) for i in range(n)],
        [
            pl.BlockSpec((half, cols), lambda s, n: (0, jnp.where(s == 0, n, total - 1))),
            pl.BlockSpec((half, cols), lambda s, n: (0, jnp.where(s == 0, 0, n))),
        ],
        [struct((half, total * cols))] * 2,
        after=after,
    )


def split_outputs(split, rows, half, count):
    if split is None:
        return [(0, half, {m: m for m in range(count)}, lambda m, blk: (m, 0))]
    send_first = (({0: 1, 1: 0}), lambda m, blk: (jnp.where(m < 1, 1, 0), 0))
    keep_first = (({2: 1, 3: 0}), lambda m, blk: (jnp.where(m < 3, 1, 0), 0))
    send_second = (({0: 1, 2: 0}), lambda m, blk: (jnp.where(m < 2, 1, 0), 0))
    keep_second = (({1: 1, 3: 0}), lambda m, blk: (jnp.where(m < 3, 1, 0), 0))
    if split == "first":
        return [(0, half, *send_first), (0, half, *keep_first)]
    if split == "second":
        return [(0, half, *send_second), (0, half, *keep_second)]
    part = half // 2
    return [
        (0, part, *send_first),
        (0, part, *keep_first),
        (part, part, *send_second),
        (part, part, *keep_second),
    ]


def rows_back(blocks, order, split, lefts, groups, side, name, after=()):
    length = lefts[0].shape[0]
    count, places = blocks.shape[0], order.shape[0]
    half = groups[0][0].rows // 2
    rows = length // places
    widths = [left.shape[1] for left in lefts]
    depth = sum(widths)
    n = len(lefts)
    arrays = [array for weights, _, _ in groups for array in weights.arrays]
    k = len(arrays)
    pieces = count // 2
    plan = split_outputs(split, rows, half, places)

    def kernel(blk, places_ref, *refs):
        left_refs, w_refs = refs[:n], refs[n : n + k]
        out_refs = refs[n + k : n + k + len(plan)]
        joined_ref, w_ref, left_sems, sems = refs[-4:]
        step = pl.program_id(0)

        def left_copies(at):
            slot, start, col, found = lax.rem(at, 2), pl.multiple_of(places_ref[at] * rows, rows), 0, []
            for i, (ref, cols) in enumerate(zip(left_refs, widths)):
                found.append(
                    pltpu.make_async_copy(
                        ref.at[pl.ds(start, rows), :],
                        joined_ref.at[slot, :, pl.ds(col, cols)],
                        left_sems.at[slot, i],
                    )
                )
                col += cols
            return found

        per_group, at, col = [], 0, 0
        for i, (weights, start, cols) in enumerate(groups):
            more = len(weights.arrays)
            per_group.append(
                weights.copies(
                    w_refs[at : at + more], blk, count, side, start, cols, w_ref.at[:, pl.ds(col, cols)], sems.at[i]
                )
            )
            at, col = at + more, col + cols

        @pl.when(step == 0)
        def _():
            for copy in left_copies(0):
                copy.start()
            for piece in per_group:
                for copy in piece:
                    copy.start()

        @pl.when(step + 1 < places)
        def _():
            for copy in left_copies(step + 1):
                copy.start()

        for copy in left_copies(step):
            copy.wait()

        @pl.when(step == 0)
        def _():
            for piece in per_group:
                for copy in piece:
                    copy.wait()

        low = dot(joined_ref[lax.rem(step, 2)], w_ref[...], NT).astype(BF)
        for (col, cols, steps, _), ref in zip(plan, out_refs):

            def store(ref=ref, col=col, cols=cols):
                ref[...] = low[:, col : col + cols]

            if len(steps) > 2:
                store()
            else:
                pl.when(functools.reduce(jnp.logical_or, [step == at for at in steps]))(store)

    def out_spec(cols, where):
        return pl.BlockSpec((rows, cols), lambda m, blk, o: where(m, blk))

    return call(
        kernel,
        name,
        2 * length * half * depth,
        2 * length * depth + 2 * half * depth + 2 * length * half,
        (*lefts, *arrays),
        (places,),
        [pl.BlockSpec(memory_space=pl.ANY)] * (n + k),
        [out_spec(cols, where) for _, cols, _, where in plan],
        [struct((len(steps) * rows, cols)) for _, cols, steps, _ in plan],
        scratch=[
            pltpu.VMEM((2, rows, depth), BF),
            pltpu.VMEM((half, depth), BF),
            pltpu.SemaphoreType.DMA((2, n)),
            pltpu.SemaphoreType.DMA((len(groups), pieces)),
        ],
        prefetch=(blocks, order),
        after=after,
    )


def gain_sums(order, split, parts, unit, after=()):
    length, width = unit.shape
    half, places = width // 2, order.shape[0]
    rows = length // places
    plan = split_outputs(split, rows, half, places)
    n = len(plan)

    def kernel(places_ref, unit_ref, *refs):
        sum_ref = refs[2 * n]
        step = pl.program_id(0)

        @pl.when(step == 0)
        def _():
            sum_ref[...] = jnp.zeros_like(sum_ref)

        for side in range(2):
            for i, (col, cols, steps, _) in enumerate(plan):

                def add(ref=refs[side * n + i], start=side * half + col, cols=cols):
                    here = slice(start, start + cols)
                    wide = ref[...].astype(F32)
                    sum_ref[0:8, here] += eight_rows(wide * unit_ref[:, here].astype(F32))
                    sum_ref[8:16, here] += eight_rows(wide)

                if len(steps) > 2:
                    add()
                else:
                    pl.when(functools.reduce(jnp.logical_or, [step == at for at in steps]))(add)

    def spec(cols, where):
        return pl.BlockSpec((rows, cols), lambda m, o: where(m, o))

    return call(
        kernel,
        "gain_sums",
        0,
        4 * length * width,
        (unit, *parts[0], *parts[1]),
        (places,),
        [pl.BlockSpec((rows, width), lambda m, o: (o[m], 0))]
        + [spec(cols, where) for _, cols, _, where in plan] * 2,
        pl.BlockSpec((16, width), lambda m, o: (0, 0)),
        struct((16, width), F32),
        prefetch=(order,),
        after=after,
    )


def turned_sums(sums, units):
    depth, cols = sums.shape
    inner = cols - units

    def kernel(sums_ref, fc2_ref, out_ref):
        fc2_ref[...] = sums_ref[:, :units].T.astype(F32)
        out_ref[...] = sums_ref[:, units:].T.astype(F32)

    def whole(shape):
        return pl.BlockSpec(shape, lambda i: (0, 0))

    return call(
        kernel,
        "turned_sums",
        0,
        6 * depth * cols,
        (sums,),
        (1,),
        [whole((depth, cols))],
        [whole((units, depth)), whole((inner, depth))],
        [struct((units, depth), F32), struct((inner, depth), F32)],
    )


def end_call(kernel, name, blocks, fulls, terms, vector, dtype, after):
    length, width = fulls[0].shape
    rows = min(128, length)
    n = len(fulls)
    counts = [len(part) for part in terms]

    def body(blk, *refs):
        at, parts = n, []
        for number in counts:
            total = refs[at][...].astype(F32)
            for ref in refs[at + 1 : at + number]:
                total = total + ref[...].astype(F32)
            parts.append(total)
            at += number
        count, out_ref = blocks.shape[0], refs[at + 1]
        cols = width // count
        values = [ordered(ref, blk, count, cols).astype(F32) for ref in refs[:n]]
        result = kernel(values, jnp.concatenate(parts, axis=1), refs[at][...])
        for p in range(count):
            place = pl.ds(pl.multiple_of(blk[p] * cols, cols), cols)
            out_ref[:, place] = result[:, p * cols : (p + 1) * cols].astype(dtype)

    full = pl.BlockSpec((rows, width), lambda m, blk: (m, 0))
    flat = [array for part in terms for array in part]
    return call(
        body,
        name,
        0,
        10 * length * width,
        (*fulls, *flat, vector),
        (length // rows,),
        [full] * n
        + [pl.BlockSpec((rows, array.shape[1]), lambda m, blk: (m, 0)) for array in flat]
        + [pl.BlockSpec((1, width), lambda m, blk: (0, 0))],
        full,
        struct((length, width), dtype),
        prefetch=(blocks,),
        after=after,
    )


def add_branch(blocks, x, terms, out_bias, after=()):
    return end_call(
        lambda fulls, branch, bias: fulls[0] + branch + bias, "add_branch", blocks, (x,), terms, out_bias, BF, after
    )


def norm_back(blocks, x, g, terms, gain, after=()):
    def kernel(fulls, grads, scale):
        x, g = fulls
        centered = x - jnp.mean(x, axis=1, keepdims=True)
        variance = jnp.mean(centered * centered, axis=1, keepdims=True)
        inv_std = lax.rsqrt(variance + EPSILON)
        unit = centered * inv_std
        scaled = grads * scale
        mean = jnp.mean(scaled, axis=1, keepdims=True)
        along = jnp.mean(scaled * unit, axis=1, keepdims=True)
        return g + inv_std * (scaled - mean - unit * along)

    return end_call(kernel, "norm_back", blocks, (x, g), terms, gain, F32, after)


def flip(value, axis, size, bit):
    return lax.ppermute(value, axis, [(i, i ^ bit) for i in range(size)])


def flip_sum(value, axis, size):
    bit = 1
    while bit < size:
        value = value + flip(value, axis, size, bit)
        bit *= 2
    return value


class Ring:
    def __init__(self, n_dp):
        self.size = n_dp
        self.chips = n_dp // 2

    def send(self, value):
        pairs = [
            (z * 2 + c, ((z + 1) % self.chips) * 2 + c) for z in range(self.chips) for c in range(2)
        ]
        return lax.ppermute(value, "dp", pairs)

    def swap(self, value):
        return flip(value, "dp", self.size, 1)


def per_device(
    sizes, layer_input, ln_gain, ln_bias, out_bias, w_qkv, b_qkv, w_out, w_fc1, b_fc1, w_fc2, out_grad
):
    n_dp, n_tensor = sizes
    ring = Ring(n_dp)
    chips = ring.chips
    d_index, t_index = lax.axis_index("dp"), lax.axis_index("tensor")
    place, core = d_index // 2, d_index % 2
    steps = jnp.arange(chips, dtype=jnp.int32)
    behind = ((place - steps) % chips) * 2
    blocks = jnp.concatenate([behind + core, behind + (1 - core)]).astype(jnp.int32)
    square = n_tensor == 4

    local, width = layer_input.shape[1:]
    depth = w_qkv.shape[0]
    inner = w_qkv.shape[2]
    units = w_fc1.shape[1]
    heads = inner // HD
    length = local * n_tensor
    pairs = inner // 128

    third = ln_gain.shape[0]
    x, g = layer_input[0], out_grad[0]
    x_all = lax.all_gather(x, "tensor", axis=0, tiled=True)
    heads_own, heads_sib = [heads_shard(w_qkv.reshape(depth, 3 * inner), w_out)], []

    def ring_step(own, sib, after):
        own.append(ring.send(own[-1]))
        sib.append(ring.swap(own[-2]))
        own[-1], sib[-1], *rest = tie([own[-1], sib[-1], *after], [])
        return rest

    vectors = jnp.stack([ln_gain, ln_bias, out_bias]).astype(F32).reshape(1, 3 * third)
    table = jnp.where(jnp.arange(n_tensor)[:, None] == t_index, vectors, 0.0)
    table = flip_sum(table, "tensor", n_tensor)
    small = jnp.concatenate([table.reshape(-1), b_qkv.astype(F32).reshape(-1), b_fc1.astype(F32).reshape(-1)])
    g_placed, bias_part = order_columns(blocks, g, after=heads_own)
    small, g_placed = ring_step(heads_own, heads_sib, [small, g_placed])
    fc1_shard = stage(w_fc1, False, [small])
    tables = rotary_rows(length)
    small = flip_sum(
        jnp.where(jnp.arange(n_dp)[:, None] == d_index, small[None, :], 0.0), "dp", n_dp
    )
    small, fc1_shard = ring_step(heads_own, heads_sib, [small, fc1_shard])
    chosen = (blocks[:, None] == jnp.arange(n_dp)[None, :]).astype(F32)
    cut = n_tensor * 3 * third
    vectors = jnp.einsum("pd,dj->pj", chosen, small[:, :cut], precision=lax.Precision.HIGHEST)
    vectors = jnp.transpose(vectors.reshape(n_dp, n_tensor, 3, third), (2, 0, 1, 3))
    gain, shift, bias_out = (vectors[i].reshape(1, width) for i in range(3))
    b_width = HD // n_dp
    tail = cut + b_qkv.size
    bias_qkv = jnp.transpose(small[:, cut:tail].reshape(n_dp, 3, heads, b_width), (1, 2, 0, 3))
    bias_qkv = bias_qkv.reshape(1, 3 * inner)
    bias_fc1 = jnp.transpose(small[:, tail:].reshape(n_dp, units // HD, b_width), (1, 0, 2))
    bias_fc1 = bias_fc1.reshape(1, units)
    gain, bias_qkv, bias_fc1, fc1_shard, *tables = ring_step(
        heads_own, heads_sib, [gain, bias_qkv, bias_fc1, fc1_shard, *tables]
    )
    while len(heads_own) < chips:
        ring_step(heads_own, heads_sib, [])
    heads_sib.append(ring.swap(heads_own[-1]))
    heads_weights = Weights(heads_own + heads_sib)
    g_all = lax.all_gather(g_placed, "tensor", axis=0, tiled=True)
    if square:
        order = (jnp.array([3, 1, 2, 0], jnp.int32) ^ t_index).astype(jnp.int32)
    else:
        order = jnp.arange(n_tensor, dtype=jnp.int32)

    def split(kind):
        return kind if square else None

    bits = {"first": [1], "second": [2], "both": [1, 2]}

    def cross_once(kind, parts):
        if not square:
            return [lax.psum_scatter(parts[0], "tensor", scatter_dimension=0, tiled=True)]
        return [flip(parts[2 * i], "tensor", 4, bit) for i, bit in enumerate(bits[kind])]

    def cross_add(parts, got):
        if not square:
            return []
        kept = parts[1::2]
        return [(k[local:].astype(F32) + r[local:].astype(F32)).astype(BF) for k, r in zip(kept, got)]

    def cross_twice(kind, sums):
        return [flip(value, "tensor", 4, 3 - bit) for value, bit in zip(sums, bits[kind])] if square else []

    def cross_terms(parts, got, last):
        if not square:
            return [got]
        return [list(terms) for terms in zip(parts[1::2], got, last)]

    fc1_own, fc1_sib = [fc1_shard], []
    normed, unit, qkv = norm_project(
        blocks, x_all, gain, shift, bias_qkv, tables, heads_weights, after=[fc1_shard]
    )
    (qkv,) = ring_step(fc1_own, fc1_sib, [qkv])
    first = pairs // 2
    context, log_first = attend(qkv, 0, first, after=[fc1_own[-1]])
    (log_first,) = ring_step(fc1_own, fc1_sib, [log_first])
    context, log_second = attend(qkv, first, pairs - first, before=context, after=[fc1_own[-1]])
    (log_second,) = ring_step(fc1_own, fc1_sib, [log_second])
    while len(fc1_own) < chips:
        ring_step(fc1_own, fc1_sib, [])
    fc1_sib.append(ring.swap(fc1_own[-1]))
    log_total = jnp.concatenate([log_first, log_second], axis=0)
    fc1_weights = Weights(fc1_own + fc1_sib)
    fc2_shard = stage(w_fc2, True, [log_second])
    fc2_weights = Weights([lax.all_gather(fc2_shard, "dp", axis=0, tiled=True)], depth, placed=True)
    act, slope = expand(blocks, normed, fc1_weights, bias_fc1, after=[fc2_shard])

    def scatter(parts):
        return lax.psum_scatter(parts, "dp", scatter_dimension=0, tiled=True)

    fc2_grad, context_grad = weight_grad(
        blocks, g_all, [act, context], min(512, inner), "fc2_grad", heads_weights
    )
    fc2_sums = scatter(fc2_grad)
    *backs, b_qkv_part = attend_back(qkv, context, context_grad, log_total, tables)
    heads_sib_grad, heads_own_grad = weight_grad_halves(normed, backs, inner, "heads_grad")

    def ring_add(k, moving=None):
        cut = slice(k * depth, (k + 1) * depth)
        total = heads_own_grad[cut].astype(F32) + heads_other[cut].astype(F32)
        return total if moving is None else total + moving.astype(F32)

    heads_cols, fc2_cols = (heads_weights, 0, 3 * inner), (fc2_weights, 0, units)
    out_cols, fc1_cols = (heads_weights, 3 * inner, inner), (fc1_weights, 0, units)
    lefts = [act, context]
    branch_own = rows_back(
        blocks, order, split("first"), lefts, [fc2_cols, out_cols], 0, "branch_half", after=[heads_own_grad]
    )
    *branch_own, heads_other = tie([*branch_own, ring.swap(heads_sib_grad)], [])
    message = ring_add(1).astype(BF)
    branch_sib = rows_back(
        blocks, order, split("second"), lefts, [fc2_cols, out_cols], 1, "branch_half", after=[message]
    )
    *branch_sib, moving = tie([*branch_sib, ring.send(message)], [])
    message = ring_add(2, moving).astype(BF)
    hidden_grad, b_fc1_part = hidden_back(blocks, g_all, fc2_weights, slope, after=[message])
    hidden_grad, moving = tie([hidden_grad, ring.send(message)], [])
    for k in range(3, chips):
        message = ring_add(k, moving).astype(BF)
        if k < chips - 1:
            moving = ring.send(message)
    (fc1_grad,) = weight_grad(blocks, normed, [hidden_grad], min(1024, units), "fc1_grad", after=[message])
    branch_got = cross_once("first", branch_own) + cross_once("second", branch_sib)
    n = len(branch_got)
    fc1_grad, moving, *branch_got = tie([fc1_grad, ring.send(message), *branch_got], [])
    fc1_sums = scatter(fc1_grad)
    heads_sums = ring_add(0, moving)
    branch_sums = cross_add(branch_own, branch_got[:1]) + cross_add(branch_sib, branch_got[1:])
    branch_last = cross_twice("first", branch_sums[:1]) + cross_twice("second", branch_sums[1:])

    lefts = [*backs, hidden_grad]
    back_own = rows_back(
        blocks, order, split("both"), lefts, [heads_cols, fc1_cols], 0, "normed_back_half",
        after=[fc1_grad, *branch_sums],
    )
    n = len(back_own)
    joined = tie([*back_own, *branch_last], [])
    back_own, branch_last = joined[:n], joined[n:]
    branch_terms = cross_terms(branch_own, branch_got[:1], branch_last[:1])
    branch_terms += cross_terms(branch_sib, branch_got[1:], branch_last[1:])
    own_got = cross_once("both", back_own)
    back_sib = rows_back(
        blocks, order, split("both"), lefts, [heads_cols, fc1_cols], 1, "normed_back_half",
        after=[back_own[0]],
    )
    joined = tie([*back_sib, *own_got], [])
    back_sib, own_got = joined[:n], joined[n:]

    sib_got = cross_once("both", back_sib)
    own_last = cross_twice("both", cross_add(back_own, own_got))
    norm_sums = gain_sums(order, split("both"), (back_own, back_sib), unit).reshape(2, 8, n_dp, depth)
    norm_sums = jnp.einsum("pd,kpj->dkj", chosen, jnp.sum(norm_sums, axis=1), precision=lax.Precision.HIGHEST)
    b_qkv_part = jnp.sum(b_qkv_part.reshape(pairs, 3, 8, 128), axis=2)
    b_qkv_part = jnp.transpose(b_qkv_part, (1, 0, 2)).reshape(3, heads, n_dp, b_width)
    b_fc1_part = jnp.sum(b_fc1_part, axis=0).reshape(units // HD, n_dp, b_width)
    by_owner = jnp.concatenate(
        [
            norm_sums.reshape(n_dp, 2 * depth),
            bias_part[0].reshape(n_dp, depth),
            jnp.transpose(b_qkv_part, (2, 0, 1, 3)).reshape(n_dp, -1),
            jnp.transpose(b_fc1_part, (1, 0, 2)).reshape(n_dp, -1),
        ],
        axis=1,
    )

    sums = flip_sum(by_owner, "dp", n_dp)
    sums = lax.dynamic_index_in_dim(sums, d_index, 0, keepdims=False)
    w_fc2_grad, w_out_grad = turned_sums(fc2_sums, units)
    layer_output = add_branch(
        blocks, x, branch_terms, bias_out, after=[back_sib[0], w_fc2_grad, w_out_grad]
    )
    layer_output, sums, *sib_got = tie([layer_output, sums, *sib_got], [])
    sib_last = cross_twice("both", cross_add(back_sib, sib_got))
    mine = flip_sum(sums[: 3 * depth].reshape(3, depth), "tensor", n_tensor)
    mine = lax.dynamic_slice_in_dim(mine, t_index * third, third, 1)
    b_qkv_grad = sums[3 * depth : 3 * depth + b_qkv.size].reshape(b_qkv.shape)
    b_fc1_grad = sums[3 * depth + b_qkv.size :].reshape(b_fc1.shape)
    w_fc1_grad = fc1_sums.astype(F32)
    w_qkv_grad = heads_sums.reshape(depth, 3, inner)
    back_terms = cross_terms(back_own, own_got, own_last) + cross_terms(back_sib, sib_got, sib_last)
    input_grad = norm_back(blocks, x, g, back_terms, gain, after=[w_fc1_grad, w_qkv_grad])
    return (
        layer_output[None],
        input_grad[None],
        mine[0],
        mine[1],
        mine[2],
        w_qkv_grad,
        b_qkv_grad,
        w_out_grad,
        w_fc1_grad,
        b_fc1_grad,
        w_fc2_grad,
    )


def solution(mesh):
    in_specs = (
        P("dp", "tensor", None),
        P(("dp", "tensor")),
        P(("dp", "tensor")),
        P(("dp", "tensor")),
        P("dp", None, "tensor"),
        P(None, "tensor", "dp"),
        P("tensor", "dp"),
        P("dp", "tensor"),
        P("tensor", "dp"),
        P("tensor", "dp"),
        P("dp", "tensor", None),
    )
    out_specs = (
        P("dp", "tensor", None),
        P("dp", "tensor", None),
        P(("dp", "tensor")),
        P(("dp", "tensor")),
        P(("dp", "tensor")),
        P("dp", None, "tensor"),
        P(None, "tensor", "dp"),
        P("tensor", "dp"),
        P("dp", "tensor"),
        P("tensor", "dp"),
        P("tensor", "dp"),
    )
    sizes = (mesh.shape["dp"], mesh.shape["tensor"])
    return jax.shard_map(
        functools.partial(per_device, sizes),
        mesh=mesh,
        in_specs=in_specs,
        out_specs=out_specs,
        check_vma=False,
    )
```

```python
import functools
import math

import jax
import jax.numpy as jnp
from jax import lax
from jax.experimental import pallas as pl
from jax.experimental.pallas import tpu as pltpu
from jax.sharding import PartitionSpec as P

HD = 64
ROT = 32
EPSILON = 1e-05
NEG = -1e30
LOG2E = math.log2(math.e)
BF = jnp.bfloat16
F32 = jnp.float32
VMEM_BYTES = 56 << 20

NN = (((1,), (0,)), ((), ()))
NT = (((1,), (1,)), ((), ()))
TN = (((0,), (0,)), ((), ()))


def dot(a, b, dims):
    return lax.dot_general(a, b, dims, preferred_element_type=F32)


def eight_rows(value):
    rows, cols = value.shape
    return jnp.sum(value.reshape(rows // 8, 8, cols), axis=0)


def call(kernel, name, flops, moved, operands, grid, in_specs, out_specs, out_shape, scratch=(), prefetch=(), aliases=None, after=()):
    front = len(prefetch) + len(in_specs)

    def body(*refs):
        kernel(*refs[:front], *refs[front + len(after) :])

    return pl.pallas_call(
        body,
        name=name,
        grid_spec=pltpu.PrefetchScalarGridSpec(
            num_scalar_prefetch=len(prefetch),
            grid=grid,
            in_specs=list(in_specs) + [pl.BlockSpec(memory_space=pl.ANY)] * len(after),
            out_specs=out_specs,
            scratch_shapes=list(scratch),
        ),
        out_shape=out_shape,
        input_output_aliases=aliases or {},
        compiler_params=pltpu.CompilerParams(vmem_limit_bytes=VMEM_BYTES),
        cost_estimate=pl.CostEstimate(flops=int(flops), bytes_accessed=int(moved), transcendentals=0),
    )(*prefetch, *operands, *after)


class Weights:
    def __init__(self, arrays, size=None, placed=False):
        self.arrays = list(arrays)
        self.placed = placed
        self.cols = self.arrays[0].shape[1]
        self.size = size or self.arrays[0].shape[0]
        self.rows = self.arrays[0].shape[0] if placed else self.size * len(self.arrays)

    def copies(self, refs, blk, count, side, col, cols, target, sems):
        found = []

        def add(source, start, size, place):
            found.append(
                pltpu.make_async_copy(
                    source.at[pl.ds(start, size), pl.ds(col, cols)],
                    target.at[pl.ds(place, size), :],
                    sems.at[len(found)],
                )
            )

        half = self.rows // 2
        if self.placed:
            size = self.rows // count
            first, last = (0, count) if side is None else (side * count // 2, (side + 1) * count // 2)
            for p in range(first, last):
                add(refs[0], pl.multiple_of(blk[p] * size, size), size, (p - first) * size)
            return found
        place = 0
        for ref in refs:
            size = self.size
            if side is None or place // half == side:
                add(ref, 0, size, place - (side or 0) * half)
            place += size
        return found

    def number(self, count, side=None):
        total = count if self.placed else len(self.arrays)
        return total if side is None else total // 2


def struct(shape, dtype=BF):
    return jax.ShapeDtypeStruct(shape, dtype)


def tie(values, after):
    n = len(values)
    anywhere = pl.BlockSpec(memory_space=pltpu.HBM)

    def kernel(*refs):
        del refs

    return pl.pallas_call(
        kernel,
        name="tie",
        in_specs=[anywhere] * (n + len(after)),
        out_specs=[anywhere] * n,
        out_shape=[struct(v.shape, v.dtype) for v in values],
        input_output_aliases={i: i for i in range(n)},
    )(*values, *after)


def order_columns(blocks, x, after=()):
    rows, width = x.shape
    count = blocks.shape[0]
    cols = width // count
    step_rows = min(256, rows)

    def kernel(blk, x_ref, out_ref, sum_ref):
        for p in range(count):
            place = pl.ds(pl.multiple_of(blk[p] * cols, cols), cols)
            out_ref[:, p * cols : (p + 1) * cols] = x_ref[:, place]

        @pl.when(pl.program_id(0) == 0)
        def _():
            sum_ref[...] = jnp.zeros_like(sum_ref)

        sum_ref[0:1, :] += jnp.sum(x_ref[...].astype(F32), axis=0, keepdims=True)

    block = pl.BlockSpec((step_rows, width), lambda m, blk: (m, 0))
    return call(
        kernel,
        "order_columns",
        0,
        4 * rows * width,
        (x,),
        (rows // step_rows,),
        [block],
        [block, pl.BlockSpec((8, width), lambda m, blk: (0, 0))],
        [struct(x.shape), struct((8, width), F32)],
        prefetch=(blocks,),
        after=after,
    )


def heads_shard(w_qkv, w_out):
    _, depth, inner = w_qkv.shape

    def kernel(q_ref, o_ref, out_ref):
        for part in range(3):
            out_ref[:, part * inner : (part + 1) * inner] = q_ref[part]
        out_ref[:, 3 * inner :] = o_ref[...].T

    return call(
        kernel,
        "heads_shard",
        0,
        16 * depth * inner,
        (w_qkv, w_out),
        (1,),
        [
            pl.BlockSpec(w_qkv.shape, lambda i: (0, 0, 0)),
            pl.BlockSpec(w_out.shape, lambda i: (0, 0)),
        ],
        pl.BlockSpec((depth, 4 * inner), lambda i: (0, 0)),
        struct((depth, 4 * inner)),
    )


def heads_sum(own, other, moving):
    depth, wide = moving.shape
    inner = wide // 3
    rows = min(64, depth)

    def kernel(own_ref, other_ref, moving_ref, out_ref):
        total = own_ref[...].astype(F32) + other_ref[...].astype(F32) + moving_ref[...].astype(F32)
        for part in range(3):
            out_ref[part] = total[:, part * inner : (part + 1) * inner]

    block = pl.BlockSpec((rows, wide), lambda m: (m, 0))
    return call(
        kernel,
        "heads_sum",
        0,
        10 * depth * wide,
        (own, other, moving),
        (depth // rows,),
        [block] * 3,
        pl.BlockSpec((3, rows, inner), lambda m: (0, m, 0)),
        struct((3, depth, inner), F32),
    )


def stage(weight, flip, after, rows=None):
    start, count = rows or (0, weight.shape[0])
    taken = (count, weight.shape[1])
    shape = taken[::-1] if flip else taken

    def kernel(w_ref, out_ref):
        out_ref[...] = w_ref[...].T if flip else w_ref[...]

    return call(
        kernel,
        "stage_weight",
        0,
        4 * taken[0] * taken[1],
        (weight,),
        (1,),
        [pl.BlockSpec(taken, lambda i: (start // count, 0))],
        pl.BlockSpec(shape, lambda i: (0, 0)),
        struct(shape),
        after=after,
    )


def rotary_rows(length):
    lane = jnp.arange(128, dtype=jnp.int32)[None, :] % HD
    half = ROT // 2
    frequency = 10000.0 ** (-2.0 * (lane % half).astype(F32) / ROT)
    angles = jnp.arange(length, dtype=F32)[:, None] * frequency
    cosine, sine = jnp.cos(angles), jnp.sin(angles)
    keep = jnp.where(lane < ROT, cosine, 1.0)
    ahead = jnp.where(lane < half, -sine, 0.0)
    behind = jnp.where((lane >= half) & (lane < ROT), sine, 0.0)
    return keep, ahead, behind


def turn(u, keep, ahead, behind):
    return u * keep + pltpu.roll(u, 128 - ROT // 2, 1) * ahead + pltpu.roll(u, ROT // 2, 1) * behind


def ordered(ref, blk, count, cols):
    return jnp.concatenate(
        [ref[:, pl.ds(pl.multiple_of(blk[p] * cols, cols), cols)] for p in range(count)], axis=1
    )


def norm_project(blocks, x_all, gain, shift, bias, tables, weights, after=()):
    length, width = x_all.shape
    wide = bias.shape[1]
    inner = wide // 3
    rows = min(512, length)
    k, count = len(weights.arrays), blocks.shape[0]

    def kernel(blk, x_ref, gain_ref, shift_ref, bias_ref, keep_ref, ahead_ref, behind_ref, *refs):
        w_refs = refs[:k]
        normed_ref, unit_ref, qkv_ref, w_ref, sems = refs[k:]
        step = pl.program_id(0)
        copies = weights.copies(w_refs, blk, count, None, 0, wide, w_ref, sems)

        @pl.when(step == 0)
        def _():
            for copy in copies:
                copy.start()

        x = ordered(x_ref, blk, count, width // count).astype(F32)
        centered = x - jnp.mean(x, axis=1, keepdims=True)
        variance = jnp.mean(centered * centered, axis=1, keepdims=True)
        unit = centered * lax.rsqrt(variance + EPSILON)
        unit_ref[...] = unit.astype(BF)
        normed_ref[...] = (unit * gain_ref[...] + shift_ref[...]).astype(BF)

        @pl.when(step == 0)
        def _():
            for copy in copies:
                copy.wait()

        merged = dot(normed_ref[...], w_ref[...], NN) + bias_ref[...]
        for start in range(0, wide, 128):
            u = merged[:, start : start + 128]
            if start < 2 * inner:
                u = turn(u, keep_ref[...], ahead_ref[...], behind_ref[...])
            qkv_ref[:, start : start + 128] = u.astype(BF)

    def whole(shape):
        return pl.BlockSpec(shape, lambda j, blk: (0, 0))

    def block(cols):
        return pl.BlockSpec((rows, cols), lambda j, blk: (j, 0))

    return call(
        kernel,
        "norm_project",
        0,
        0,
        (x_all, gain, shift, bias, *tables, *weights.arrays),
        (length // rows,),
        [block(width), whole((1, width)), whole((1, width)), whole((1, wide))]
        + [block(128)] * 3
        + [pl.BlockSpec(memory_space=pl.ANY)] * k,
        [block(width), block(width), block(wide)],
        [struct((length, width)), struct((length, width)), struct((length, wide))],
        scratch=[pltpu.VMEM((width, wide), BF), pltpu.SemaphoreType.DMA((weights.number(count),))],
        prefetch=(blocks,),
        after=after,
    )


def attend(qkv, first, number, before=None, after=()):
    length = qkv.shape[0]
    inner = qkv.shape[1] // 3
    pairs = inner // 128
    block = min(1024, length)
    count = length // block
    scale = LOG2E / math.sqrt(HD)
    n = 0 if before is None else 1

    def kernel(q_ref, k_ref, v_ref, *refs):
        o_ref, lse_ref, turned_ref = refs[n:]
        lane = lax.broadcasted_iota(jnp.int32, (1, 128), 1)

        @pl.when(pl.program_id(1) == 0)
        def _():
            turned_ref[...] = v_ref[...].T

        for index in range(count):

            @pl.when(pl.program_id(1) == index)
            def _(index=index):
                queries = q_ref[...]
                blank = jnp.zeros_like(queries)
                end = (index + 1) * block
                found = []
                for head in range(2):
                    mine = (lane < HD) if head == 0 else (lane >= HD)
                    scores = dot(k_ref[:end, :], jnp.where(mine, queries, blank), NT)
                    row = lax.broadcasted_iota(jnp.int32, (block, block), 0)
                    col = lax.broadcasted_iota(jnp.int32, (block, block), 1)
                    last = jnp.where(row <= col, scores[end - block :], NEG)
                    if index:
                        scores = jnp.concatenate([scores[: end - block], last], axis=0)
                    else:
                        scores = last
                    top = jnp.max(scores, axis=0, keepdims=True)
                    weights = jnp.exp2((scores - top) * scale)
                    total = jnp.sum(weights, axis=0, keepdims=True)
                    out = dot(turned_ref[head * HD : (head + 1) * HD, :end], weights.astype(BF), NN)
                    found.append(out / total)
                    lse_ref[0, head : head + 1, :] = top * scale + jnp.log2(total)
                o_ref[...] = jnp.concatenate(found, axis=0).T.astype(BF)

    return call(
        kernel,
        "attend",
        0,
        0,
        (qkv, qkv, qkv) + ((before,) if n else ()),
        (number, count),
        [
            pl.BlockSpec((block, 128), lambda h, i: (i, first + h)),
            pl.BlockSpec((length, 128), lambda h, i: (0, pairs + first + h)),
            pl.BlockSpec((length, 128), lambda h, i: (0, 2 * pairs + first + h)),
        ]
        + [pl.BlockSpec(memory_space=pl.ANY)] * n,
        [
            pl.BlockSpec((block, 128), lambda h, i: (i, first + h)),
            pl.BlockSpec((1, 2, block), lambda h, i: (h, 0, i)),
        ],
        [struct((length, inner)), struct((number, 2, length), F32)],
        scratch=[pltpu.VMEM((128, length), BF)],
        aliases={3: 0} if n else {},
        after=after,
    )


def attend_back(qkv, context, context_grad, log_total, tables, after=()):
    length = qkv.shape[0]
    inner = qkv.shape[1] // 3
    pairs = inner // 128
    block = min(512, length)
    count = length // block
    scale = LOG2E / math.sqrt(HD)
    shrink = 1.0 / math.sqrt(HD)

    def kernel(q_ref, k_ref, v_ref, o_ref, do_ref, lse_ref, keep_ref, ahead_ref, behind_ref, *rest):
        dq_ref, dk_ref, dv_ref, sum_ref, k_total, v_total = rest
        step = pl.program_id(1)
        lane = lax.broadcasted_iota(jnp.int32, (1, 128), 1)

        @pl.when(step == 0)
        def _():
            k_total[...] = jnp.zeros_like(k_total)
            v_total[...] = jnp.zeros_like(v_total)
            sum_ref[...] = jnp.zeros_like(sum_ref)

        def turn_back(u, rows):
            return turn(u, keep_ref[rows, :], -ahead_ref[rows, :], -behind_ref[rows, :])

        for index in range(count):

            @pl.when(step == index)
            def _(index=index):
                queries, grads = q_ref[...], do_ref[...]
                blank = jnp.zeros_like(queries)
                queries_turned, grads_turned = queries.T, grads.T
                products = grads.astype(F32) * o_ref[...].astype(F32)
                log_totals = lse_ref[0].T
                q_total = [None, None]
                for other in range(index + 1):
                    rows = slice(other * block, (other + 1) * block)
                    keys, values = k_ref[rows, :], v_ref[rows, :]
                    for head in range(2):
                        mine = (lane < HD) if head == 0 else (lane >= HD)
                        here = slice(head * HD, (head + 1) * HD)
                        delta = jnp.sum(products[:, here], axis=1, keepdims=True)
                        scores = dot(jnp.where(mine, queries, blank), keys, NT)
                        if other == index:
                            row = lax.broadcasted_iota(jnp.int32, (block, block), 0)
                            col = lax.broadcasted_iota(jnp.int32, (block, block), 1)
                            scores = jnp.where(col <= row, scores, NEG)
                        probs = jnp.exp2(scores * scale - log_totals[:, head : head + 1])
                        probs_grad = dot(jnp.where(mine, grads, blank), values, NT)
                        score_grad = (probs * (probs_grad - delta)).astype(BF)
                        v_total[here, rows] += dot(grads_turned[here, :], probs.astype(BF), NN)
                        k_total[here, rows] += dot(queries_turned[here, :], score_grad, NN)
                        term = dot(score_grad, keys, NN)
                        q_total[head] = term if other == 0 else q_total[head] + term
                dq = jnp.where(lane < HD, q_total[0], q_total[1]) * shrink
                rows = slice(index * block, (index + 1) * block)
                dq = turn_back(dq, rows).astype(BF)
                dq_ref[...] = dq
                sum_ref[0, 0:8, :] += eight_rows(dq.astype(F32))

        @pl.when(step == count - 1)
        def _():
            for index in range(count):
                rows = slice(index * block, (index + 1) * block)
                dk = turn_back(k_total[:, rows].T * shrink, rows).astype(BF)
                dk_ref[rows, :] = dk
                sum_ref[0, 8:16, :] += eight_rows(dk.astype(F32))
                dv = v_total[:, rows].T.astype(BF)
                dv_ref[rows, :] = dv
                sum_ref[0, 16:24, :] += eight_rows(dv.astype(F32))

    def column(offset):
        return pl.BlockSpec((length, 128), lambda h, i: (0, offset + h))

    def rows_of(offset):
        return pl.BlockSpec((block, 128), lambda h, i: (i, offset + h))

    table = pl.BlockSpec((length, 128), lambda h, i: (0, 0))
    return call(
        kernel,
        "attend_back",
        60 * length * length * inner,
        16 * length * inner,
        (qkv, qkv, qkv, context, context_grad, log_total, *tables),
        (pairs, count),
        [
            rows_of(0),
            column(pairs),
            column(2 * pairs),
            rows_of(0),
            rows_of(0),
            pl.BlockSpec((1, 2, block), lambda h, i: (h, 0, i)),
            table,
            table,
            table,
        ],
        [rows_of(0), column(0), column(0), pl.BlockSpec((1, 24, 128), lambda h, i: (h, 0, 0))],
        [struct((length, inner))] * 3 + [struct((pairs, 24, 128), F32)],
        scratch=[pltpu.VMEM((128, length), F32)] * 2,
        after=after,
    )


def times_weights(blocks, rows_in, weights, name, extra, outs, finish, after=()):
    length, width = rows_in.shape
    total_cols = weights.cols
    rows, cols = min(512, length), min(1024, total_cols)
    chunks = total_cols // cols
    k, count, e = len(weights.arrays), blocks.shape[0], len(extra)
    number = weights.number(count)

    def kernel(blk, a_ref, *refs):
        w_refs, extra_refs, out_refs = refs[:k], refs[k : k + e], refs[k + e : -2]
        w_ref, sems = refs[-2:]
        chunk, step = pl.program_id(0), pl.program_id(1)
        copies = [
            weights.copies(w_refs, blk, count, None, c * cols, cols, w_ref.at[c], sems.at[c])
            for c in range(chunks)
        ]

        @pl.when((chunk == 0) & (step == 0))
        def _():
            for per_chunk in copies:
                for copy in per_chunk:
                    copy.start()

        for c in range(chunks):

            @pl.when((chunk == c) & (step == 0))
            def _(c=c):
                for copy in copies[c]:
                    copy.wait()

        finish(dot(a_ref[...], w_ref[chunk], NN), step == 0, extra_refs, out_refs)

    specs = {
        "block": pl.BlockSpec((rows, cols), lambda n, m, blk: (m, n)),
        "row": pl.BlockSpec((1, cols), lambda n, m, blk: (0, n)),
        "sum": pl.BlockSpec((8, cols), lambda n, m, blk: (0, n)),
    }
    shapes = {"block": struct((length, total_cols)), "sum": struct((8, total_cols), F32)}
    return call(
        kernel,
        name,
        2 * length * width * total_cols,
        2 * length * width + 2 * width * total_cols + 4 * length * total_cols,
        (rows_in, *weights.arrays, *(value for _, value in extra)),
        (chunks, length // rows),
        [pl.BlockSpec((rows, width), lambda n, m, blk: (m, 0))]
        + [pl.BlockSpec(memory_space=pl.ANY)] * k
        + [specs[kind] for kind, _ in extra],
        [specs[kind] for kind in outs],
        [shapes[kind] for kind in outs],
        scratch=[
            pltpu.VMEM((chunks, width, cols), BF),
            pltpu.SemaphoreType.DMA((chunks, number)),
        ],
        prefetch=(blocks,),
        after=after,
    )


def expand(blocks, normed, weights, bias, after=()):
    def finish(product, first, extra_refs, out_refs):
        hidden = product + extra_refs[0][...]
        c = math.sqrt(2.0 / math.pi)
        square = hidden * hidden
        inner = hidden * (c + (c * 0.044715) * square)
        gate = 0.5 + 0.5 * jnp.tanh(inner)
        act = hidden * gate
        out_refs[0][...] = act.astype(BF)
        out_refs[1][...] = (
            gate + act * (1.0 - gate) * (2.0 * c + (6.0 * c * 0.044715) * square)
        ).astype(BF)

    return times_weights(
        blocks, normed, weights, "expand", [("row", bias)], ["block", "block"], finish, after
    )


def hidden_back(blocks, g_all, weights, slope, after=()):
    def finish(product, first, extra_refs, out_refs):
        grad = product * extra_refs[0][...].astype(F32)
        out_refs[0][...] = grad.astype(BF)

        @pl.when(first)
        def _():
            out_refs[1][...] = jnp.zeros_like(out_refs[1])

        out_refs[1][...] += eight_rows(grad)

    return times_weights(
        blocks, g_all, weights, "hidden_back", [("block", slope)], ["block", "sum"], finish, after
    )


def columns_of(rights, cols):
    starts, total = [], 0
    for right in rights:
        starts.append(total)
        total += right.shape[1] // cols
    return starts + [total]


def weight_grad(blocks, rows_in, right, name, more=None, weights=None, after=()):
    length, width = rows_in.shape
    half = width // 2
    count = blocks.shape[0]
    depth = width // count
    cols = min(1024, right.shape[1])
    total = right.shape[1] // cols
    k = len(weights.arrays) if weights else 0
    extra = 2 if k else 0

    def kernel(blk, a_ref, right_ref, *refs):
        chunk, side = pl.program_id(0), pl.program_id(1)

        def product(ref, target):
            low = dot(a_ref[...], ref[...], TN).astype(BF)
            for p in range(count // 2):
                place = pl.multiple_of(blk[side * (count // 2) + p] * depth, depth)
                target[pl.ds(place, depth), :] = low[p * depth : (p + 1) * depth]

        if not k:
            product(right_ref, refs[0])
            return
        more_ref, w_refs, inner = refs[0], refs[1 : 1 + k], more.shape[1]
        out_ref, more_out_ref, back_ref, w_ref, sum_ref, sems = refs[1 + k :]
        copies = weights.copies(w_refs, blk, count, None, weights.cols - inner, inner, w_ref, sems)

        @pl.when((chunk == 0) & (side == 0))
        def _():
            for copy in copies:
                copy.start()

        pl.when(chunk < total)(lambda: product(right_ref, out_ref))
        pl.when(chunk == total)(lambda: product(more_ref, more_out_ref))

        @pl.when((chunk == total + 1) & (side == 0))
        def _():
            for copy in copies:
                copy.wait()
            sum_ref[...] = dot(a_ref[...], w_ref[:half, :], NN)

        @pl.when((chunk == total + 1) & (side == 1))
        def _():
            back_ref[...] = (sum_ref[...] + dot(a_ref[...], w_ref[half:, :], NN)).astype(BF)

    def whole(shape):
        return pl.BlockSpec(shape, lambda n, s, blk: (0, 0))

    in_specs = [
        pl.BlockSpec((length, half), lambda n, s, blk: (0, s)),
        pl.BlockSpec((length, cols), lambda n, s, blk: (0, jnp.minimum(n, total - 1))),
    ]
    out_specs = [pl.BlockSpec((width, cols), lambda n, s, blk: (0, jnp.minimum(n, total - 1)))]
    out_shape = [struct((width, right.shape[1]))]
    scratch = []
    if k:
        inner = more.shape[1]
        in_specs += [whole((length, inner))] + [pl.BlockSpec(memory_space=pl.ANY)] * k
        out_specs += [whole((width, inner)), whole((length, inner))]
        out_shape += [struct((width, inner)), struct((length, inner))]
        scratch = [
            pltpu.VMEM((width, inner), BF),
            pltpu.VMEM((length, inner), F32),
            pltpu.SemaphoreType.DMA((weights.number(count),)),
        ]
    return call(
        kernel,
        name,
        2 * length * width * right.shape[1],
        2 * length * width + 4 * length * right.shape[1] + 2 * width * right.shape[1],
        (rows_in, right, *((more, *weights.arrays) if k else ())),
        (total + extra, 2),
        in_specs,
        out_specs,
        out_shape,
        scratch=scratch,
        prefetch=(blocks,),
        after=after,
    )


def weight_grad_halves(rows_in, rights, cols, name, after=()):
    length, width = rows_in.shape
    half = width // 2
    starts = columns_of(rights, cols)
    n, total = len(rights), starts[-1]

    def kernel(a_ref, *refs):
        sib_ref, own_ref = refs[n:]
        side, chunk = pl.program_id(0), pl.program_id(1)
        for i in range(n):

            @pl.when((chunk >= starts[i]) & (chunk < starts[i + 1]))
            def _(i=i):
                product = dot(a_ref[...], refs[i][...], TN).astype(BF)

                @pl.when(side == 0)
                def _():
                    sib_ref[...] = product

                @pl.when(side == 1)
                def _():
                    own_ref[...] = product

    def right_spec(i):
        number = starts[i + 1] - starts[i]
        return pl.BlockSpec((length, cols), lambda s, n: (0, jnp.clip(n - starts[i], 0, number - 1)))

    return call(
        kernel,
        name,
        2 * length * width * total * cols,
        2 * length * width + 4 * length * total * cols + 2 * width * total * cols,
        (rows_in, *rights),
        (2, total),
        [pl.BlockSpec((length, half), lambda s, n: (0, 1 - s))] + [right_spec(i) for i in range(n)],
        [
            pl.BlockSpec((half, cols), lambda s, n: (0, jnp.where(s == 0, n, total - 1))),
            pl.BlockSpec((half, cols), lambda s, n: (0, jnp.where(s == 0, 0, n))),
        ],
        [struct((half, total * cols))] * 2,
        after=after,
    )


def split_outputs(split, rows, half, count):
    if split is None:
        return [(0, half, {m: m for m in range(count)}, lambda m, blk: (m, 0))]
    send_first = (({0: 1, 1: 0}), lambda m, blk: (jnp.where(m < 1, 1, 0), 0))
    keep_first = (({2: 1, 3: 0}), lambda m, blk: (jnp.where(m < 3, 1, 0), 0))
    send_second = (({0: 1, 2: 0}), lambda m, blk: (jnp.where(m < 2, 1, 0), 0))
    keep_second = (({1: 1, 3: 0}), lambda m, blk: (jnp.where(m < 3, 1, 0), 0))
    if split == "first":
        return [(0, half, *send_first), (0, half, *keep_first)]
    if split == "second":
        return [(0, half, *send_second), (0, half, *keep_second)]
    part = half // 2
    return [
        (0, part, *send_first),
        (0, part, *keep_first),
        (part, part, *send_second),
        (part, part, *keep_second),
    ]


def rows_back(blocks, order, splits, lefts, groups, name, after=()):
    length = lefts[0].shape[0]
    count, places = blocks.shape[0], order.shape[0]
    half = groups[0][0].rows // 2
    rows = length // places
    widths = [left.shape[1] for left in lefts]
    depth = sum(widths)
    n = len(lefts)
    arrays = [array for weights, _, _ in groups for array in weights.arrays]
    k = len(arrays)
    sides = sorted(splits)
    side = sides[0] if len(sides) == 1 else None
    plan = []
    for i, one in enumerate(sides):
        plan += [(i * half + col, *rest) for col, *rest in split_outputs(splits[one], rows, half, places)]
    whole = len(sides) * half
    pieces = max(weights.number(count, side) for weights, _, _ in groups)

    def kernel(blk, places_ref, *refs):
        left_refs, w_refs = refs[:n], refs[n : n + k]
        out_refs = refs[n + k : n + k + len(plan)]
        joined_ref, w_ref, left_sems, sems = refs[-4:]
        step = pl.program_id(0)

        def left_copies(at):
            slot, start, col, found = lax.rem(at, 2), pl.multiple_of(places_ref[at] * rows, rows), 0, []
            for i, (ref, cols) in enumerate(zip(left_refs, widths)):
                found.append(
                    pltpu.make_async_copy(
                        ref.at[pl.ds(start, rows), :],
                        joined_ref.at[slot, :, pl.ds(col, cols)],
                        left_sems.at[slot, i],
                    )
                )
                col += cols
            return found

        per_group, at, col = [], 0, 0
        for i, (weights, start, cols) in enumerate(groups):
            more = len(weights.arrays)
            per_group.append(
                weights.copies(
                    w_refs[at : at + more], blk, count, side, start, cols, w_ref.at[:, pl.ds(col, cols)], sems.at[i]
                )
            )
            at, col = at + more, col + cols

        @pl.when(step == 0)
        def _():
            for copy in left_copies(0):
                copy.start()
            for piece in per_group:
                for copy in piece:
                    copy.start()

        @pl.when(step + 1 < places)
        def _():
            for copy in left_copies(step + 1):
                copy.start()

        for copy in left_copies(step):
            copy.wait()

        @pl.when(step == 0)
        def _():
            for piece in per_group:
                for copy in piece:
                    copy.wait()

        low = dot(joined_ref[lax.rem(step, 2)], w_ref[...], NT).astype(BF)
        for (col, cols, steps, _), ref in zip(plan, out_refs):

            def store(ref=ref, col=col, cols=cols):
                ref[...] = low[:, col : col + cols]

            if len(steps) > 2:
                store()
            else:
                pl.when(functools.reduce(jnp.logical_or, [step == at for at in steps]))(store)

    def out_spec(cols, where):
        return pl.BlockSpec((rows, cols), lambda m, blk, o: where(m, blk))

    return call(
        kernel,
        name,
        2 * length * whole * depth,
        2 * length * depth + 2 * whole * depth + 2 * length * whole,
        (*lefts, *arrays),
        (places,),
        [pl.BlockSpec(memory_space=pl.ANY)] * (n + k),
        [out_spec(cols, where) for _, cols, _, where in plan],
        [struct((len(steps) * rows, cols)) for _, cols, steps, _ in plan],
        scratch=[
            pltpu.VMEM((2, rows, depth), BF),
            pltpu.VMEM((whole, depth), BF),
            pltpu.SemaphoreType.DMA((2, n)),
            pltpu.SemaphoreType.DMA((len(groups), pieces)),
        ],
        prefetch=(blocks, order),
        after=after,
    )


def gain_sums(order, split, parts, unit, after=()):
    length, width = unit.shape
    half, places = width // 2, order.shape[0]
    rows = length // places
    plan = split_outputs(split, rows, half, places)
    n = len(plan)

    def kernel(places_ref, unit_ref, *refs):
        sum_ref = refs[2 * n]
        step = pl.program_id(0)

        @pl.when(step == 0)
        def _():
            sum_ref[...] = jnp.zeros_like(sum_ref)

        for side in range(2):
            for i, (col, cols, steps, _) in enumerate(plan):

                def add(ref=refs[side * n + i], start=side * half + col, cols=cols):
                    here = slice(start, start + cols)
                    wide = ref[...].astype(F32)
                    sum_ref[0:8, here] += eight_rows(wide * unit_ref[:, here].astype(F32))
                    sum_ref[8:16, here] += eight_rows(wide)

                if len(steps) > 2:
                    add()
                else:
                    pl.when(functools.reduce(jnp.logical_or, [step == at for at in steps]))(add)

    def spec(cols, where):
        return pl.BlockSpec((rows, cols), lambda m, o: where(m, o))

    return call(
        kernel,
        "gain_sums",
        0,
        4 * length * width,
        (unit, *parts[0], *parts[1]),
        (places,),
        [pl.BlockSpec((rows, width), lambda m, o: (o[m], 0))]
        + [spec(cols, where) for _, cols, _, where in plan] * 2,
        pl.BlockSpec((16, width), lambda m, o: (0, 0)),
        struct((16, width), F32),
        prefetch=(order,),
        after=after,
    )


def turned_sums(sums):
    n = len(sums)

    def kernel(*refs):
        for ref, out_ref in zip(refs[:n], refs[n:]):
            out_ref[...] = ref[...].T.astype(F32)

    def whole(shape):
        return pl.BlockSpec(shape, lambda i: (0, 0))

    return call(
        kernel,
        "turned_sums",
        0,
        6 * sum(value.size for value in sums),
        sums,
        (1,),
        [whole(value.shape) for value in sums],
        [whole(value.shape[::-1]) for value in sums],
        [struct(value.shape[::-1], F32) for value in sums],
    )


def end_call(kernel, name, blocks, fulls, terms, vector, dtype, after):
    length, width = fulls[0].shape
    rows = min(256, length)
    n = len(fulls)
    counts = [len(part) for part in terms]

    def body(blk, *refs):
        at, parts = n, []
        for number in counts:
            total = refs[at][...].astype(F32)
            for ref in refs[at + 1 : at + number]:
                total = total + ref[...].astype(F32)
            parts.append(total)
            at += number
        count, out_ref = blocks.shape[0], refs[at + 1]
        cols = width // count
        values = [ordered(ref, blk, count, cols).astype(F32) for ref in refs[:n]]
        result = kernel(values, jnp.concatenate(parts, axis=1), refs[at][...])
        for p in range(count):
            place = pl.ds(pl.multiple_of(blk[p] * cols, cols), cols)
            out_ref[:, place] = result[:, p * cols : (p + 1) * cols].astype(dtype)

    full = pl.BlockSpec((rows, width), lambda m, blk: (m, 0))
    flat = [array for part in terms for array in part]
    return call(
        body,
        name,
        0,
        10 * length * width,
        (*fulls, *flat, vector),
        (length // rows,),
        [full] * n
        + [pl.BlockSpec((rows, array.shape[1]), lambda m, blk: (m, 0)) for array in flat]
        + [pl.BlockSpec((1, width), lambda m, blk: (0, 0))],
        full,
        struct((length, width), dtype),
        prefetch=(blocks,),
        after=after,
    )


def add_branch(blocks, x, terms, out_bias, after=()):
    return end_call(
        lambda fulls, branch, bias: fulls[0] + branch + bias, "add_branch", blocks, (x,), terms, out_bias, BF, after
    )


def norm_back(blocks, x, g, terms, gain, after=()):
    def kernel(fulls, grads, scale):
        x, g = fulls
        centered = x - jnp.mean(x, axis=1, keepdims=True)
        variance = jnp.mean(centered * centered, axis=1, keepdims=True)
        inv_std = lax.rsqrt(variance + EPSILON)
        unit = centered * inv_std
        scaled = grads * scale
        mean = jnp.mean(scaled, axis=1, keepdims=True)
        along = jnp.mean(scaled * unit, axis=1, keepdims=True)
        return g + inv_std * (scaled - mean - unit * along)

    return end_call(kernel, "norm_back", blocks, (x, g), terms, gain, F32, after)


def flip(value, axis, size, bit):
    return lax.ppermute(value, axis, [(i, i ^ bit) for i in range(size)])


def flip_sum(value, axis, size):
    bit = 1
    while bit < size:
        value = value + flip(value, axis, size, bit)
        bit *= 2
    return value


class Ring:
    def __init__(self, n_dp):
        self.size = n_dp
        self.chips = n_dp // 2

    def send(self, value, distance=1):
        pairs = [
            (z * 2 + c, ((z + distance) % self.chips) * 2 + c)
            for z in range(self.chips)
            for c in range(2)
        ]
        return lax.ppermute(value, "dp", pairs)

    def swap(self, value):
        return flip(value, "dp", self.size, 1)


def per_device(
    sizes, layer_input, ln_gain, ln_bias, out_bias, w_qkv, b_qkv, w_out, w_fc1, b_fc1, w_fc2, out_grad
):
    n_dp, n_tensor = sizes
    ring = Ring(n_dp)
    chips = ring.chips
    d_index, t_index = lax.axis_index("dp"), lax.axis_index("tensor")
    place, core = d_index // 2, d_index % 2
    steps = jnp.arange(chips, dtype=jnp.int32)
    behind = ((place - steps) % chips) * 2
    blocks = jnp.concatenate([behind + core, behind + (1 - core)]).astype(jnp.int32)
    square = n_tensor == 4

    local, width = layer_input.shape[1:]
    depth = w_qkv.shape[0]
    inner = w_qkv.shape[2]
    units = w_fc1.shape[1]
    heads = inner // HD
    length = local * n_tensor
    pairs = inner // 128

    third = ln_gain.shape[0]
    x, g = layer_input[0], out_grad[0]
    x_all = lax.all_gather(x, "tensor", axis=0, tiled=True)
    heads_own = [heads_shard(jnp.transpose(w_qkv, (1, 0, 2)), w_out)]

    vectors = jnp.stack([ln_gain, ln_bias, out_bias]).astype(F32).reshape(1, 3 * third)
    table = jnp.where(jnp.arange(n_tensor)[:, None] == t_index, vectors, 0.0)
    table = table + sum(flip(table, "tensor", n_tensor, bit) for bit in range(1, n_tensor))
    small = jnp.concatenate([table.reshape(-1), b_qkv.astype(F32).reshape(-1), b_fc1.astype(F32).reshape(-1)])
    fc1_shard, fc2_shard = stage(w_fc1, False, heads_own), stage(w_fc2, True, heads_own)
    g_placed, bias_part = order_columns(blocks, g, after=heads_own)
    heads_own.append(ring.send(heads_own[0]))
    heads_sib = [ring.swap(heads_own[0])]
    small, g_placed = tie([small, g_placed], [heads_own[1], heads_sib[0]])
    g_all = lax.all_gather(g_placed, "tensor", axis=0, tiled=True)

    heads_own.append(ring.send(heads_own[1]))
    heads_sib.append(ring.swap(heads_own[1]))
    small = jnp.where(jnp.arange(n_dp)[:, None] == d_index, small[None, :], 0.0)
    small = flip_sum(small, "dp", n_dp)
    (small,) = tie([small], [heads_own[2], heads_sib[1]])

    tables = rotary_rows(length)
    chosen = (blocks[:, None] == jnp.arange(n_dp)[None, :]).astype(F32)
    cut = n_tensor * 3 * third
    vectors = jnp.einsum("pd,dj->pj", chosen, small[:, :cut], precision=lax.Precision.HIGHEST)
    vectors = jnp.transpose(vectors.reshape(n_dp, n_tensor, 3, third), (2, 0, 1, 3))
    gain, shift, bias_out = (vectors[i].reshape(1, width) for i in range(3))
    b_width = HD // n_dp
    tail = cut + b_qkv.size
    bias_qkv = jnp.transpose(small[:, cut:tail].reshape(n_dp, 3, heads, b_width), (1, 2, 0, 3))
    bias_qkv = bias_qkv.reshape(1, 3 * inner)
    bias_fc1 = jnp.transpose(small[:, tail:].reshape(n_dp, units // HD, b_width), (1, 0, 2))
    bias_fc1 = bias_fc1.reshape(1, units)
    while len(heads_own) < chips:
        heads_own.append(ring.send(heads_own[-1]))
        heads_sib.append(ring.swap(heads_own[-2]))
    gain, bias_qkv, bias_fc1, fc1_shard, fc2_shard, *tables = tie(
        [gain, bias_qkv, bias_fc1, fc1_shard, fc2_shard, *tables], [heads_own[-1], heads_sib[-1]]
    )
    heads_sib.append(ring.swap(heads_own[-1]))
    heads_weights = Weights(heads_own + heads_sib)
    fc2_weights = Weights([lax.all_gather(fc2_shard, "dp", axis=0, tiled=True)], depth, placed=True)
    if square:
        order = (jnp.array([3, 1, 2, 0], jnp.int32) ^ t_index).astype(jnp.int32)
    else:
        order = jnp.arange(n_tensor, dtype=jnp.int32)

    def split(kind):
        return kind if square else None

    bits = {"first": [1], "second": [2], "both": [1, 2]}

    def cross_once(kind, parts):
        if not square:
            return [lax.psum_scatter(parts[0], "tensor", scatter_dimension=0, tiled=True)]
        return [flip(parts[2 * i], "tensor", 4, bit) for i, bit in enumerate(bits[kind])]

    def cross_add(parts, got):
        if not square:
            return []
        kept = parts[1::2]
        return [(k[local:].astype(F32) + r[local:].astype(F32)).astype(BF) for k, r in zip(kept, got)]

    def cross_twice(kind, sums):
        return [flip(value, "tensor", 4, 3 - bit) for value, bit in zip(sums, bits[kind])] if square else []

    def cross_terms(parts, got, last):
        if not square:
            return [got]
        return [list(terms) for terms in zip(parts[1::2], got, last)]

    fc1_own = {k: ring.send(fc1_shard, k) for k in ((1, 3) if chips == 4 else range(1, chips))}
    fc1_sib = {0: ring.swap(fc1_shard)}
    normed, unit, qkv = norm_project(
        blocks, x_all, gain, shift, bias_qkv, tables, heads_weights, after=[fc1_shard]
    )
    first = pairs // 2
    context, log_first = attend(qkv, 0, first, after=[fc1_shard])
    near = [1, 3] if chips == 4 else []
    log_first, *joined = tie([log_first, *(fc1_own[k] for k in near)], [fc1_sib[0]])
    fc1_own.update(zip(near, joined))
    if chips == 4:
        fc1_own[2] = ring.send(fc1_own[1])
    fc1_sib.update({k: ring.swap(fc1_own[k]) for k in near})
    context, log_second = attend(qkv, first, pairs - first, before=context, after=[log_first])
    far = [k for k in range(1, chips) if k not in near]
    log_second, *joined = tie([log_second, *(fc1_own[k] for k in far)], [fc1_sib[k] for k in near])
    fc1_own.update(zip(far, joined))
    fc1_sib.update({k: ring.swap(fc1_own[k]) for k in far})
    fc1_own[0] = fc1_shard
    log_total = jnp.concatenate([log_first, log_second], axis=0)
    fc1_weights = Weights([fc1[k] for fc1 in (fc1_own, fc1_sib) for k in range(chips)])
    act, slope = expand(blocks, normed, fc1_weights, bias_fc1, after=[log_second])

    def scatter(parts):
        return lax.psum_scatter(parts, "dp", scatter_dimension=0, tiled=True)

    fc2_grad, out_grads, context_grad = weight_grad(
        blocks, g_all, act, "fc2_grad", context, heads_weights
    )
    fc2_sums, out_sums = scatter(fc2_grad), scatter(out_grads)
    *backs, b_qkv_part = attend_back(qkv, context, context_grad, log_total, tables)
    heads_sib_grad, heads_own_grad = weight_grad_halves(normed, backs, inner, "heads_grad")

    def ring_add(k, moving=None):
        cut = slice(k * depth, (k + 1) * depth)
        total = heads_own_grad[cut].astype(F32) + heads_other[cut].astype(F32)
        return total if moving is None else total + moving.astype(F32)

    heads_cols, fc2_cols = (heads_weights, 0, 3 * inner), (fc2_weights, 0, units)
    out_cols, fc1_cols = (heads_weights, 3 * inner, inner), (fc1_weights, 0, units)
    lefts = [act, context]
    branch = rows_back(
        blocks, order, {0: split("first"), 1: split("second")}, lefts, [fc2_cols, out_cols], "branch",
        after=[heads_own_grad],
    )
    *branch, heads_other = tie([*branch, ring.swap(heads_sib_grad)], [])
    n = len(branch) // 2
    branch_own, branch_sib = branch[:n], branch[n:]
    message = ring_add(1).astype(BF)
    moving = ring.send(message)
    hidden_grad, b_fc1_part = hidden_back(blocks, g_all, fc2_weights, slope, after=[message])
    hidden_grad, moving = tie([hidden_grad, moving], [])
    message = ring_add(2, moving).astype(BF)
    (fc1_grad,) = weight_grad(blocks, normed, hidden_grad, "fc1_grad", after=[message])
    branch_got = cross_once("first", branch_own) + cross_once("second", branch_sib)
    n = len(branch_got)
    fc1_grad, moving, *branch_got = tie([fc1_grad, ring.send(message), *branch_got], [])
    fc1_sums = scatter(fc1_grad)
    for k in range(3, chips):
        message = ring_add(k, moving).astype(BF)
        moving = ring.send(message)
    branch_sums = cross_add(branch_own, branch_got[:1]) + cross_add(branch_sib, branch_got[1:])
    branch_last = cross_twice("first", branch_sums[:1]) + cross_twice("second", branch_sums[1:])

    lefts = [*backs, hidden_grad]
    back_own = rows_back(
        blocks, order, {0: split("both")}, lefts, [heads_cols, fc1_cols], "normed_back_half",
        after=[fc1_grad, message, *branch_sums],
    )
    n = len(back_own)
    joined = tie([*back_own, moving, *branch_last], [])
    back_own, moving, branch_last = joined[:n], joined[n], joined[n + 1 :]
    heads_sums = heads_sum(heads_own_grad, heads_other, moving)
    branch_terms = cross_terms(branch_own, branch_got[:1], branch_last[:1])
    branch_terms += cross_terms(branch_sib, branch_got[1:], branch_last[1:])
    own_got = cross_once("both", back_own)
    back_sib = rows_back(
        blocks, order, {1: split("both")}, lefts, [heads_cols, fc1_cols], "normed_back_half",
        after=[back_own[0]],
    )
    joined = tie([*back_sib, *own_got], [])
    back_sib, own_got = joined[:n], joined[n:]

    sib_got = cross_once("both", back_sib)
    own_sums = cross_add(back_own, own_got)
    own_last = cross_twice("both", own_sums)
    norm_sums = gain_sums(order, split("both"), (back_own, back_sib), unit).reshape(2, 8, n_dp, depth)
    norm_sums = jnp.einsum("pd,kpj->dkj", chosen, jnp.sum(norm_sums, axis=1), precision=lax.Precision.HIGHEST)
    b_qkv_part = jnp.sum(b_qkv_part.reshape(pairs, 3, 8, 128), axis=2)
    b_qkv_part = jnp.transpose(b_qkv_part, (1, 0, 2)).reshape(3, heads, n_dp, b_width)
    b_fc1_part = jnp.sum(b_fc1_part, axis=0).reshape(units // HD, n_dp, b_width)
    by_owner = jnp.concatenate(
        [
            norm_sums.reshape(n_dp, 2 * depth),
            bias_part[0].reshape(n_dp, depth),
            jnp.transpose(b_qkv_part, (2, 0, 1, 3)).reshape(n_dp, -1),
            jnp.transpose(b_fc1_part, (1, 0, 2)).reshape(n_dp, -1),
        ],
        axis=1,
    )

    sums = flip_sum(by_owner, "dp", n_dp)
    sums = lax.dynamic_index_in_dim(sums, d_index, 0, keepdims=False)
    w_fc2_grad, w_out_grad = turned_sums((fc2_sums, out_sums))
    sums, *sib_got = tie([sums, *sib_got], [w_fc2_grad, *own_sums])
    sib_sums = cross_add(back_sib, sib_got)
    sib_last = cross_twice("both", sib_sums)
    layer_output = add_branch(blocks, x, branch_terms, bias_out, after=[*sib_sums, *back_sib[:1]])
    w_fc1_grad = fc1_sums.astype(F32)
    (sums,) = tie([sums], [layer_output, heads_sums, w_fc1_grad])
    mine = sums[: 3 * depth].reshape(3, depth)
    mine = mine + sum(flip(mine, "tensor", n_tensor, bit) for bit in range(1, n_tensor))
    mine = lax.dynamic_slice_in_dim(mine, t_index * third, third, 1)
    b_qkv_grad = sums[3 * depth : 3 * depth + b_qkv.size].reshape(b_qkv.shape)
    b_fc1_grad = sums[3 * depth + b_qkv.size :].reshape(b_fc1.shape)
    w_qkv_grad = jnp.transpose(heads_sums, (1, 0, 2))
    back_terms = cross_terms(back_own, own_got, own_last) + cross_terms(back_sib, sib_got, sib_last)
    input_grad = norm_back(blocks, x, g, back_terms, gain, after=[sums])
    return (
        layer_output[None],
        input_grad[None],
        mine[0],
        mine[1],
        mine[2],
        w_qkv_grad,
        b_qkv_grad,
        w_out_grad,
        w_fc1_grad,
        b_fc1_grad,
        w_fc2_grad,
    )


def solution(mesh):
    in_specs = (
        P("dp", "tensor", None),
        P(("dp", "tensor")),
        P(("dp", "tensor")),
        P(("dp", "tensor")),
        P("dp", None, "tensor"),
        P(None, "tensor", "dp"),
        P("tensor", "dp"),
        P("dp", "tensor"),
        P("tensor", "dp"),
        P("tensor", "dp"),
        P("dp", "tensor", None),
    )
    out_specs = (
        P("dp", "tensor", None),
        P("dp", "tensor", None),
        P(("dp", "tensor")),
        P(("dp", "tensor")),
        P(("dp", "tensor")),
        P("dp", None, "tensor"),
        P(None, "tensor", "dp"),
        P("tensor", "dp"),
        P("dp", "tensor"),
        P("tensor", "dp"),
        P("tensor", "dp"),
    )
    sizes = (mesh.shape["dp"], mesh.shape["tensor"])
    return jax.shard_map(
        functools.partial(per_device, sizes),
        mesh=mesh,
        in_specs=in_specs,
        out_specs=out_specs,
        check_vma=False,
    )
```

```python
import functools
import math

import jax
import jax.numpy as jnp
from jax import lax
from jax.experimental import pallas as pl
from jax.experimental.pallas import tpu as pltpu
from jax.sharding import PartitionSpec as P

HD = 64
ROT = 32
EPSILON = 1e-05
NEG = -1e30
LOG2E = math.log2(math.e)
BF = jnp.bfloat16
F32 = jnp.float32
VMEM_BYTES = 56 << 20

NN = (((1,), (0,)), ((), ()))
NT = (((1,), (1,)), ((), ()))
TN = (((0,), (0,)), ((), ()))


def dot(a, b, dims):
    return lax.dot_general(a, b, dims, preferred_element_type=F32)


def eight_rows(value):
    rows, cols = value.shape
    return jnp.sum(value.reshape(rows // 8, 8, cols), axis=0)


def call(kernel, name, flops, moved, operands, grid, in_specs, out_specs, out_shape, scratch=(), prefetch=(), aliases=None, after=()):
    front = len(prefetch) + len(in_specs)

    def body(*refs):
        kernel(*refs[:front], *refs[front + len(after) :])

    return pl.pallas_call(
        body,
        name=name,
        grid_spec=pltpu.PrefetchScalarGridSpec(
            num_scalar_prefetch=len(prefetch),
            grid=grid,
            in_specs=list(in_specs) + [pl.BlockSpec(memory_space=pl.ANY)] * len(after),
            out_specs=out_specs,
            scratch_shapes=list(scratch),
        ),
        out_shape=out_shape,
        input_output_aliases=aliases or {},
        compiler_params=pltpu.CompilerParams(vmem_limit_bytes=VMEM_BYTES),
        cost_estimate=pl.CostEstimate(flops=int(flops), bytes_accessed=int(moved), transcendentals=0),
    )(*prefetch, *operands, *after)


class Weights:
    def __init__(self, arrays, size=None, placed=False):
        self.arrays = list(arrays)
        self.placed = placed
        self.cols = self.arrays[0].shape[1]
        self.size = size or self.arrays[0].shape[0]
        self.rows = self.arrays[0].shape[0] if placed else self.size * len(self.arrays)

    def copies(self, refs, blk, count, side, col, cols, target, sems):
        found = []

        def add(source, start, size, place):
            found.append(
                pltpu.make_async_copy(
                    source.at[pl.ds(start, size), pl.ds(col, cols)],
                    target.at[pl.ds(place, size), :],
                    sems.at[len(found)],
                )
            )

        half = self.rows // 2
        if self.placed:
            size = self.rows // count
            first, last = (0, count) if side is None else (side * count // 2, (side + 1) * count // 2)
            for p in range(first, last):
                add(refs[0], pl.multiple_of(blk[p] * size, size), size, (p - first) * size)
            return found
        place = 0
        for ref in refs:
            size = self.size
            if side is None or place // half == side:
                add(ref, 0, size, place - (side or 0) * half)
            place += size
        return found

    def number(self, count, side=None):
        total = count if self.placed else len(self.arrays)
        return total if side is None else total // 2


def struct(shape, dtype=BF):
    return jax.ShapeDtypeStruct(shape, dtype)


def tie(values, after):
    n = len(values)
    anywhere = pl.BlockSpec(memory_space=pltpu.HBM)

    def kernel(*refs):
        del refs

    return pl.pallas_call(
        kernel,
        name="tie",
        in_specs=[anywhere] * (n + len(after)),
        out_specs=[anywhere] * n,
        out_shape=[struct(v.shape, v.dtype) for v in values],
        input_output_aliases={i: i for i in range(n)},
    )(*values, *after)


def order_columns(blocks, x, after=()):
    rows, width = x.shape
    count = blocks.shape[0]
    cols = width // count
    step_rows = min(256, rows)

    def kernel(blk, x_ref, out_ref, sum_ref):
        for p in range(count):
            place = pl.ds(pl.multiple_of(blk[p] * cols, cols), cols)
            out_ref[:, p * cols : (p + 1) * cols] = x_ref[:, place]

        @pl.when(pl.program_id(0) == 0)
        def _():
            sum_ref[...] = jnp.zeros_like(sum_ref)

        sum_ref[0:1, :] += jnp.sum(x_ref[...].astype(F32), axis=0, keepdims=True)

    block = pl.BlockSpec((step_rows, width), lambda m, blk: (m, 0))
    return call(
        kernel,
        "order_columns",
        0,
        4 * rows * width,
        (x,),
        (rows // step_rows,),
        [block],
        [block, pl.BlockSpec((8, width), lambda m, blk: (0, 0))],
        [struct(x.shape), struct((8, width), F32)],
        prefetch=(blocks,),
        after=after,
    )


def heads_shard(w_qkv, w_out):
    _, depth, inner = w_qkv.shape

    def kernel(q_ref, o_ref, out_ref):
        for part in range(3):
            out_ref[:, part * inner : (part + 1) * inner] = q_ref[part]
        out_ref[:, 3 * inner :] = o_ref[...].T

    return call(
        kernel,
        "heads_shard",
        0,
        16 * depth * inner,
        (w_qkv, w_out),
        (1,),
        [
            pl.BlockSpec(w_qkv.shape, lambda i: (0, 0, 0)),
            pl.BlockSpec(w_out.shape, lambda i: (0, 0)),
        ],
        pl.BlockSpec((depth, 4 * inner), lambda i: (0, 0)),
        struct((depth, 4 * inner)),
    )


def heads_sum(own, other, moving):
    depth, wide = moving.shape
    inner = wide // 3
    rows = min(64, depth)

    def kernel(own_ref, other_ref, moving_ref, out_ref):
        total = own_ref[...].astype(F32) + other_ref[...].astype(F32) + moving_ref[...].astype(F32)
        for part in range(3):
            out_ref[part] = total[:, part * inner : (part + 1) * inner]

    block = pl.BlockSpec((rows, wide), lambda m: (m, 0))
    return call(
        kernel,
        "heads_sum",
        0,
        10 * depth * wide,
        (own, other, moving),
        (depth // rows,),
        [block] * 3,
        pl.BlockSpec((3, rows, inner), lambda m: (0, m, 0)),
        struct((3, depth, inner), F32),
    )


def stage(weight, flip, after, rows=None):
    start, count = rows or (0, weight.shape[0])
    taken = (count, weight.shape[1])
    shape = taken[::-1] if flip else taken

    def kernel(w_ref, out_ref):
        out_ref[...] = w_ref[...].T if flip else w_ref[...]

    return call(
        kernel,
        "stage_weight",
        0,
        4 * taken[0] * taken[1],
        (weight,),
        (1,),
        [pl.BlockSpec(taken, lambda i: (start // count, 0))],
        pl.BlockSpec(shape, lambda i: (0, 0)),
        struct(shape),
        after=after,
    )


def rotary_rows(length):
    lane = jnp.arange(128, dtype=jnp.int32)[None, :] % HD
    half = ROT // 2
    frequency = 10000.0 ** (-2.0 * (lane % half).astype(F32) / ROT)
    angles = jnp.arange(length, dtype=F32)[:, None] * frequency
    cosine, sine = jnp.cos(angles), jnp.sin(angles)
    keep = jnp.where(lane < ROT, cosine, 1.0)
    ahead = jnp.where(lane < half, -sine, 0.0)
    behind = jnp.where((lane >= half) & (lane < ROT), sine, 0.0)
    return keep, ahead, behind


def turn(u, keep, ahead, behind):
    return u * keep + pltpu.roll(u, 128 - ROT // 2, 1) * ahead + pltpu.roll(u, ROT // 2, 1) * behind


def ordered(ref, blk, count, cols):
    return jnp.concatenate(
        [ref[:, pl.ds(pl.multiple_of(blk[p] * cols, cols), cols)] for p in range(count)], axis=1
    )


def norm_project(blocks, x_all, gain, shift, bias, tables, weights, after=()):
    length, width = x_all.shape
    wide = bias.shape[1]
    inner = wide // 3
    rows = min(512, length)
    k, count = len(weights.arrays), blocks.shape[0]

    def kernel(blk, x_ref, gain_ref, shift_ref, bias_ref, keep_ref, ahead_ref, behind_ref, *refs):
        w_refs = refs[:k]
        normed_ref, unit_ref, qkv_ref, w_ref, sems = refs[k:]
        step = pl.program_id(0)
        copies = weights.copies(w_refs, blk, count, None, 0, wide, w_ref, sems)

        @pl.when(step == 0)
        def _():
            for copy in copies:
                copy.start()

        x = ordered(x_ref, blk, count, width // count).astype(F32)
        centered = x - jnp.mean(x, axis=1, keepdims=True)
        variance = jnp.mean(centered * centered, axis=1, keepdims=True)
        unit = centered * lax.rsqrt(variance + EPSILON)
        unit_ref[...] = unit.astype(BF)
        normed_ref[...] = (unit * gain_ref[...] + shift_ref[...]).astype(BF)

        @pl.when(step == 0)
        def _():
            for copy in copies:
                copy.wait()

        merged = dot(normed_ref[...], w_ref[...], NN) + bias_ref[...]
        for start in range(0, wide, 128):
            u = merged[:, start : start + 128]
            if start < 2 * inner:
                u = turn(u, keep_ref[...], ahead_ref[...], behind_ref[...])
            qkv_ref[:, start : start + 128] = u.astype(BF)

    def whole(shape):
        return pl.BlockSpec(shape, lambda j, blk: (0, 0))

    def block(cols):
        return pl.BlockSpec((rows, cols), lambda j, blk: (j, 0))

    return call(
        kernel,
        "norm_project",
        0,
        0,
        (x_all, gain, shift, bias, *tables, *weights.arrays),
        (length // rows,),
        [block(width), whole((1, width)), whole((1, width)), whole((1, wide))]
        + [block(128)] * 3
        + [pl.BlockSpec(memory_space=pl.ANY)] * k,
        [block(width), block(width), block(wide)],
        [struct((length, width)), struct((length, width)), struct((length, wide))],
        scratch=[pltpu.VMEM((width, wide), BF), pltpu.SemaphoreType.DMA((weights.number(count),))],
        prefetch=(blocks,),
        after=after,
    )


def attend(qkv, first, number, before=None, after=()):
    length = qkv.shape[0]
    inner = qkv.shape[1] // 3
    pairs = inner // 128
    block = min(1024, length)
    count = length // block
    scale = LOG2E / math.sqrt(HD)
    n = 0 if before is None else 1

    def kernel(q_ref, k_ref, v_ref, *refs):
        o_ref, lse_ref, turned_ref = refs[n:]
        lane = lax.broadcasted_iota(jnp.int32, (1, 128), 1)

        @pl.when(pl.program_id(1) == 0)
        def _():
            turned_ref[...] = v_ref[...].T

        for index in range(count):

            @pl.when(pl.program_id(1) == index)
            def _(index=index):
                queries = q_ref[...]
                blank = jnp.zeros_like(queries)
                end = (index + 1) * block
                found = []
                for head in range(2):
                    mine = (lane < HD) if head == 0 else (lane >= HD)
                    scores = dot(k_ref[:end, :], jnp.where(mine, queries, blank), NT)
                    row = lax.broadcasted_iota(jnp.int32, (block, block), 0)
                    col = lax.broadcasted_iota(jnp.int32, (block, block), 1)
                    last = jnp.where(row <= col, scores[end - block :], NEG)
                    if index:
                        scores = jnp.concatenate([scores[: end - block], last], axis=0)
                    else:
                        scores = last
                    top = jnp.max(scores, axis=0, keepdims=True)
                    weights = jnp.exp2((scores - top) * scale)
                    total = jnp.sum(weights, axis=0, keepdims=True)
                    out = dot(turned_ref[head * HD : (head + 1) * HD, :end], weights.astype(BF), NN)
                    found.append(out / total)
                    lse_ref[0, head : head + 1, :] = top * scale + jnp.log2(total)
                o_ref[...] = jnp.concatenate(found, axis=0).T.astype(BF)

    return call(
        kernel,
        "attend",
        0,
        0,
        (qkv, qkv, qkv) + ((before,) if n else ()),
        (number, count),
        [
            pl.BlockSpec((block, 128), lambda h, i: (i, first + h)),
            pl.BlockSpec((length, 128), lambda h, i: (0, pairs + first + h)),
            pl.BlockSpec((length, 128), lambda h, i: (0, 2 * pairs + first + h)),
        ]
        + [pl.BlockSpec(memory_space=pl.ANY)] * n,
        [
            pl.BlockSpec((block, 128), lambda h, i: (i, first + h)),
            pl.BlockSpec((1, 2, block), lambda h, i: (h, 0, i)),
        ],
        [struct((length, inner)), struct((number, 2, length), F32)],
        scratch=[pltpu.VMEM((128, length), BF)],
        aliases={3: 0} if n else {},
        after=after,
    )


def attend_back(qkv, context, context_grad, log_total, tables, after=()):
    length = qkv.shape[0]
    inner = qkv.shape[1] // 3
    pairs = inner // 128
    block = min(512, length)
    count = length // block
    scale = LOG2E / math.sqrt(HD)
    shrink = 1.0 / math.sqrt(HD)

    def kernel(q_ref, k_ref, v_ref, o_ref, do_ref, lse_ref, keep_ref, ahead_ref, behind_ref, *rest):
        dq_ref, dk_ref, dv_ref, sum_ref, k_total, v_total = rest
        step = pl.program_id(1)
        lane = lax.broadcasted_iota(jnp.int32, (1, 128), 1)

        @pl.when(step == 0)
        def _():
            k_total[...] = jnp.zeros_like(k_total)
            v_total[...] = jnp.zeros_like(v_total)
            sum_ref[...] = jnp.zeros_like(sum_ref)

        def turn_back(u, rows):
            return turn(u, keep_ref[rows, :], -ahead_ref[rows, :], -behind_ref[rows, :])

        for index in range(count):

            @pl.when(step == index)
            def _(index=index):
                queries, grads = q_ref[...], do_ref[...]
                blank = jnp.zeros_like(queries)
                queries_turned, grads_turned = queries.T, grads.T
                products = grads.astype(F32) * o_ref[...].astype(F32)
                log_totals = lse_ref[0].T
                q_total = [None, None]
                for other in range(index + 1):
                    rows = slice(other * block, (other + 1) * block)
                    keys, values = k_ref[rows, :], v_ref[rows, :]
                    for head in range(2):
                        mine = (lane < HD) if head == 0 else (lane >= HD)
                        here = slice(head * HD, (head + 1) * HD)
                        delta = jnp.sum(products[:, here], axis=1, keepdims=True)
                        scores = dot(jnp.where(mine, queries, blank), keys, NT)
                        if other == index:
                            row = lax.broadcasted_iota(jnp.int32, (block, block), 0)
                            col = lax.broadcasted_iota(jnp.int32, (block, block), 1)
                            scores = jnp.where(col <= row, scores, NEG)
                        probs = jnp.exp2(scores * scale - log_totals[:, head : head + 1])
                        probs_grad = dot(jnp.where(mine, grads, blank), values, NT)
                        score_grad = (probs * (probs_grad - delta)).astype(BF)
                        v_total[here, rows] += dot(grads_turned[here, :], probs.astype(BF), NN)
                        k_total[here, rows] += dot(queries_turned[here, :], score_grad, NN)
                        term = dot(score_grad, keys, NN)
                        q_total[head] = term if other == 0 else q_total[head] + term
                dq = jnp.where(lane < HD, q_total[0], q_total[1]) * shrink
                rows = slice(index * block, (index + 1) * block)
                dq = turn_back(dq, rows).astype(BF)
                dq_ref[...] = dq
                sum_ref[0, 0:8, :] += eight_rows(dq.astype(F32))

        @pl.when(step == count - 1)
        def _():
            for index in range(count):
                rows = slice(index * block, (index + 1) * block)
                dk = turn_back(k_total[:, rows].T * shrink, rows).astype(BF)
                dk_ref[rows, :] = dk
                sum_ref[0, 8:16, :] += eight_rows(dk.astype(F32))
                dv = v_total[:, rows].T.astype(BF)
                dv_ref[rows, :] = dv
                sum_ref[0, 16:24, :] += eight_rows(dv.astype(F32))

    def column(offset):
        return pl.BlockSpec((length, 128), lambda h, i: (0, offset + h))

    def rows_of(offset):
        return pl.BlockSpec((block, 128), lambda h, i: (i, offset + h))

    table = pl.BlockSpec((length, 128), lambda h, i: (0, 0))
    return call(
        kernel,
        "attend_back",
        60 * length * length * inner,
        16 * length * inner,
        (qkv, qkv, qkv, context, context_grad, log_total, *tables),
        (pairs, count),
        [
            rows_of(0),
            column(pairs),
            column(2 * pairs),
            rows_of(0),
            rows_of(0),
            pl.BlockSpec((1, 2, block), lambda h, i: (h, 0, i)),
            table,
            table,
            table,
        ],
        [rows_of(0), column(0), column(0), pl.BlockSpec((1, 24, 128), lambda h, i: (h, 0, 0))],
        [struct((length, inner))] * 3 + [struct((pairs, 24, 128), F32)],
        scratch=[pltpu.VMEM((128, length), F32)] * 2,
        after=after,
    )


def times_weights(blocks, rows_in, weights, name, extra, outs, finish, after=()):
    length, width = rows_in.shape
    total_cols = weights.cols
    rows, cols = min(512, length), min(1024, total_cols)
    chunks = total_cols // cols
    k, count, e = len(weights.arrays), blocks.shape[0], len(extra)
    number = weights.number(count)

    def kernel(blk, a_ref, *refs):
        w_refs, extra_refs, out_refs = refs[:k], refs[k : k + e], refs[k + e : -2]
        w_ref, sems = refs[-2:]
        chunk, step = pl.program_id(0), pl.program_id(1)
        copies = [
            weights.copies(w_refs, blk, count, None, c * cols, cols, w_ref.at[c], sems.at[c])
            for c in range(chunks)
        ]

        @pl.when((chunk == 0) & (step == 0))
        def _():
            for per_chunk in copies:
                for copy in per_chunk:
                    copy.start()

        for c in range(chunks):

            @pl.when((chunk == c) & (step == 0))
            def _(c=c):
                for copy in copies[c]:
                    copy.wait()

        finish(dot(a_ref[...], w_ref[chunk], NN), step == 0, extra_refs, out_refs)

    specs = {
        "block": pl.BlockSpec((rows, cols), lambda n, m, blk: (m, n)),
        "row": pl.BlockSpec((1, cols), lambda n, m, blk: (0, n)),
        "sum": pl.BlockSpec((8, cols), lambda n, m, blk: (0, n)),
    }
    shapes = {"block": struct((length, total_cols)), "sum": struct((8, total_cols), F32)}
    return call(
        kernel,
        name,
        2 * length * width * total_cols,
        2 * length * width + 2 * width * total_cols + 4 * length * total_cols,
        (rows_in, *weights.arrays, *(value for _, value in extra)),
        (chunks, length // rows),
        [pl.BlockSpec((rows, width), lambda n, m, blk: (m, 0))]
        + [pl.BlockSpec(memory_space=pl.ANY)] * k
        + [specs[kind] for kind, _ in extra],
        [specs[kind] for kind in outs],
        [shapes[kind] for kind in outs],
        scratch=[
            pltpu.VMEM((chunks, width, cols), BF),
            pltpu.SemaphoreType.DMA((chunks, number)),
        ],
        prefetch=(blocks,),
        after=after,
    )


def expand(blocks, normed, weights, bias, after=()):
    def finish(product, first, extra_refs, out_refs):
        hidden = product + extra_refs[0][...]
        c = math.sqrt(2.0 / math.pi)
        square = hidden * hidden
        inner = hidden * (c + (c * 0.044715) * square)
        gate = 0.5 + 0.5 * jnp.tanh(inner)
        act = hidden * gate
        out_refs[0][...] = act.astype(BF)
        out_refs[1][...] = (
            gate + act * (1.0 - gate) * (2.0 * c + (6.0 * c * 0.044715) * square)
        ).astype(BF)

    return times_weights(
        blocks, normed, weights, "expand", [("row", bias)], ["block", "block"], finish, after
    )


def hidden_back(blocks, g_all, weights, slope, after=()):
    def finish(product, first, extra_refs, out_refs):
        grad = product * extra_refs[0][...].astype(F32)
        out_refs[0][...] = grad.astype(BF)

        @pl.when(first)
        def _():
            out_refs[1][...] = jnp.zeros_like(out_refs[1])

        out_refs[1][...] += eight_rows(grad)

    return times_weights(
        blocks, g_all, weights, "hidden_back", [("block", slope)], ["block", "sum"], finish, after
    )


def columns_of(rights, cols):
    starts, total = [], 0
    for right in rights:
        starts.append(total)
        total += right.shape[1] // cols
    return starts + [total]


def weight_grad(blocks, rows_in, right, name, more=None, weights=None, after=()):
    length, width = rows_in.shape
    half = width // 2
    count = blocks.shape[0]
    depth = width // count
    cols = min(1024, right.shape[1])
    total = right.shape[1] // cols
    k = len(weights.arrays) if weights else 0
    extra = 2 if k else 0

    def kernel(blk, a_ref, right_ref, *refs):
        chunk, side = pl.program_id(0), pl.program_id(1)

        def product(ref, target):
            low = dot(a_ref[...], ref[...], TN).astype(BF)
            for p in range(count // 2):
                place = pl.multiple_of(blk[side * (count // 2) + p] * depth, depth)
                target[pl.ds(place, depth), :] = low[p * depth : (p + 1) * depth]

        if not k:
            product(right_ref, refs[0])
            return
        more_ref, w_refs, inner = refs[0], refs[1 : 1 + k], more.shape[1]
        out_ref, more_out_ref, back_ref, w_ref, sum_ref, sems = refs[1 + k :]
        copies = weights.copies(w_refs, blk, count, None, weights.cols - inner, inner, w_ref, sems)

        @pl.when((chunk == 0) & (side == 0))
        def _():
            for copy in copies:
                copy.start()

        pl.when(chunk < total)(lambda: product(right_ref, out_ref))
        pl.when(chunk == total)(lambda: product(more_ref, more_out_ref))

        @pl.when((chunk == total + 1) & (side == 0))
        def _():
            for copy in copies:
                copy.wait()
            sum_ref[...] = dot(a_ref[...], w_ref[:half, :], NN)

        @pl.when((chunk == total + 1) & (side == 1))
        def _():
            back_ref[...] = (sum_ref[...] + dot(a_ref[...], w_ref[half:, :], NN)).astype(BF)

    def whole(shape):
        return pl.BlockSpec(shape, lambda n, s, blk: (0, 0))

    in_specs = [
        pl.BlockSpec((length, half), lambda n, s, blk: (0, s)),
        pl.BlockSpec((length, cols), lambda n, s, blk: (0, jnp.minimum(n, total - 1))),
    ]
    out_specs = [pl.BlockSpec((width, cols), lambda n, s, blk: (0, jnp.minimum(n, total - 1)))]
    out_shape = [struct((width, right.shape[1]))]
    scratch = []
    if k:
        inner = more.shape[1]
        in_specs += [whole((length, inner))] + [pl.BlockSpec(memory_space=pl.ANY)] * k
        out_specs += [whole((width, inner)), whole((length, inner))]
        out_shape += [struct((width, inner)), struct((length, inner))]
        scratch = [
            pltpu.VMEM((width, inner), BF),
            pltpu.VMEM((length, inner), F32),
            pltpu.SemaphoreType.DMA((weights.number(count),)),
        ]
    return call(
        kernel,
        name,
        2 * length * width * right.shape[1],
        2 * length * width + 4 * length * right.shape[1] + 2 * width * right.shape[1],
        (rows_in, right, *((more, *weights.arrays) if k else ())),
        (total + extra, 2),
        in_specs,
        out_specs,
        out_shape,
        scratch=scratch,
        prefetch=(blocks,),
        after=after,
    )


def weight_grad_halves(rows_in, rights, cols, name, after=()):
    length, width = rows_in.shape
    half = width // 2
    starts = columns_of(rights, cols)
    n, total = len(rights), starts[-1]

    def kernel(a_ref, *refs):
        sib_ref, own_ref = refs[n:]
        side, chunk = pl.program_id(0), pl.program_id(1)
        for i in range(n):

            @pl.when((chunk >= starts[i]) & (chunk < starts[i + 1]))
            def _(i=i):
                product = dot(a_ref[...], refs[i][...], TN).astype(BF)

                @pl.when(side == 0)
                def _():
                    sib_ref[...] = product

                @pl.when(side == 1)
                def _():
                    own_ref[...] = product

    def right_spec(i):
        number = starts[i + 1] - starts[i]
        return pl.BlockSpec((length, cols), lambda s, n: (0, jnp.clip(n - starts[i], 0, number - 1)))

    return call(
        kernel,
        name,
        2 * length * width * total * cols,
        2 * length * width + 4 * length * total * cols + 2 * width * total * cols,
        (rows_in, *rights),
        (2, total),
        [pl.BlockSpec((length, half), lambda s, n: (0, 1 - s))] + [right_spec(i) for i in range(n)],
        [
            pl.BlockSpec((half, cols), lambda s, n: (0, jnp.where(s == 0, n, total - 1))),
            pl.BlockSpec((half, cols), lambda s, n: (0, jnp.where(s == 0, 0, n))),
        ],
        [struct((half, total * cols))] * 2,
        after=after,
    )


def split_outputs(split, rows, half, count):
    if split is None:
        return [(0, half, {m: m for m in range(count)}, lambda m, blk: (m, 0))]
    send_first = (({0: 1, 1: 0}), lambda m, blk: (jnp.where(m < 1, 1, 0), 0))
    keep_first = (({2: 1, 3: 0}), lambda m, blk: (jnp.where(m < 3, 1, 0), 0))
    send_second = (({0: 1, 2: 0}), lambda m, blk: (jnp.where(m < 2, 1, 0), 0))
    keep_second = (({1: 1, 3: 0}), lambda m, blk: (jnp.where(m < 3, 1, 0), 0))
    if split == "first":
        return [(0, half, *send_first), (0, half, *keep_first)]
    if split == "second":
        return [(0, half, *send_second), (0, half, *keep_second)]
    part = half // 2
    return [
        (0, part, *send_first),
        (0, part, *keep_first),
        (part, part, *send_second),
        (part, part, *keep_second),
    ]


def rows_back(blocks, order, splits, lefts, groups, name, after=()):
    length = lefts[0].shape[0]
    count, places = blocks.shape[0], order.shape[0]
    half = groups[0][0].rows // 2
    rows = length // places
    widths = [left.shape[1] for left in lefts]
    depth = sum(widths)
    n = len(lefts)
    arrays = [array for weights, _, _ in groups for array in weights.arrays]
    k = len(arrays)
    sides = sorted(splits)
    side = sides[0] if len(sides) == 1 else None
    plan = []
    for i, one in enumerate(sides):
        plan += [(i * half + col, *rest) for col, *rest in split_outputs(splits[one], rows, half, places)]
    whole = len(sides) * half
    pieces = max(weights.number(count, side) for weights, _, _ in groups)

    def kernel(blk, places_ref, *refs):
        left_refs, w_refs = refs[:n], refs[n : n + k]
        out_refs = refs[n + k : n + k + len(plan)]
        joined_ref, w_ref, left_sems, sems = refs[-4:]
        step = pl.program_id(0)

        def left_copies(at):
            slot, start, col, found = lax.rem(at, 2), pl.multiple_of(places_ref[at] * rows, rows), 0, []
            for i, (ref, cols) in enumerate(zip(left_refs, widths)):
                found.append(
                    pltpu.make_async_copy(
                        ref.at[pl.ds(start, rows), :],
                        joined_ref.at[slot, :, pl.ds(col, cols)],
                        left_sems.at[slot, i],
                    )
                )
                col += cols
            return found

        per_group, at, col = [], 0, 0
        for i, (weights, start, cols) in enumerate(groups):
            more = len(weights.arrays)
            per_group.append(
                weights.copies(
                    w_refs[at : at + more], blk, count, side, start, cols, w_ref.at[:, pl.ds(col, cols)], sems.at[i]
                )
            )
            at, col = at + more, col + cols

        @pl.when(step == 0)
        def _():
            for copy in left_copies(0):
                copy.start()
            for piece in per_group:
                for copy in piece:
                    copy.start()

        @pl.when(step + 1 < places)
        def _():
            for copy in left_copies(step + 1):
                copy.start()

        for copy in left_copies(step):
            copy.wait()

        @pl.when(step == 0)
        def _():
            for piece in per_group:
                for copy in piece:
                    copy.wait()

        low = dot(joined_ref[lax.rem(step, 2)], w_ref[...], NT).astype(BF)
        for (col, cols, steps, _), ref in zip(plan, out_refs):

            def store(ref=ref, col=col, cols=cols):
                ref[...] = low[:, col : col + cols]

            if len(steps) > 2:
                store()
            else:
                pl.when(functools.reduce(jnp.logical_or, [step == at for at in steps]))(store)

    def out_spec(cols, where):
        return pl.BlockSpec((rows, cols), lambda m, blk, o: where(m, blk))

    return call(
        kernel,
        name,
        2 * length * whole * depth,
        2 * length * depth + 2 * whole * depth + 2 * length * whole,
        (*lefts, *arrays),
        (places,),
        [pl.BlockSpec(memory_space=pl.ANY)] * (n + k),
        [out_spec(cols, where) for _, cols, _, where in plan],
        [struct((len(steps) * rows, cols)) for _, cols, steps, _ in plan],
        scratch=[
            pltpu.VMEM((2, rows, depth), BF),
            pltpu.VMEM((whole, depth), BF),
            pltpu.SemaphoreType.DMA((2, n)),
            pltpu.SemaphoreType.DMA((len(groups), pieces)),
        ],
        prefetch=(blocks, order),
        after=after,
    )


def gain_sums(order, split, parts, unit, side):
    length, width = unit.shape
    half, places = width // 2, order.shape[0]
    rows = length // places
    plan = split_outputs(split, rows, half, places)
    n = len(plan)

    def kernel(places_ref, unit_ref, *refs):
        sum_ref = refs[n]
        step = pl.program_id(0)

        @pl.when(step == 0)
        def _():
            sum_ref[...] = jnp.zeros_like(sum_ref)

        for (col, cols, steps, _), ref in zip(plan, refs):

            def add(ref=ref, here=slice(col, col + cols)):
                wide = ref[...].astype(F32)
                sum_ref[0:8, here] += eight_rows(wide * unit_ref[:, here].astype(F32))
                sum_ref[8:16, here] += eight_rows(wide)

            if len(steps) > 2:
                add()
            else:
                pl.when(functools.reduce(jnp.logical_or, [step == at for at in steps]))(add)

    def spec(cols, where):
        return pl.BlockSpec((rows, cols), lambda m, o: where(m, o))

    return call(
        kernel,
        "gain_sums",
        0,
        2 * length * width,
        (unit, *parts),
        (places,),
        [pl.BlockSpec((rows, half), lambda m, o: (o[m], side))]
        + [spec(cols, where) for _, cols, _, where in plan],
        pl.BlockSpec((16, half), lambda m, o: (0, 0)),
        struct((16, half), F32),
        prefetch=(order,),
    )


def turned_sums(sums):
    n = len(sums)

    def kernel(*refs):
        for ref, out_ref in zip(refs[:n], refs[n:]):
            out_ref[...] = ref[...].T.astype(F32)

    def whole(shape):
        return pl.BlockSpec(shape, lambda i: (0, 0))

    return call(
        kernel,
        "turned_sums",
        0,
        6 * sum(value.size for value in sums),
        sums,
        (1,),
        [whole(value.shape) for value in sums],
        [whole(value.shape[::-1]) for value in sums],
        [struct(value.shape[::-1], F32) for value in sums],
    )


def end_call(kernel, name, blocks, fulls, terms, vector, dtype, after):
    length, width = fulls[0].shape
    rows = min(256, length)
    n = len(fulls)
    counts = [len(part) for part in terms]

    def body(blk, *refs):
        at, parts = n, []
        for number in counts:
            total = refs[at][...].astype(F32)
            for ref in refs[at + 1 : at + number]:
                total = total + ref[...].astype(F32)
            parts.append(total)
            at += number
        count, out_ref = blocks.shape[0], refs[at + 1]
        cols = width // count
        values = [ordered(ref, blk, count, cols).astype(F32) for ref in refs[:n]]
        result = kernel(values, jnp.concatenate(parts, axis=1), refs[at][...])
        for p in range(count):
            place = pl.ds(pl.multiple_of(blk[p] * cols, cols), cols)
            out_ref[:, place] = result[:, p * cols : (p + 1) * cols].astype(dtype)

    full = pl.BlockSpec((rows, width), lambda m, blk: (m, 0))
    flat = [array for part in terms for array in part]
    return call(
        body,
        name,
        0,
        10 * length * width,
        (*fulls, *flat, vector),
        (length // rows,),
        [full] * n
        + [pl.BlockSpec((rows, array.shape[1]), lambda m, blk: (m, 0)) for array in flat]
        + [pl.BlockSpec((1, width), lambda m, blk: (0, 0))],
        full,
        struct((length, width), dtype),
        prefetch=(blocks,),
        after=after,
    )


def add_branch(blocks, x, terms, out_bias, after=()):
    return end_call(
        lambda fulls, branch, bias: fulls[0] + branch + bias, "add_branch", blocks, (x,), terms, out_bias, BF, after
    )


def norm_back(blocks, x, g, terms, gain, after=()):
    def kernel(fulls, grads, scale):
        x, g = fulls
        centered = x - jnp.mean(x, axis=1, keepdims=True)
        variance = jnp.mean(centered * centered, axis=1, keepdims=True)
        inv_std = lax.rsqrt(variance + EPSILON)
        unit = centered * inv_std
        scaled = grads * scale
        mean = jnp.mean(scaled, axis=1, keepdims=True)
        along = jnp.mean(scaled * unit, axis=1, keepdims=True)
        return g + inv_std * (scaled - mean - unit * along)

    return end_call(kernel, "norm_back", blocks, (x, g), terms, gain, F32, after)


def flip(value, axis, size, bit):
    return lax.ppermute(value, axis, [(i, i ^ bit) for i in range(size)])


def flip_sum(value, axis, size):
    bit = 1
    while bit < size:
        value = value + flip(value, axis, size, bit)
        bit *= 2
    return value


class Ring:
    def __init__(self, n_dp):
        self.size = n_dp
        self.chips = n_dp // 2

    def send(self, value, distance=1):
        pairs = [
            (z * 2 + c, ((z + distance) % self.chips) * 2 + c)
            for z in range(self.chips)
            for c in range(2)
        ]
        return lax.ppermute(value, "dp", pairs)

    def swap(self, value):
        return flip(value, "dp", self.size, 1)


def per_device(
    sizes, layer_input, ln_gain, ln_bias, out_bias, w_qkv, b_qkv, w_out, w_fc1, b_fc1, w_fc2, out_grad
):
    n_dp, n_tensor = sizes
    ring = Ring(n_dp)
    chips = ring.chips
    d_index, t_index = lax.axis_index("dp"), lax.axis_index("tensor")
    place, core = d_index // 2, d_index % 2
    steps = jnp.arange(chips, dtype=jnp.int32)
    behind = ((place - steps) % chips) * 2
    blocks = jnp.concatenate([behind + core, behind + (1 - core)]).astype(jnp.int32)
    square = n_tensor == 4

    local, width = layer_input.shape[1:]
    depth = w_qkv.shape[0]
    inner = w_qkv.shape[2]
    units = w_fc1.shape[1]
    heads = inner // HD
    length = local * n_tensor
    pairs = inner // 128

    third = ln_gain.shape[0]
    x, g = layer_input[0], out_grad[0]
    x_all = lax.all_gather(x, "tensor", axis=0, tiled=True)
    heads_own = [heads_shard(jnp.transpose(w_qkv, (1, 0, 2)), w_out)]

    vectors = jnp.stack([ln_gain, ln_bias, out_bias]).astype(F32).reshape(1, 3 * third)
    table = jnp.where(jnp.arange(n_tensor)[:, None] == t_index, vectors, 0.0)
    table = table + sum(flip(table, "tensor", n_tensor, bit) for bit in range(1, n_tensor))
    small = jnp.concatenate([table.reshape(-1), b_qkv.astype(F32).reshape(-1), b_fc1.astype(F32).reshape(-1)])
    fc1_shard, fc2_shard = stage(w_fc1, False, heads_own), stage(w_fc2, True, heads_own)
    g_placed, bias_part = order_columns(blocks, g, after=heads_own)
    heads_own.append(ring.send(heads_own[0]))
    heads_sib = [ring.swap(heads_own[0])]
    small, g_placed = tie([small, g_placed], [heads_own[1], heads_sib[0]])
    g_all = lax.all_gather(g_placed, "tensor", axis=0, tiled=True)

    heads_own.append(ring.send(heads_own[1]))
    heads_sib.append(ring.swap(heads_own[1]))
    small = jnp.where(jnp.arange(n_dp)[:, None] == d_index, small[None, :], 0.0)
    small = flip_sum(small, "dp", n_dp)
    tables = rotary_rows(length)
    (small,) = tie([small], [heads_own[2], heads_sib[1], *tables])

    chosen = (blocks[:, None] == jnp.arange(n_dp)[None, :]).astype(F32)
    cut = n_tensor * 3 * third
    vectors = jnp.einsum("pd,dj->pj", chosen, small[:, :cut], precision=lax.Precision.HIGHEST)
    vectors = jnp.transpose(vectors.reshape(n_dp, n_tensor, 3, third), (2, 0, 1, 3))
    gain, shift, bias_out = (vectors[i].reshape(1, width) for i in range(3))
    b_width = HD // n_dp
    tail = cut + b_qkv.size
    bias_qkv = jnp.transpose(small[:, cut:tail].reshape(n_dp, 3, heads, b_width), (1, 2, 0, 3))
    bias_qkv = bias_qkv.reshape(1, 3 * inner)
    bias_fc1 = jnp.transpose(small[:, tail:].reshape(n_dp, units // HD, b_width), (1, 0, 2))
    bias_fc1 = bias_fc1.reshape(1, units)
    while len(heads_own) < chips:
        heads_own.append(ring.send(heads_own[-1]))
        heads_sib.append(ring.swap(heads_own[-2]))
    fc1_shard, fc2_shard = tie(
        [fc1_shard, fc2_shard], [heads_own[-1], heads_sib[-1], gain, bias_qkv, bias_fc1]
    )
    heads_sib.append(ring.swap(heads_own[-1]))
    heads_weights = Weights(heads_own + heads_sib)
    fc2_weights = Weights([lax.all_gather(fc2_shard, "dp", axis=0, tiled=True)], depth, placed=True)
    if square:
        order = (jnp.array([3, 1, 2, 0], jnp.int32) ^ t_index).astype(jnp.int32)
    else:
        order = jnp.arange(n_tensor, dtype=jnp.int32)

    def split(kind):
        return kind if square else None

    bits = {"first": [1], "second": [2], "both": [1, 2]}

    def cross_once(kind, parts):
        if not square:
            return [lax.psum_scatter(parts[0], "tensor", scatter_dimension=0, tiled=True)]
        return [flip(parts[2 * i], "tensor", 4, bit) for i, bit in enumerate(bits[kind])]

    def cross_add(parts, got):
        if not square:
            return []
        kept = parts[1::2]
        return [(k[local:].astype(F32) + r[local:].astype(F32)).astype(BF) for k, r in zip(kept, got)]

    def cross_twice(kind, sums):
        return [flip(value, "tensor", 4, 3 - bit) for value, bit in zip(sums, bits[kind])] if square else []

    def cross_terms(parts, got, last):
        if not square:
            return [got]
        return [list(terms) for terms in zip(parts[1::2], got, last)]

    fc1_own = {k: ring.send(fc1_shard, k) for k in ((1, 3) if chips == 4 else range(1, chips))}
    fc1_sib = {0: ring.swap(fc1_shard)}
    normed, unit, qkv = norm_project(
        blocks, x_all, gain, shift, bias_qkv, tables, heads_weights, after=[fc1_shard]
    )
    first = pairs // 2
    context, log_first = attend(qkv, 0, first, after=[fc1_shard])
    near = [1, 3] if chips == 4 else []
    log_first, *joined = tie([log_first, *(fc1_own[k] for k in near)], [fc1_sib[0]])
    fc1_own.update(zip(near, joined))
    if chips == 4:
        fc1_own[2] = ring.send(fc1_own[1])
    fc1_sib.update({k: ring.swap(fc1_own[k]) for k in near})
    context, log_second = attend(qkv, first, pairs - first, before=context, after=[log_first])
    far = [k for k in range(1, chips) if k not in near]
    log_second, *joined = tie([log_second, *(fc1_own[k] for k in far)], [fc1_sib[k] for k in near])
    fc1_own.update(zip(far, joined))
    fc1_sib.update({k: ring.swap(fc1_own[k]) for k in far})
    fc1_own[0] = fc1_shard
    log_total = jnp.concatenate([log_first, log_second], axis=0)
    fc1_weights = Weights([fc1[k] for fc1 in (fc1_own, fc1_sib) for k in range(chips)])
    act, slope = expand(blocks, normed, fc1_weights, bias_fc1, after=[log_second])

    def scatter(parts):
        return lax.psum_scatter(parts, "dp", scatter_dimension=0, tiled=True)

    fc2_grad, out_grads, context_grad = weight_grad(
        blocks, g_all, act, "fc2_grad", context, heads_weights
    )
    fc2_sums, out_sums = scatter(fc2_grad), scatter(out_grads)
    *backs, b_qkv_part = attend_back(qkv, context, context_grad, log_total, tables)
    heads_sib_grad, heads_own_grad = weight_grad_halves(normed, backs, inner, "heads_grad")

    def ring_add(k, moving=None):
        cut = slice(k * depth, (k + 1) * depth)
        total = heads_own_grad[cut].astype(F32) + heads_other[cut].astype(F32)
        return total if moving is None else total + moving.astype(F32)

    heads_cols, fc2_cols = (heads_weights, 0, 3 * inner), (fc2_weights, 0, units)
    out_cols, fc1_cols = (heads_weights, 3 * inner, inner), (fc1_weights, 0, units)
    lefts = [act, context]
    branch = rows_back(
        blocks, order, {0: split("first"), 1: split("second")}, lefts, [fc2_cols, out_cols], "branch",
        after=[heads_own_grad],
    )
    *branch, heads_other = tie([*branch, ring.swap(heads_sib_grad)], [])
    n = len(branch) // 2
    branch_own, branch_sib = branch[:n], branch[n:]
    message = ring_add(1).astype(BF)
    moving = ring.send(message)
    hidden_grad, b_fc1_part = hidden_back(blocks, g_all, fc2_weights, slope, after=[message])
    hidden_grad, moving = tie([hidden_grad, moving], [])
    message = ring_add(2, moving).astype(BF)
    (fc1_grad,) = weight_grad(blocks, normed, hidden_grad, "fc1_grad", after=[message])
    branch_got = cross_once("first", branch_own) + cross_once("second", branch_sib)
    n = len(branch_got)
    fc1_grad, moving, *branch_got = tie([fc1_grad, ring.send(message), *branch_got], [])
    fc1_sums = scatter(fc1_grad)
    for k in range(3, chips):
        message = ring_add(k, moving).astype(BF)
        moving = ring.send(message)
    branch_sums = cross_add(branch_own, branch_got[:1]) + cross_add(branch_sib, branch_got[1:])
    branch_last = cross_twice("first", branch_sums[:1]) + cross_twice("second", branch_sums[1:])

    lefts = [*backs, hidden_grad]
    back_own = rows_back(
        blocks, order, {0: split("both")}, lefts, [heads_cols, fc1_cols], "normed_back_half",
        after=[fc1_grad, message, *branch_sums],
    )
    n = len(back_own)
    sums_own = gain_sums(order, split("both"), back_own, unit, 0)
    joined = tie([*back_own, moving, *branch_last], [sums_own])
    back_own, moving, branch_last = joined[:n], joined[n], joined[n + 1 :]
    heads_sums = heads_sum(heads_own_grad, heads_other, moving)
    branch_terms = cross_terms(branch_own, branch_got[:1], branch_last[:1])
    branch_terms += cross_terms(branch_sib, branch_got[1:], branch_last[1:])
    own_got = cross_once("both", back_own)
    back_sib = rows_back(
        blocks, order, {1: split("both")}, lefts, [heads_cols, fc1_cols], "normed_back_half",
        after=[back_own[0]],
    )
    joined = tie([*back_sib, *own_got], [])
    back_sib, own_got = joined[:n], joined[n:]

    sib_got = cross_once("both", back_sib)
    own_sums = cross_add(back_own, own_got)
    own_last = cross_twice("both", own_sums)
    norm_sums = [sums_own, gain_sums(order, split("both"), back_sib, unit, 1)]
    norm_sums = jnp.concatenate(norm_sums, axis=1).reshape(2, 8, n_dp, depth)
    norm_sums = jnp.einsum("pd,kpj->dkj", chosen, jnp.sum(norm_sums, axis=1), precision=lax.Precision.HIGHEST)
    b_qkv_part = jnp.sum(b_qkv_part.reshape(pairs, 3, 8, 128), axis=2)
    b_qkv_part = jnp.transpose(b_qkv_part, (1, 0, 2)).reshape(3, heads, n_dp, b_width)
    b_fc1_part = jnp.sum(b_fc1_part, axis=0).reshape(units // HD, n_dp, b_width)
    by_owner = jnp.concatenate(
        [
            norm_sums.reshape(n_dp, 2 * depth),
            bias_part[0].reshape(n_dp, depth),
            jnp.transpose(b_qkv_part, (2, 0, 1, 3)).reshape(n_dp, -1),
            jnp.transpose(b_fc1_part, (1, 0, 2)).reshape(n_dp, -1),
        ],
        axis=1,
    )

    sums = flip_sum(by_owner, "dp", n_dp)
    sums = lax.dynamic_index_in_dim(sums, d_index, 0, keepdims=False)
    w_fc2_grad, w_out_grad = turned_sums((fc2_sums, out_sums))
    sums, *sib_got = tie([sums, *sib_got], [heads_sums, *own_sums])
    sib_sums = cross_add(back_sib, sib_got)
    sib_last = cross_twice("both", sib_sums)
    layer_output = add_branch(blocks, x, branch_terms, bias_out, after=[*sib_sums, *back_sib[:1]])
    w_fc1_grad = fc1_sums.astype(F32)
    (sums,) = tie([sums], [layer_output, w_fc2_grad, w_fc1_grad])
    mine = sums[: 3 * depth].reshape(3, depth)
    mine = flip_sum(mine, "tensor", n_tensor)
    mine = lax.dynamic_slice_in_dim(mine, t_index * third, third, 1)
    b_qkv_grad = sums[3 * depth : 3 * depth + b_qkv.size].reshape(b_qkv.shape)
    b_fc1_grad = sums[3 * depth + b_qkv.size :].reshape(b_fc1.shape)
    w_qkv_grad = jnp.transpose(heads_sums, (1, 0, 2))
    back_terms = cross_terms(back_own, own_got, own_last) + cross_terms(back_sib, sib_got, sib_last)
    input_grad = norm_back(blocks, x, g, back_terms, gain, after=[sums])
    return (
        layer_output[None],
        input_grad[None],
        mine[0],
        mine[1],
        mine[2],
        w_qkv_grad,
        b_qkv_grad,
        w_out_grad,
        w_fc1_grad,
        b_fc1_grad,
        w_fc2_grad,
    )


def solution(mesh):
    in_specs = (
        P("dp", "tensor", None),
        P(("dp", "tensor")),
        P(("dp", "tensor")),
        P(("dp", "tensor")),
        P("dp", None, "tensor"),
        P(None, "tensor", "dp"),
        P("tensor", "dp"),
        P("dp", "tensor"),
        P("tensor", "dp"),
        P("tensor", "dp"),
        P("dp", "tensor", None),
    )
    out_specs = (
        P("dp", "tensor", None),
        P("dp", "tensor", None),
        P(("dp", "tensor")),
        P(("dp", "tensor")),
        P(("dp", "tensor")),
        P("dp", None, "tensor"),
        P(None, "tensor", "dp"),
        P("tensor", "dp"),
        P("dp", "tensor"),
        P("tensor", "dp"),
        P("tensor", "dp"),
    )
    sizes = (mesh.shape["dp"], mesh.shape["tensor"])
    return jax.shard_map(
        functools.partial(per_device, sizes),
        mesh=mesh,
        in_specs=in_specs,
        out_specs=out_specs,
        check_vma=False,
    )
```

```python
import functools
import math

import jax
import jax.numpy as jnp
from jax import lax
from jax.experimental import pallas as pl
from jax.experimental.pallas import tpu as pltpu
from jax.sharding import PartitionSpec as P

HD = 64
ROT = 32
EPSILON = 1e-05
NEG = -1e30
LOG2E = math.log2(math.e)
BF = jnp.bfloat16
F32 = jnp.float32
VMEM_BYTES = 56 << 20

NN = (((1,), (0,)), ((), ()))
NT = (((1,), (1,)), ((), ()))
TN = (((0,), (0,)), ((), ()))


def dot(a, b, dims):
    return lax.dot_general(a, b, dims, preferred_element_type=F32)


def eight_rows(value):
    rows, cols = value.shape
    return jnp.sum(value.reshape(rows // 8, 8, cols), axis=0)


def call(kernel, name, flops, moved, operands, grid, in_specs, out_specs, out_shape, scratch=(), prefetch=(), aliases=None, after=()):
    front = len(prefetch) + len(in_specs)

    def body(*refs):
        kernel(*refs[:front], *refs[front + len(after) :])

    return pl.pallas_call(
        body,
        name=name,
        grid_spec=pltpu.PrefetchScalarGridSpec(
            num_scalar_prefetch=len(prefetch),
            grid=grid,
            in_specs=list(in_specs) + [pl.BlockSpec(memory_space=pl.ANY)] * len(after),
            out_specs=out_specs,
            scratch_shapes=list(scratch),
        ),
        out_shape=out_shape,
        input_output_aliases=aliases or {},
        compiler_params=pltpu.CompilerParams(vmem_limit_bytes=VMEM_BYTES),
        cost_estimate=pl.CostEstimate(flops=int(flops), bytes_accessed=int(moved), transcendentals=0),
    )(*prefetch, *operands, *after)


class Weights:
    def __init__(self, arrays, size=None, placed=False):
        self.arrays = list(arrays)
        self.placed = placed
        self.cols = self.arrays[0].shape[1]
        self.size = size or self.arrays[0].shape[0]
        self.rows = self.arrays[0].shape[0] if placed else self.size * len(self.arrays)

    def copies(self, refs, blk, count, side, col, cols, target, sems):
        found = []

        def add(source, start, size, place):
            found.append(
                pltpu.make_async_copy(
                    source.at[pl.ds(start, size), pl.ds(col, cols)],
                    target.at[pl.ds(place, size), :],
                    sems.at[len(found)],
                )
            )

        half = self.rows // 2
        if self.placed:
            size = self.rows // count
            first, last = (0, count) if side is None else (side * count // 2, (side + 1) * count // 2)
            for p in range(first, last):
                add(refs[0], pl.multiple_of(blk[p] * size, size), size, (p - first) * size)
            return found
        place = 0
        for ref in refs:
            size = self.size
            if side is None or place // half == side:
                add(ref, 0, size, place - (side or 0) * half)
            place += size
        return found

    def number(self, count, side=None):
        total = count if self.placed else len(self.arrays)
        return total if side is None else total // 2


def struct(shape, dtype=BF):
    return jax.ShapeDtypeStruct(shape, dtype)


def tie(values, after):
    n = len(values)
    anywhere = pl.BlockSpec(memory_space=pltpu.HBM)

    def kernel(*refs):
        del refs

    return pl.pallas_call(
        kernel,
        name="tie",
        in_specs=[anywhere] * (n + len(after)),
        out_specs=[anywhere] * n,
        out_shape=[struct(v.shape, v.dtype) for v in values],
        input_output_aliases={i: i for i in range(n)},
    )(*values, *after)


def order_columns(blocks, x, after=()):
    rows, width = x.shape
    count = blocks.shape[0]
    cols = width // count
    step_rows = min(256, rows)

    def kernel(blk, x_ref, out_ref, sum_ref):
        for p in range(count):
            place = pl.ds(pl.multiple_of(blk[p] * cols, cols), cols)
            out_ref[:, p * cols : (p + 1) * cols] = x_ref[:, place]

        @pl.when(pl.program_id(0) == 0)
        def _():
            sum_ref[...] = jnp.zeros_like(sum_ref)

        sum_ref[0:1, :] += jnp.sum(x_ref[...].astype(F32), axis=0, keepdims=True)

    block = pl.BlockSpec((step_rows, width), lambda m, blk: (m, 0))
    return call(
        kernel,
        "order_columns",
        0,
        4 * rows * width,
        (x,),
        (rows // step_rows,),
        [block],
        [block, pl.BlockSpec((8, width), lambda m, blk: (0, 0))],
        [struct(x.shape), struct((8, width), F32)],
        prefetch=(blocks,),
        after=after,
    )


def heads_shard(w_qkv, w_out):
    _, depth, inner = w_qkv.shape

    def kernel(q_ref, o_ref, out_ref):
        for part in range(3):
            out_ref[:, part * inner : (part + 1) * inner] = q_ref[part]
        out_ref[:, 3 * inner :] = o_ref[...].T

    return call(
        kernel,
        "heads_shard",
        0,
        16 * depth * inner,
        (w_qkv, w_out),
        (1,),
        [
            pl.BlockSpec(w_qkv.shape, lambda i: (0, 0, 0)),
            pl.BlockSpec(w_out.shape, lambda i: (0, 0)),
        ],
        pl.BlockSpec((depth, 4 * inner), lambda i: (0, 0)),
        struct((depth, 4 * inner)),
    )


def heads_sum(sums):
    depth, wide = sums.shape
    inner = wide // 3

    def kernel(sums_ref, out_ref):
        for part in range(3):
            out_ref[part] = sums_ref[:, part * inner : (part + 1) * inner].astype(F32)

    return call(
        kernel,
        "heads_sum",
        0,
        6 * depth * wide,
        (sums,),
        (1,),
        [pl.BlockSpec((depth, wide), lambda m: (0, 0))],
        pl.BlockSpec((3, depth, inner), lambda m: (0, 0, 0)),
        struct((3, depth, inner), F32),
    )


def stage(weight, flip, after, rows=None):
    start, count = rows or (0, weight.shape[0])
    taken = (count, weight.shape[1])
    shape = taken[::-1] if flip else taken

    def kernel(w_ref, out_ref):
        out_ref[...] = w_ref[...].T if flip else w_ref[...]

    return call(
        kernel,
        "stage_weight",
        0,
        4 * taken[0] * taken[1],
        (weight,),
        (1,),
        [pl.BlockSpec(taken, lambda i: (start // count, 0))],
        pl.BlockSpec(shape, lambda i: (0, 0)),
        struct(shape),
        after=after,
    )


def rotary_rows(length):
    lane = jnp.arange(128, dtype=jnp.int32)[None, :] % HD
    half = ROT // 2
    frequency = 10000.0 ** (-2.0 * (lane % half).astype(F32) / ROT)
    angles = jnp.arange(length, dtype=F32)[:, None] * frequency
    cosine, sine = jnp.cos(angles), jnp.sin(angles)
    keep = jnp.where(lane < ROT, cosine, 1.0)
    ahead = jnp.where(lane < half, -sine, 0.0)
    behind = jnp.where((lane >= half) & (lane < ROT), sine, 0.0)
    return keep, ahead, behind


def turn(u, keep, ahead, behind):
    return u * keep + pltpu.roll(u, 128 - ROT // 2, 1) * ahead + pltpu.roll(u, ROT // 2, 1) * behind


def ordered(ref, blk, count, cols):
    return jnp.concatenate(
        [ref[:, pl.ds(pl.multiple_of(blk[p] * cols, cols), cols)] for p in range(count)], axis=1
    )


def norm_project(blocks, x_all, gain, shift, bias, tables, weights, after=()):
    length, width = x_all.shape
    wide = bias.shape[1]
    inner = wide // 3
    rows = min(512, length)
    k, count = len(weights.arrays), blocks.shape[0]

    def kernel(blk, x_ref, gain_ref, shift_ref, bias_ref, keep_ref, ahead_ref, behind_ref, *refs):
        w_refs = refs[:k]
        normed_ref, unit_ref, qkv_ref, w_ref, sems = refs[k:]
        step = pl.program_id(0)
        copies = weights.copies(w_refs, blk, count, None, 0, wide, w_ref, sems)

        @pl.when(step == 0)
        def _():
            for copy in copies:
                copy.start()

        x = ordered(x_ref, blk, count, width // count).astype(F32)
        centered = x - jnp.mean(x, axis=1, keepdims=True)
        variance = jnp.mean(centered * centered, axis=1, keepdims=True)
        unit = centered * lax.rsqrt(variance + EPSILON)
        unit_ref[...] = unit.astype(BF)
        normed_ref[...] = (unit * gain_ref[...] + shift_ref[...]).astype(BF)

        @pl.when(step == 0)
        def _():
            for copy in copies:
                copy.wait()

        merged = dot(normed_ref[...], w_ref[...], NN) + bias_ref[...]
        for start in range(0, wide, 128):
            u = merged[:, start : start + 128]
            if start < 2 * inner:
                u = turn(u, keep_ref[...], ahead_ref[...], behind_ref[...])
            qkv_ref[:, start : start + 128] = u.astype(BF)

    def whole(shape):
        return pl.BlockSpec(shape, lambda j, blk: (0, 0))

    def block(cols):
        return pl.BlockSpec((rows, cols), lambda j, blk: (j, 0))

    return call(
        kernel,
        "norm_project",
        0,
        0,
        (x_all, gain, shift, bias, *tables, *weights.arrays),
        (length // rows,),
        [block(width), whole((1, width)), whole((1, width)), whole((1, wide))]
        + [block(128)] * 3
        + [pl.BlockSpec(memory_space=pl.ANY)] * k,
        [block(width), block(width), block(wide)],
        [struct((length, width)), struct((length, width)), struct((length, wide))],
        scratch=[pltpu.VMEM((width, wide), BF), pltpu.SemaphoreType.DMA((weights.number(count),))],
        prefetch=(blocks,),
        after=after,
    )


def attend(qkv, first, number, before=None, after=()):
    length = qkv.shape[0]
    inner = qkv.shape[1] // 3
    pairs = inner // 128
    block = min(1024, length)
    count = length // block
    scale = LOG2E / math.sqrt(HD)
    n = 0 if before is None else 1

    def kernel(q_ref, k_ref, v_ref, *refs):
        o_ref, lse_ref, turned_ref = refs[n:]
        lane = lax.broadcasted_iota(jnp.int32, (1, 128), 1)

        @pl.when(pl.program_id(1) == 0)
        def _():
            turned_ref[...] = v_ref[...].T

        for index in range(count):

            @pl.when(pl.program_id(1) == index)
            def _(index=index):
                queries = q_ref[...]
                blank = jnp.zeros_like(queries)
                end = (index + 1) * block
                found = []
                for head in range(2):
                    mine = (lane < HD) if head == 0 else (lane >= HD)
                    scores = dot(k_ref[:end, :], jnp.where(mine, queries, blank), NT)
                    row = lax.broadcasted_iota(jnp.int32, (block, block), 0)
                    col = lax.broadcasted_iota(jnp.int32, (block, block), 1)
                    last = jnp.where(row <= col, scores[end - block :], NEG)
                    if index:
                        scores = jnp.concatenate([scores[: end - block], last], axis=0)
                    else:
                        scores = last
                    top = jnp.max(scores, axis=0, keepdims=True)
                    weights = jnp.exp2((scores - top) * scale)
                    total = jnp.sum(weights, axis=0, keepdims=True)
                    out = dot(turned_ref[head * HD : (head + 1) * HD, :end], weights.astype(BF), NN)
                    found.append(out / total)
                    lse_ref[0, head : head + 1, :] = top * scale + jnp.log2(total)
                o_ref[...] = jnp.concatenate(found, axis=0).T.astype(BF)

    return call(
        kernel,
        "attend",
        0,
        0,
        (qkv, qkv, qkv) + ((before,) if n else ()),
        (number, count),
        [
            pl.BlockSpec((block, 128), lambda h, i: (i, first + h)),
            pl.BlockSpec((length, 128), lambda h, i: (0, pairs + first + h)),
            pl.BlockSpec((length, 128), lambda h, i: (0, 2 * pairs + first + h)),
        ]
        + [pl.BlockSpec(memory_space=pl.ANY)] * n,
        [
            pl.BlockSpec((block, 128), lambda h, i: (i, first + h)),
            pl.BlockSpec((1, 2, block), lambda h, i: (h, 0, i)),
        ],
        [struct((length, inner)), struct((number, 2, length), F32)],
        scratch=[pltpu.VMEM((128, length), BF)],
        aliases={3: 0} if n else {},
        after=after,
    )


def attend_back(qkv, context, context_grad, log_total, tables, after=()):
    length = qkv.shape[0]
    inner = qkv.shape[1] // 3
    pairs = inner // 128
    block = min(512, length)
    count = length // block
    scale = LOG2E / math.sqrt(HD)
    shrink = 1.0 / math.sqrt(HD)

    def kernel(q_ref, k_ref, v_ref, o_ref, do_ref, lse_ref, keep_ref, ahead_ref, behind_ref, *rest):
        dq_ref, dk_ref, dv_ref, sum_ref, k_total, v_total = rest
        step = pl.program_id(1)
        lane = lax.broadcasted_iota(jnp.int32, (1, 128), 1)

        @pl.when(step == 0)
        def _():
            k_total[...] = jnp.zeros_like(k_total)
            v_total[...] = jnp.zeros_like(v_total)
            sum_ref[...] = jnp.zeros_like(sum_ref)

        def turn_back(u, rows):
            return turn(u, keep_ref[rows, :], -ahead_ref[rows, :], -behind_ref[rows, :])

        for index in range(count):

            @pl.when(step == index)
            def _(index=index):
                queries, grads = q_ref[...], do_ref[...]
                blank = jnp.zeros_like(queries)
                queries_turned, grads_turned = queries.T, grads.T
                products = grads.astype(F32) * o_ref[...].astype(F32)
                log_totals = lse_ref[0].T
                q_total = [None, None]
                for other in range(index + 1):
                    rows = slice(other * block, (other + 1) * block)
                    keys, values = k_ref[rows, :], v_ref[rows, :]
                    for head in range(2):
                        mine = (lane < HD) if head == 0 else (lane >= HD)
                        here = slice(head * HD, (head + 1) * HD)
                        delta = jnp.sum(products[:, here], axis=1, keepdims=True)
                        scores = dot(jnp.where(mine, queries, blank), keys, NT)
                        if other == index:
                            row = lax.broadcasted_iota(jnp.int32, (block, block), 0)
                            col = lax.broadcasted_iota(jnp.int32, (block, block), 1)
                            scores = jnp.where(col <= row, scores, NEG)
                        probs = jnp.exp2(scores * scale - log_totals[:, head : head + 1])
                        probs_grad = dot(jnp.where(mine, grads, blank), values, NT)
                        score_grad = (probs * (probs_grad - delta)).astype(BF)
                        v_total[here, rows] += dot(grads_turned[here, :], probs.astype(BF), NN)
                        k_total[here, rows] += dot(queries_turned[here, :], score_grad, NN)
                        term = dot(score_grad, keys, NN)
                        q_total[head] = term if other == 0 else q_total[head] + term
                dq = jnp.where(lane < HD, q_total[0], q_total[1]) * shrink
                rows = slice(index * block, (index + 1) * block)
                dq = turn_back(dq, rows).astype(BF)
                dq_ref[...] = dq
                sum_ref[0, 0:8, :] += eight_rows(dq.astype(F32))

        @pl.when(step == count - 1)
        def _():
            for index in range(count):
                rows = slice(index * block, (index + 1) * block)
                dk = turn_back(k_total[:, rows].T * shrink, rows).astype(BF)
                dk_ref[rows, :] = dk
                sum_ref[0, 8:16, :] += eight_rows(dk.astype(F32))
                dv = v_total[:, rows].T.astype(BF)
                dv_ref[rows, :] = dv
                sum_ref[0, 16:24, :] += eight_rows(dv.astype(F32))

    def column(offset):
        return pl.BlockSpec((length, 128), lambda h, i: (0, offset + h))

    def rows_of(offset):
        return pl.BlockSpec((block, 128), lambda h, i: (i, offset + h))

    table = pl.BlockSpec((length, 128), lambda h, i: (0, 0))
    return call(
        kernel,
        "attend_back",
        60 * length * length * inner,
        16 * length * inner,
        (qkv, qkv, qkv, context, context_grad, log_total, *tables),
        (pairs, count),
        [
            rows_of(0),
            column(pairs),
            column(2 * pairs),
            rows_of(0),
            rows_of(0),
            pl.BlockSpec((1, 2, block), lambda h, i: (h, 0, i)),
            table,
            table,
            table,
        ],
        [rows_of(0), column(0), column(0), pl.BlockSpec((1, 24, 128), lambda h, i: (h, 0, 0))],
        [struct((length, inner))] * 3 + [struct((pairs, 24, 128), F32)],
        scratch=[pltpu.VMEM((128, length), F32)] * 2,
        after=after,
    )


def times_weights(blocks, rows_in, weights, name, extra, outs, finish, after=()):
    length, width = rows_in.shape
    total_cols = weights.cols
    rows, cols = min(512, length), min(1024, total_cols)
    chunks = total_cols // cols
    k, count, e = len(weights.arrays), blocks.shape[0], len(extra)
    number = weights.number(count)

    def kernel(blk, a_ref, *refs):
        w_refs, extra_refs, out_refs = refs[:k], refs[k : k + e], refs[k + e : -2]
        w_ref, sems = refs[-2:]
        chunk, step = pl.program_id(0), pl.program_id(1)
        copies = [
            weights.copies(w_refs, blk, count, None, c * cols, cols, w_ref.at[c], sems.at[c])
            for c in range(chunks)
        ]

        @pl.when((chunk == 0) & (step == 0))
        def _():
            for per_chunk in copies:
                for copy in per_chunk:
                    copy.start()

        for c in range(chunks):

            @pl.when((chunk == c) & (step == 0))
            def _(c=c):
                for copy in copies[c]:
                    copy.wait()

        finish(dot(a_ref[...], w_ref[chunk], NN), step == 0, extra_refs, out_refs)

    specs = {
        "block": pl.BlockSpec((rows, cols), lambda n, m, blk: (m, n)),
        "row": pl.BlockSpec((1, cols), lambda n, m, blk: (0, n)),
        "sum": pl.BlockSpec((8, cols), lambda n, m, blk: (0, n)),
    }
    shapes = {"block": struct((length, total_cols)), "sum": struct((8, total_cols), F32)}
    return call(
        kernel,
        name,
        2 * length * width * total_cols,
        2 * length * width + 2 * width * total_cols + 4 * length * total_cols,
        (rows_in, *weights.arrays, *(value for _, value in extra)),
        (chunks, length // rows),
        [pl.BlockSpec((rows, width), lambda n, m, blk: (m, 0))]
        + [pl.BlockSpec(memory_space=pl.ANY)] * k
        + [specs[kind] for kind, _ in extra],
        [specs[kind] for kind in outs],
        [shapes[kind] for kind in outs],
        scratch=[
            pltpu.VMEM((chunks, width, cols), BF),
            pltpu.SemaphoreType.DMA((chunks, number)),
        ],
        prefetch=(blocks,),
        after=after,
    )


def expand(blocks, normed, weights, bias, after=()):
    def finish(product, first, extra_refs, out_refs):
        hidden = product + extra_refs[0][...]
        c = math.sqrt(2.0 / math.pi)
        square = hidden * hidden
        inner = hidden * (c + (c * 0.044715) * square)
        gate = 0.5 + 0.5 * jnp.tanh(inner)
        act = hidden * gate
        out_refs[0][...] = act.astype(BF)
        out_refs[1][...] = (
            gate + act * (1.0 - gate) * (2.0 * c + (6.0 * c * 0.044715) * square)
        ).astype(BF)

    return times_weights(
        blocks, normed, weights, "expand", [("row", bias)], ["block", "block"], finish, after
    )


def hidden_back(blocks, g_all, weights, slope, after=()):
    def finish(product, first, extra_refs, out_refs):
        grad = product * extra_refs[0][...].astype(F32)
        out_refs[0][...] = grad.astype(BF)

        @pl.when(first)
        def _():
            out_refs[1][...] = jnp.zeros_like(out_refs[1])

        out_refs[1][...] += eight_rows(grad)

    return times_weights(
        blocks, g_all, weights, "hidden_back", [("block", slope)], ["block", "sum"], finish, after
    )


def columns_of(rights, cols):
    starts, total = [], 0
    for right in rights:
        starts.append(total)
        total += right.shape[1] // cols
    return starts + [total]


def columns_of(rights, cols):
    starts, total = [], 0
    for right in rights:
        starts.append(total)
        total += right.shape[1] // cols
    return starts + [total]


def weight_grad(blocks, rows_in, rights, cols, name, weights=None, after=()):
    length, width = rows_in.shape
    half = width // 2
    count = blocks.shape[0]
    depth = width // count
    starts = columns_of(rights, cols)
    n, total = len(rights), starts[-1]
    k = len(weights.arrays) if weights else 0
    more = 1 if k else 0

    def kernel(blk, a_ref, *refs):
        w_refs, out_ref = refs[n : n + k], refs[n + k]
        chunk, side = pl.program_id(0), pl.program_id(1)
        if more:
            back_ref, w_ref, sum_ref, sems = refs[n + k + 1 :]
            inner = w_ref.shape[1]
            copies = weights.copies(w_refs, blk, count, None, 3 * inner, inner, w_ref, sems)

            @pl.when((chunk == 0) & (side == 0))
            def _():
                for copy in copies:
                    copy.start()

            @pl.when((chunk == total) & (side == 0))
            def _():
                for copy in copies:
                    copy.wait()
                sum_ref[...] = dot(a_ref[...], w_ref[:half, :], NN)

            @pl.when((chunk == total) & (side == 1))
            def _():
                back_ref[...] = (sum_ref[...] + dot(a_ref[...], w_ref[half:, :], NN)).astype(BF)

        for i in range(n):

            @pl.when((chunk >= starts[i]) & (chunk < starts[i + 1]))
            def _(i=i):
                product = dot(a_ref[...], refs[i][...], TN).astype(BF)
                for p in range(count // 2):
                    place = pl.multiple_of(blk[side * (count // 2) + p] * depth, depth)
                    out_ref[pl.ds(place, depth), :] = product[p * depth : (p + 1) * depth]

    def right_spec(i):
        number = starts[i + 1] - starts[i]
        return pl.BlockSpec(
            (length, cols), lambda n, s, blk: (0, jnp.clip(n - starts[i], 0, number - 1))
        )

    out_specs = [pl.BlockSpec((width, cols), lambda n, s, blk: (0, jnp.minimum(n, total - 1)))]
    out_shape = [struct((width, total * cols))]
    scratch = []
    if more:
        inner = weights.cols // 4
        out_specs.append(pl.BlockSpec((length, inner), lambda n, s, blk: (0, 0)))
        out_shape.append(struct((length, inner)))
        scratch = [
            pltpu.VMEM((width, inner), BF),
            pltpu.VMEM((length, inner), F32),
            pltpu.SemaphoreType.DMA((weights.number(count),)),
        ]
    return call(
        kernel,
        name,
        2 * length * width * total * cols,
        2 * length * width + 4 * length * total * cols + 2 * width * total * cols,
        (rows_in, *rights, *(weights.arrays if more else ())),
        (total + more, 2),
        [pl.BlockSpec((length, half), lambda n, s, blk: (0, s))]
        + [right_spec(i) for i in range(n)]
        + [pl.BlockSpec(memory_space=pl.ANY)] * k,
        out_specs,
        out_shape,
        scratch=scratch,
        prefetch=(blocks,),
        after=after,
    )


def split_outputs(split, rows, half, count):
    if split is None:
        return [(0, half, {m: m for m in range(count)}, lambda m, blk: (m, 0))]
    send_first = (({0: 1, 1: 0}), lambda m, blk: (jnp.where(m < 1, 1, 0), 0))
    keep_first = (({2: 1, 3: 0}), lambda m, blk: (jnp.where(m < 3, 1, 0), 0))
    send_second = (({0: 1, 2: 0}), lambda m, blk: (jnp.where(m < 2, 1, 0), 0))
    keep_second = (({1: 1, 3: 0}), lambda m, blk: (jnp.where(m < 3, 1, 0), 0))
    if split == "first":
        return [(0, half, *send_first), (0, half, *keep_first)]
    if split == "second":
        return [(0, half, *send_second), (0, half, *keep_second)]
    part = half // 2
    return [
        (0, part, *send_first),
        (0, part, *keep_first),
        (part, part, *send_second),
        (part, part, *keep_second),
    ]


def rows_back(blocks, order, splits, lefts, groups, name, after=()):
    length = lefts[0].shape[0]
    count, places = blocks.shape[0], order.shape[0]
    half = groups[0][0].rows // 2
    rows = length // places
    widths = [left.shape[1] for left in lefts]
    depth = sum(widths)
    n = len(lefts)
    arrays = [array for weights, _, _ in groups for array in weights.arrays]
    k = len(arrays)
    sides = sorted(splits)
    side = sides[0] if len(sides) == 1 else None
    plan = []
    for i, one in enumerate(sides):
        plan += [(i * half + col, *rest) for col, *rest in split_outputs(splits[one], rows, half, places)]
    whole = len(sides) * half
    pieces = max(weights.number(count, side) for weights, _, _ in groups)

    def kernel(blk, places_ref, *refs):
        left_refs, w_refs = refs[:n], refs[n : n + k]
        out_refs = refs[n + k : n + k + len(plan)]
        joined_ref, w_ref, left_sems, sems = refs[-4:]
        step = pl.program_id(0)

        def left_copies(at):
            slot, start, col, found = lax.rem(at, 2), pl.multiple_of(places_ref[at] * rows, rows), 0, []
            for i, (ref, cols) in enumerate(zip(left_refs, widths)):
                found.append(
                    pltpu.make_async_copy(
                        ref.at[pl.ds(start, rows), :],
                        joined_ref.at[slot, :, pl.ds(col, cols)],
                        left_sems.at[slot, i],
                    )
                )
                col += cols
            return found

        per_group, at, col = [], 0, 0
        for i, (weights, start, cols) in enumerate(groups):
            more = len(weights.arrays)
            per_group.append(
                weights.copies(
                    w_refs[at : at + more], blk, count, side, start, cols, w_ref.at[:, pl.ds(col, cols)], sems.at[i]
                )
            )
            at, col = at + more, col + cols

        @pl.when(step == 0)
        def _():
            for copy in left_copies(0):
                copy.start()
            for piece in per_group:
                for copy in piece:
                    copy.start()

        @pl.when(step + 1 < places)
        def _():
            for copy in left_copies(step + 1):
                copy.start()

        for copy in left_copies(step):
            copy.wait()

        @pl.when(step == 0)
        def _():
            for piece in per_group:
                for copy in piece:
                    copy.wait()

        low = dot(joined_ref[lax.rem(step, 2)], w_ref[...], NT).astype(BF)
        for (col, cols, steps, _), ref in zip(plan, out_refs):

            def store(ref=ref, col=col, cols=cols):
                ref[...] = low[:, col : col + cols]

            if len(steps) > 2:
                store()
            else:
                pl.when(functools.reduce(jnp.logical_or, [step == at for at in steps]))(store)

    def out_spec(cols, where):
        return pl.BlockSpec((rows, cols), lambda m, blk, o: where(m, blk))

    return call(
        kernel,
        name,
        2 * length * whole * depth,
        2 * length * depth + 2 * whole * depth + 2 * length * whole,
        (*lefts, *arrays),
        (places,),
        [pl.BlockSpec(memory_space=pl.ANY)] * (n + k),
        [out_spec(cols, where) for _, cols, _, where in plan],
        [struct((len(steps) * rows, cols)) for _, cols, steps, _ in plan],
        scratch=[
            pltpu.VMEM((2, rows, depth), BF),
            pltpu.VMEM((whole, depth), BF),
            pltpu.SemaphoreType.DMA((2, n)),
            pltpu.SemaphoreType.DMA((len(groups), pieces)),
        ],
        prefetch=(blocks, order),
        after=after,
    )


def gain_sums(order, split, parts, unit, side):
    length, width = unit.shape
    half, places = width // 2, order.shape[0]
    rows = length // places
    plan = split_outputs(split, rows, half, places)
    n = len(plan)

    def kernel(places_ref, unit_ref, *refs):
        sum_ref = refs[n]
        step = pl.program_id(0)

        @pl.when(step == 0)
        def _():
            sum_ref[...] = jnp.zeros_like(sum_ref)

        for (col, cols, steps, _), ref in zip(plan, refs):

            def add(ref=ref, here=slice(col, col + cols)):
                wide = ref[...].astype(F32)
                sum_ref[0:8, here] += eight_rows(wide * unit_ref[:, here].astype(F32))
                sum_ref[8:16, here] += eight_rows(wide)

            if len(steps) > 2:
                add()
            else:
                pl.when(functools.reduce(jnp.logical_or, [step == at for at in steps]))(add)

    def spec(cols, where):
        return pl.BlockSpec((rows, cols), lambda m, o: where(m, o))

    return call(
        kernel,
        "gain_sums",
        0,
        2 * length * width,
        (unit, *parts),
        (places,),
        [pl.BlockSpec((rows, half), lambda m, o: (o[m], side))]
        + [spec(cols, where) for _, cols, _, where in plan],
        pl.BlockSpec((16, half), lambda m, o: (0, 0)),
        struct((16, half), F32),
        prefetch=(order,),
    )


def turned_sums(sums, units):
    depth, cols = sums.shape
    inner = cols - units

    def kernel(sums_ref, fc2_ref, out_ref):
        fc2_ref[...] = sums_ref[:, :units].T.astype(F32)
        out_ref[...] = sums_ref[:, units:].T.astype(F32)

    def whole(shape):
        return pl.BlockSpec(shape, lambda i: (0, 0))

    return call(
        kernel,
        "turned_sums",
        0,
        6 * depth * cols,
        (sums,),
        (1,),
        [whole((depth, cols))],
        [whole((units, depth)), whole((inner, depth))],
        [struct((units, depth), F32), struct((inner, depth), F32)],
    )


def end_call(kernel, name, blocks, fulls, terms, vector, dtype, after):
    length, width = fulls[0].shape
    rows = min(256, length)
    n = len(fulls)
    counts = [len(part) for part in terms]

    def body(blk, *refs):
        at, parts = n, []
        for number in counts:
            total = refs[at][...].astype(F32)
            for ref in refs[at + 1 : at + number]:
                total = total + ref[...].astype(F32)
            parts.append(total)
            at += number
        count, out_ref = blocks.shape[0], refs[at + 1]
        cols = width // count
        values = [ordered(ref, blk, count, cols).astype(F32) for ref in refs[:n]]
        result = kernel(values, jnp.concatenate(parts, axis=1), refs[at][...])
        for p in range(count):
            place = pl.ds(pl.multiple_of(blk[p] * cols, cols), cols)
            out_ref[:, place] = result[:, p * cols : (p + 1) * cols].astype(dtype)

    full = pl.BlockSpec((rows, width), lambda m, blk: (m, 0))
    flat = [array for part in terms for array in part]
    return call(
        body,
        name,
        0,
        10 * length * width,
        (*fulls, *flat, vector),
        (length // rows,),
        [full] * n
        + [pl.BlockSpec((rows, array.shape[1]), lambda m, blk: (m, 0)) for array in flat]
        + [pl.BlockSpec((1, width), lambda m, blk: (0, 0))],
        full,
        struct((length, width), dtype),
        prefetch=(blocks,),
        after=after,
    )


def add_branch(blocks, x, terms, out_bias, after=()):
    return end_call(
        lambda fulls, branch, bias: fulls[0] + branch + bias, "add_branch", blocks, (x,), terms, out_bias, BF, after
    )


def norm_back(blocks, x, g, terms, gain, after=()):
    def kernel(fulls, grads, scale):
        x, g = fulls
        centered = x - jnp.mean(x, axis=1, keepdims=True)
        variance = jnp.mean(centered * centered, axis=1, keepdims=True)
        inv_std = lax.rsqrt(variance + EPSILON)
        unit = centered * inv_std
        scaled = grads * scale
        mean = jnp.mean(scaled, axis=1, keepdims=True)
        along = jnp.mean(scaled * unit, axis=1, keepdims=True)
        return g + inv_std * (scaled - mean - unit * along)

    return end_call(kernel, "norm_back", blocks, (x, g), terms, gain, F32, after)


def flip(value, axis, size, bit):
    return lax.ppermute(value, axis, [(i, i ^ bit) for i in range(size)])


def flip_sum(value, axis, size):
    bit = 1
    while bit < size:
        value = value + flip(value, axis, size, bit)
        bit *= 2
    return value


class Ring:
    def __init__(self, n_dp):
        self.size = n_dp
        self.chips = n_dp // 2

    def send(self, value, distance=1):
        pairs = [
            (z * 2 + c, ((z + distance) % self.chips) * 2 + c)
            for z in range(self.chips)
            for c in range(2)
        ]
        return lax.ppermute(value, "dp", pairs)

    def swap(self, value):
        return flip(value, "dp", self.size, 1)


def per_device(
    sizes, layer_input, ln_gain, ln_bias, out_bias, w_qkv, b_qkv, w_out, w_fc1, b_fc1, w_fc2, out_grad
):
    n_dp, n_tensor = sizes
    ring = Ring(n_dp)
    chips = ring.chips
    d_index, t_index = lax.axis_index("dp"), lax.axis_index("tensor")
    place, core = d_index // 2, d_index % 2
    steps = jnp.arange(chips, dtype=jnp.int32)
    behind = ((place - steps) % chips) * 2
    blocks = jnp.concatenate([behind + core, behind + (1 - core)]).astype(jnp.int32)
    square = n_tensor == 4

    local, width = layer_input.shape[1:]
    depth = w_qkv.shape[0]
    inner = w_qkv.shape[2]
    units = w_fc1.shape[1]
    heads = inner // HD
    length = local * n_tensor
    pairs = inner // 128

    third = ln_gain.shape[0]
    x, g = layer_input[0], out_grad[0]
    x_all = lax.all_gather(x, "tensor", axis=0, tiled=True)
    heads_own = [heads_shard(jnp.transpose(w_qkv, (1, 0, 2)), w_out)]

    vectors = jnp.stack([ln_gain, ln_bias, out_bias]).astype(F32).reshape(1, 3 * third)
    table = jnp.where(jnp.arange(n_tensor)[:, None] == t_index, vectors, 0.0)
    table = table + sum(flip(table, "tensor", n_tensor, bit) for bit in range(1, n_tensor))
    small = jnp.concatenate([table.reshape(-1), b_qkv.astype(F32).reshape(-1), b_fc1.astype(F32).reshape(-1)])
    fc1_shard, fc2_shard = stage(w_fc1, False, heads_own), stage(w_fc2, True, heads_own)
    g_placed, bias_part = order_columns(blocks, g, after=heads_own)
    heads_own.append(ring.send(heads_own[0]))
    heads_sib = [ring.swap(heads_own[0])]
    small, g_placed = tie([small, g_placed], [heads_own[1], heads_sib[0]])
    g_all = lax.all_gather(g_placed, "tensor", axis=0, tiled=True)

    heads_own.append(ring.send(heads_own[1]))
    heads_sib.append(ring.swap(heads_own[1]))
    small = jnp.where(jnp.arange(n_dp)[:, None] == d_index, small[None, :], 0.0)
    small = flip_sum(small, "dp", n_dp)
    tables = rotary_rows(length)
    (small,) = tie([small], [heads_own[2], heads_sib[1], *tables])

    chosen = (blocks[:, None] == jnp.arange(n_dp)[None, :]).astype(F32)
    cut = n_tensor * 3 * third
    vectors = jnp.einsum("pd,dj->pj", chosen, small[:, :cut], precision=lax.Precision.HIGHEST)
    vectors = jnp.transpose(vectors.reshape(n_dp, n_tensor, 3, third), (2, 0, 1, 3))
    gain, shift, bias_out = (vectors[i].reshape(1, width) for i in range(3))
    b_width = HD // n_dp
    tail = cut + b_qkv.size
    bias_qkv = jnp.transpose(small[:, cut:tail].reshape(n_dp, 3, heads, b_width), (1, 2, 0, 3))
    bias_qkv = bias_qkv.reshape(1, 3 * inner)
    bias_fc1 = jnp.transpose(small[:, tail:].reshape(n_dp, units // HD, b_width), (1, 0, 2))
    bias_fc1 = bias_fc1.reshape(1, units)
    while len(heads_own) < chips:
        heads_own.append(ring.send(heads_own[-1]))
        heads_sib.append(ring.swap(heads_own[-2]))
    fc1_shard, fc2_shard = tie(
        [fc1_shard, fc2_shard], [heads_own[-1], heads_sib[-1], gain, bias_qkv, bias_fc1]
    )
    heads_sib.append(ring.swap(heads_own[-1]))
    heads_weights = Weights(heads_own + heads_sib)
    fc2_weights = Weights([lax.all_gather(fc2_shard, "dp", axis=0, tiled=True)], depth, placed=True)
    if square:
        order = (jnp.array([3, 1, 2, 0], jnp.int32) ^ t_index).astype(jnp.int32)
    else:
        order = jnp.arange(n_tensor, dtype=jnp.int32)

    def split(kind):
        return kind if square else None

    bits = {"first": [1], "second": [2], "both": [1, 2]}

    def cross_once(kind, parts):
        if not square:
            return [lax.psum_scatter(parts[0], "tensor", scatter_dimension=0, tiled=True)]
        return [flip(parts[2 * i], "tensor", 4, bit) for i, bit in enumerate(bits[kind])]

    def cross_add(parts, got):
        if not square:
            return []
        kept = parts[1::2]
        return [(k[local:].astype(F32) + r[local:].astype(F32)).astype(BF) for k, r in zip(kept, got)]

    def cross_twice(kind, sums):
        return [flip(value, "tensor", 4, 3 - bit) for value, bit in zip(sums, bits[kind])] if square else []

    def cross_terms(parts, got, last):
        if not square:
            return [got]
        return [list(terms) for terms in zip(parts[1::2], got, last)]

    fc1_own = {k: ring.send(fc1_shard, k) for k in ((1, 3) if chips == 4 else range(1, chips))}
    fc1_sib = {0: ring.swap(fc1_shard)}
    normed, unit, qkv = norm_project(
        blocks, x_all, gain, shift, bias_qkv, tables, heads_weights, after=[fc1_shard]
    )
    first = pairs // 2
    context, log_first = attend(qkv, 0, first, after=[fc1_shard])
    near = [1, 3] if chips == 4 else []
    log_first, *joined = tie([log_first, *(fc1_own[k] for k in near)], [fc1_sib[0]])
    fc1_own.update(zip(near, joined))
    if chips == 4:
        fc1_own[2] = ring.send(fc1_own[1])
    fc1_sib.update({k: ring.swap(fc1_own[k]) for k in near})
    context, log_second = attend(qkv, first, pairs - first, before=context, after=[log_first])
    far = [k for k in range(1, chips) if k not in near]
    log_second, *joined = tie([log_second, *(fc1_own[k] for k in far)], [fc1_sib[k] for k in near])
    fc1_own.update(zip(far, joined))
    fc1_sib.update({k: ring.swap(fc1_own[k]) for k in far})
    fc1_own[0] = fc1_shard
    log_total = jnp.concatenate([log_first, log_second], axis=0)
    fc1_weights = Weights([fc1[k] for fc1 in (fc1_own, fc1_sib) for k in range(chips)])
    act, slope = expand(blocks, normed, fc1_weights, bias_fc1, after=[log_second])

    def scatter(parts):
        return lax.psum_scatter(parts, "dp", scatter_dimension=0, tiled=True)

    fc2_grad, context_grad = weight_grad(
        blocks, g_all, [act, context], min(512, inner), "fc2_grad", heads_weights
    )
    fc2_sums = scatter(fc2_grad)
    *backs, b_qkv_part = attend_back(qkv, context, context_grad, log_total, tables)
    (heads_grad,) = weight_grad(blocks, normed, backs, inner, "heads_grad")
    heads_scattered = scatter(heads_grad)

    heads_cols, fc2_cols = (heads_weights, 0, 3 * inner), (fc2_weights, 0, units)
    out_cols, fc1_cols = (heads_weights, 3 * inner, inner), (fc1_weights, 0, units)
    lefts = [act, context]
    branch = rows_back(
        blocks, order, {0: split("first"), 1: split("second")}, lefts, [fc2_cols, out_cols], "branch",
        after=[heads_grad],
    )
    n = len(branch) // 2
    branch_own, branch_sib = branch[:n], branch[n:]
    hidden_grad, b_fc1_part = hidden_back(blocks, g_all, fc2_weights, slope, after=branch)
    (fc1_grad,) = weight_grad(blocks, normed, [hidden_grad], min(1024, units), "fc1_grad")
    branch_got = cross_once("first", branch_own) + cross_once("second", branch_sib)
    n = len(branch_got)
    fc1_grad, *branch_got = tie([fc1_grad, *branch_got], [])
    fc1_sums = scatter(fc1_grad)
    branch_sums = cross_add(branch_own, branch_got[:1]) + cross_add(branch_sib, branch_got[1:])
    branch_last = cross_twice("first", branch_sums[:1]) + cross_twice("second", branch_sums[1:])

    lefts = [*backs, hidden_grad]
    back_own = rows_back(
        blocks, order, {0: split("both")}, lefts, [heads_cols, fc1_cols], "normed_back_half",
        after=[fc1_grad, *branch_sums],
    )
    n = len(back_own)
    sums_own = gain_sums(order, split("both"), back_own, unit, 0)
    joined = tie([*back_own, *branch_last], [sums_own])
    back_own, branch_last = joined[:n], joined[n:]
    heads_sums = heads_sum(heads_scattered)
    branch_terms = cross_terms(branch_own, branch_got[:1], branch_last[:1])
    branch_terms += cross_terms(branch_sib, branch_got[1:], branch_last[1:])
    own_got = cross_once("both", back_own)
    back_sib = rows_back(
        blocks, order, {1: split("both")}, lefts, [heads_cols, fc1_cols], "normed_back_half",
        after=[back_own[0]],
    )
    joined = tie([*back_sib, *own_got], [])
    back_sib, own_got = joined[:n], joined[n:]

    sib_got = cross_once("both", back_sib)
    own_sums = cross_add(back_own, own_got)
    own_last = cross_twice("both", own_sums)
    norm_sums = [sums_own, gain_sums(order, split("both"), back_sib, unit, 1)]
    norm_sums = jnp.concatenate(norm_sums, axis=1).reshape(2, 8, n_dp, depth)
    norm_sums = jnp.einsum("pd,kpj->dkj", chosen, jnp.sum(norm_sums, axis=1), precision=lax.Precision.HIGHEST)
    b_qkv_part = jnp.sum(b_qkv_part.reshape(pairs, 3, 8, 128), axis=2)
    b_qkv_part = jnp.transpose(b_qkv_part, (1, 0, 2)).reshape(3, heads, n_dp, b_width)
    b_fc1_part = jnp.sum(b_fc1_part, axis=0).reshape(units // HD, n_dp, b_width)
    by_owner = jnp.concatenate(
        [
            norm_sums.reshape(n_dp, 2 * depth),
            bias_part[0].reshape(n_dp, depth),
            jnp.transpose(b_qkv_part, (2, 0, 1, 3)).reshape(n_dp, -1),
            jnp.transpose(b_fc1_part, (1, 0, 2)).reshape(n_dp, -1),
        ],
        axis=1,
    )

    sums = flip_sum(by_owner, "dp", n_dp)
    sums = lax.dynamic_index_in_dim(sums, d_index, 0, keepdims=False)
    w_fc2_grad, w_out_grad = turned_sums(fc2_sums, units)
    sums, *sib_got = tie([sums, *sib_got], [heads_sums, *own_sums])
    sib_sums = cross_add(back_sib, sib_got)
    sib_last = cross_twice("both", sib_sums)
    layer_output = add_branch(blocks, x, branch_terms, bias_out, after=[*sib_sums, *back_sib[:1]])
    w_fc1_grad = fc1_sums.astype(F32)
    (sums,) = tie([sums], [layer_output, w_fc2_grad, w_fc1_grad])
    mine = sums[: 3 * depth].reshape(3, depth)
    mine = flip_sum(mine, "tensor", n_tensor)
    mine = lax.dynamic_slice_in_dim(mine, t_index * third, third, 1)
    b_qkv_grad = sums[3 * depth : 3 * depth + b_qkv.size].reshape(b_qkv.shape)
    b_fc1_grad = sums[3 * depth + b_qkv.size :].reshape(b_fc1.shape)
    w_qkv_grad = jnp.transpose(heads_sums, (1, 0, 2))
    back_terms = cross_terms(back_own, own_got, own_last) + cross_terms(back_sib, sib_got, sib_last)
    input_grad = norm_back(blocks, x, g, back_terms, gain, after=[sums])
    return (
        layer_output[None],
        input_grad[None],
        mine[0],
        mine[1],
        mine[2],
        w_qkv_grad,
        b_qkv_grad,
        w_out_grad,
        w_fc1_grad,
        b_fc1_grad,
        w_fc2_grad,
    )


def solution(mesh):
    in_specs = (
        P("dp", "tensor", None),
        P(("dp", "tensor")),
        P(("dp", "tensor")),
        P(("dp", "tensor")),
        P("dp", None, "tensor"),
        P(None, "tensor", "dp"),
        P("tensor", "dp"),
        P("dp", "tensor"),
        P("tensor", "dp"),
        P("tensor", "dp"),
        P("dp", "tensor", None),
    )
    out_specs = (
        P("dp", "tensor", None),
        P("dp", "tensor", None),
        P(("dp", "tensor")),
        P(("dp", "tensor")),
        P(("dp", "tensor")),
        P("dp", None, "tensor"),
        P(None, "tensor", "dp"),
        P("tensor", "dp"),
        P("dp", "tensor"),
        P("tensor", "dp"),
        P("tensor", "dp"),
    )
    sizes = (mesh.shape["dp"], mesh.shape["tensor"])
    return jax.shard_map(
        functools.partial(per_device, sizes),
        mesh=mesh,
        in_specs=in_specs,
        out_specs=out_specs,
        check_vma=False,
    )
```
